32 devices in a mesh: batch: 4 (over z), ha: 2 (over core), wa: 4 (over y, x).
Axes of the slice: x: 2, y: 2, z: 4, core: 2. Of those that a mesh axis runs over, the one named last changes fastest.
Arguments:
- clip_features: bfloat16 [128, 16, 16, 832], P('batch', 'ha', 'wa'), may hold values from -6 to 6
- frame_counts: int32 [8], P('batch'), may hold values from 2 to 16, as said below
- w_reduce: bfloat16 [2, 832, 448], replicated, may hold values from -0.21875 to 0.21875
- w_mid: bfloat16 [2, 27, 160, 320], replicated, may hold values from -0.09375 to 0.09375
- w_small: bfloat16 [2, 27, 32, 128], replicated, may hold values from -0.21875 to 0.21875
- w_pool: bfloat16 [2, 832, 128], replicated, may hold values from -0.21875 to 0.21875
- norm_gain: float32 [2, 1024], replicated, may hold values from 0.5 to 1.5
- norm_bias: float32 [2, 1024], replicated, may hold values from -3 to 3
- out_grad: bfloat16 [64, 8, 8, 832], P('batch', 'ha', 'wa'), may hold values from -6 to 6
Outputs:
- block_output: bfloat16 [64, 8, 8, 832], P('batch', 'ha', 'wa')
- input_grad: bfloat16 [128, 16, 16, 832], P('batch', 'ha', 'wa')
- reduce_grad: float32 [2, 832, 448], replicated
- mid_grad: float32 [2, 27, 160, 320], replicated
- small_grad: float32 [2, 27, 32, 128], replicated
- pool_grad: float32 [2, 832, 128], replicated
- gain_grad: float32 [2, 1024], replicated
- bias_grad: float32 [2, 1024], replicated
The draws below stay inside these ranges and needn't reach their ends.
Inputs may be any that keep to these rules, and one draw needn't show every extreme that they name: `frame_counts`: even; some clip has 16 frames and some 2.
All inputs are finite; a program needn't handle non-finite values.
Results may differ from the reference program's by a relative error of at most 0.015.
Values may be sent and summed in bfloat16 or wider, within the bound.
A program may use at most 192 MiB of HBM per device.

```python
import jax
import jax.numpy as jnp
from jax import lax

C_IN = 832
B0 = 256
B1R = 160
B1 = 320
B2R = 32
B2 = 128
BP = 128
HEIGHT = 14
GRID = 16
SLOT = 16
CLIPS = 8
FRAMES = 128


def draw_frame_counts(key, part):
    key = jax.random.fold_in(key, 7)
    halves_key, long_key, short_key = jax.random.split(key, 3)
    halves = jax.random.randint(halves_key, (CLIPS,), 1, SLOT // 2 + 1)
    longest = jax.random.randint(long_key, (), 0, CLIPS)
    shortest = (longest + 1 + jax.random.randint(short_key, (), 0, CLIPS - 1)) % CLIPS
    halves = halves.at[longest].set(SLOT // 2).at[shortest].set(1)
    return (2 * halves).astype(jnp.int32)


def block_scale(own_key, dims, shards, smallest, largest):
    def one(axis_at, shards_of):
        heights = jax.random.uniform(jax.random.fold_in(jax.random.fold_in(own_key, 6), axis_at), (shards_of,), jnp.float32, smallest / len(shards), largest / len(shards))
        return jnp.repeat(jnp.exp(heights), dims[axis_at] // shards_of).reshape((-1,) + (1,) * (len(dims) - axis_at - 1))

    factor_of = one(*shards[0])
    for cut in shards[1:]:
        factor_of = factor_of * one(*cut)
    return factor_of


def normal_values(key, shape, scale, most, cuts=(), held_as=jnp.bfloat16):
    level = block_scale(key, shape, cuts, -0.22, 0.18) if cuts else 1.0
    values = jax.random.normal(key, shape, jnp.float32) * scale * level
    return jnp.minimum(jnp.maximum(values, -most), most).astype(held_as)


def setup_inputs(seed: int = 0) -> dict:
    seeds = jax.random.split(jax.random.key(seed), 10)
    return {
        "clip_features": normal_values(seeds[0], (FRAMES, GRID, GRID, C_IN), 1.0, 6.0, ((0, 4), (1, 2), (2, 4))),
        "frame_counts": draw_frame_counts(jax.random.fold_in(seeds[9], 71), 0),
        "w_reduce": normal_values(seeds[2], (2, C_IN, B0 + B1R + B2R), C_IN ** -0.5, 0.21875),
        "w_mid": normal_values(seeds[3], (2, 27, B1R, B1), (27 * B1R) ** -0.5, 0.09375),
        "w_small": normal_values(seeds[4], (2, 27, B2R, B2), (27 * B2R) ** -0.5, 0.21875),
        "w_pool": normal_values(seeds[5], (2, C_IN, BP), C_IN ** -0.5, 0.21875),
        "norm_gain": jnp.clip(1.0 + 0.1 * jax.random.normal(seeds[6], (2, B0 + B1R + B2R + B1 + B2 + BP), jnp.float32), 0.5, 1.5),
        "norm_bias": normal_values(seeds[7], (2, B0 + B1R + B2R + B1 + B2 + BP), 0.5, 3.0, (), jnp.float32),
        "out_grad": normal_values(seeds[8], (FRAMES // 2, GRID // 2, GRID // 2, C_IN), 1.0, 6.0, ((0, 4), (1, 2), (2, 4))),
    }


EPSILON = 1e-05

@jax.custom_vjp
def low(v):
    return lax.optimization_barrier(v.astype(jnp.bfloat16)).astype(jnp.float32)

@jax.custom_vjp
def low_back(v):
    return v

def low_keep(v):
    return (low(v), None)

def low_pass(kept, grad):
    return (grad,)

def back_keep(v):
    return (v, None)

def back_low(kept, grad):
    return (low(grad),)
low.defvjp(low_keep, low_pass)
low_back.defvjp(back_keep, back_low)

def validity(frame_counts, slot_len, grid_size, height):
    grid_shape = (frame_counts.shape[0], slot_len, grid_size, grid_size, 1)
    frame_at = lax.broadcasted_iota(jnp.int32, grid_shape, 1)
    row_at = lax.broadcasted_iota(jnp.int32, grid_shape, 2)
    col_at = lax.broadcasted_iota(jnp.int32, grid_shape, 3)
    inside = (frame_at < frame_counts[:, None, None, None, None]) & (row_at < height) & (col_at < height)
    return inside.astype(jnp.float32)

def box_pool(volume):
    padded = jnp.pad(volume, ((0, 0), (1, 1), (1, 1), (1, 1), (0, 0)))
    slot_len, grid_rows, grid_cols = (volume.shape[1], volume.shape[2], volume.shape[3])
    summed = jnp.zeros_like(volume)
    for offset in range(27):
        off_time, off_row, off_col = (offset // 9, offset // 3 % 3, offset % 3)
        summed = summed + padded[:, off_time:off_time + slot_len, off_row:off_row + grid_rows, off_col:off_col + grid_cols, :]
    return summed / 27.0

def conv_cube(volume, kernel):
    kernel_cube = kernel.reshape(3, 3, 3, kernel.shape[1], kernel.shape[2])
    return lax.conv_general_dilated(volume, kernel_cube, (1, 1, 1), 'SAME', dimension_numbers=('NDHWC', 'DHWIO', 'NDHWC'), precision=lax.Precision.HIGHEST)

def pointwise(volume, kernel):
    return jnp.einsum('abcdi,io->abcdo', volume, kernel, precision=lax.Precision.HIGHEST)

def batch_norm(volume, inside, gain_vec, bias_vec):
    count_sum = jnp.sum(inside)
    average = lax.optimization_barrier(jnp.sum(volume * inside, axis=(0, 1, 2, 3))) / count_sum
    square_mean = lax.optimization_barrier(jnp.sum(volume * volume * inside, axis=(0, 1, 2, 3))) / count_sum
    variance = square_mean - average * average
    normed = (volume - average) * lax.rsqrt(variance + EPSILON)
    return jax.nn.softplus(normed * gain_vec + bias_vec) * inside

def layer(features, inside, reduce_k, mid_k, small_k, pool_k, gain_vec, bias_vec):
    reduce_width = reduce_k.shape[1]
    mid_in = mid_k.shape[1]
    first_width = reduce_width - mid_in - small_k.shape[1]
    block_in = low(features * inside)
    reduced = low_back(pointwise(block_in, reduce_k))
    first = batch_norm(reduced, inside, gain_vec[:reduce_width], bias_vec[:reduce_width])
    narrow = low(first[..., first_width:])
    projected = low_back(low(pointwise(block_in, pool_k)))
    second = jnp.concatenate([conv_cube(narrow[..., :mid_in], mid_k), conv_cube(narrow[..., mid_in:], small_k), box_pool(projected)], axis=-1)
    second = low_back(second)
    second_out = batch_norm(second, inside, gain_vec[reduce_width:], bias_vec[reduce_width:])
    return jnp.concatenate([first[..., :first_width], second_out], axis=-1)

def reference(clip_features, frame_counts, w_reduce, w_mid, w_small, w_pool, norm_gain, norm_bias, out_grad):
    clip_total = frame_counts.shape[0]
    first_inside = validity(frame_counts, SLOT, GRID, HEIGHT)
    second_inside = validity(frame_counts // 2, SLOT // 2, GRID // 2, HEIGHT // 2)

    def forward(volume, reduce_k, mid_k, small_k, pool_k, gain_all, bias_all):
        first_out = layer(volume, first_inside, reduce_k[0], mid_k[0], small_k[0], pool_k[0], gain_all[0], bias_all[0])
        halved = first_out.reshape(clip_total, SLOT // 2, 2, GRID // 2, 2, GRID // 2, 2, C_IN)
        halved = lax.optimization_barrier(jnp.mean(halved, axis=(2, 4, 6)))
        return layer(halved, second_inside, reduce_k[1], mid_k[1], small_k[1], pool_k[1], gain_all[1], bias_all[1])
    volume = clip_features.astype(jnp.float32).reshape(clip_total, SLOT, GRID, GRID, C_IN)
    result, pullback = jax.vjp(forward, volume, w_reduce.astype(jnp.float32), w_mid.astype(jnp.float32), w_small.astype(jnp.float32), w_pool.astype(jnp.float32), norm_gain.astype(jnp.float32), norm_bias.astype(jnp.float32))
    incoming = out_grad.astype(jnp.float32).reshape(clip_total, SLOT // 2, GRID // 2, GRID // 2, C_IN)
    grads = pullback(incoming)
    block_output = result.astype(jnp.bfloat16).reshape(clip_total * SLOT // 2, GRID // 2, GRID // 2, C_IN)
    input_grad = grads[0].astype(jnp.bfloat16).reshape(clip_total * SLOT, GRID, GRID, C_IN)
    return (block_output, input_grad, grads[1], grads[2], grads[3], grads[4], grads[5], grads[6])
```

```python
import functools
from types import SimpleNamespace

import jax
import jax.numpy as jnp
from jax import lax
from jax.experimental import pallas as pl
from jax.experimental.pallas import tpu as pltpu
from jax.sharding import PartitionSpec as P

HEIGHT = 14
EPSILON = 1e-05
MESH = pl.DeviceIdType.MESH
F32 = jnp.float32
BF16 = jnp.bfloat16

B0, B1R, B2R, B1, B2, BP = 256, 160, 32, 320, 128, 128
NARROW = B1R + B2R
REDUCE = B0 + NARROW
SECOND = (B1, B2, BP)
SECOND_AT = (0, 384, 512)
SECOND_WIDTH = 640
SUM_WIDTH = 1280
AXES = ("batch", "ha", "wa")

TAP_BLOCKS = 88
LOW_AT = 800
LOW_OUT = 1024
GRAD_BLOCKS = 1056
BUNDLES = ((0, 352), (352, 448), (800, 256))
OWNERS = 4

SCHEDULE = {
    (1, 1): ((1, 0), (1, 1)),
    (1, 5): ((1, 0), (1, 1)),
    (1, 6): (),
    (0, 7): ((1, 0), (1, 1), (1, 2)),
    (0, 0): ((1, 0), (1, 1), (1, 2)),
    (0, 1): ((0, 0), (0, 1), (1, 0), (1, 1), (1, 2)),
    (0, 2): ((1, 0), (1, 1), (1, 2)),
    (0, 3): ((0, 0), (0, 1), (1, 0), (1, 1), (1, 2)),
    (0, 4): ((1, 0), (1, 1), (1, 2)),
    (0, 5): ((0, 0), (0, 1), (1, 0), (1, 1), (1, 2)),
    (0, 6): ((0, 0), (0, 1)),
}
LAST_STEPS = ((0, 2), (0, 0), (0, 1)) * 9

NN = (((1,), (0,)), ((), ()))
NT = (((1,), (1,)), ((), ()))


def dot(a, b, dims=NN):
    return lax.dot_general(a, b, dims, preferred_element_type=F32)


def softplus(x):
    return jnp.maximum(x, 0.0) + jnp.log1p(jnp.exp(-jnp.abs(x)))


def sigmoid(x):
    return 1.0 / (1.0 + jnp.exp(-x))


class Layer:
    def __init__(self, index, rows, cols, clips, slot):
        self.index, self.rows, self.cols = index, rows, cols
        self.clips, self.slot = clips, slot
        self.frames = clips * slot
        self.cells = rows * cols * self.frames
        self.row_cells = cols * self.frames

    def scratch(self, channels):
        r, c, t, n = self.rows, self.cols, self.frames, self.cells
        pad = (r + 2, c + 2, t)
        return dict(
            mask=pltpu.VMEM(pad + (1,), F32),
            block_in=pltpu.VMEM((r, c, t, channels), BF16),
            first=pltpu.VMEM((r, c, t, B0), F32),
            narrow=pltpu.VMEM(pad + (NARROW,), F32),
            border=pltpu.VMEM(pad + (BP + NARROW,), BF16),
            mid_in=pltpu.VMEM(pad + (3 * B1R,), BF16),
            small_in=pltpu.VMEM(pad + (3 * B2R,), BF16),
            box=pltpu.VMEM((r + 2, c, t, BP), F32),
            mid=pltpu.VMEM((n, 3 * B1R), F32),
            small=pltpu.VMEM((n, B2), F32),
            pool=pltpu.VMEM((n, BP), F32),
            normed=pltpu.VMEM(pad + (SECOND_WIDTH,), BF16),
            projected_slope=pltpu.VMEM((n, BP), BF16),
            low=pltpu.VMEM((n, REDUCE), BF16),
        )


def batch_norm_scale(total, square, count, gain):
    average = total / count
    variance = square / count - average * average
    inv_std = lax.rsqrt(variance + EPSILON)
    return average, inv_std, inv_std * gain


def kernel_body(names, sizes, refs):
    k = SimpleNamespace(**dict(zip(names, refs)))
    n_batch, n_wa, layers = sizes
    b, h, w = (lax.axis_index(a) for a in AXES)
    chips = n_batch * n_wa
    my_chip = b * n_wa + w
    one, two = layers

    def chip_at(p):
        return lax.div(p, n_wa), h, lax.rem(p, n_wa)

    def rotated(i):
        return lax.rem(my_chip + i, chips)

    loads = []
    for at, (source, target) in enumerate(
        (
            (k.features, one.s.block_in),
            (k.w_reduce, k.v_w_reduce),
            (k.w_pool, k.v_w_pool),
            (k.w_mid, k.v_w_mid),
            (k.w_small, k.v_w_small),
            (k.out_grad, k.v_out_grad),
        )
    ):
        copy = pltpu.make_async_copy(source, target, k.load_sem.at[at])
        copy.start()
        loads.append(copy)

    for lay in layers:
        s = lay.s
        for ref in (s.border, s.normed):
            for row in (0, lay.rows + 1):
                ref[row] = jnp.zeros(ref.shape[1:], ref.dtype)
            for col in (0, lay.cols + 1):
                ref[:, col] = jnp.zeros((ref.shape[0],) + ref.shape[2:], ref.dtype)
    ref = k.grad_border
    ref[...] = jnp.zeros(ref.shape, ref.dtype)
    for layer in range(2):
        for begin, end in ((9 * TAP_BLOCKS, LOW_AT), (LOW_AT + 252, GRAD_BLOCKS)):
            k.grads[layer, begin:end] = jnp.zeros((end - begin, 16, 128), BF16)
    k.sums[...] = jnp.zeros(k.sums.shape, F32)

    barrier = pltpu.get_barrier_semaphore()
    pl.semaphore_signal(barrier, inc=1, device_id=(b, 1 - h, w), device_id_type=MESH)

    @pl.when(w > 0)
    def _():
        pl.semaphore_signal(barrier, inc=1, device_id=(b, 1 - h, w - 1), device_id_type=MESH)

    @pl.when(w < n_wa - 1)
    def _():
        pl.semaphore_signal(barrier, inc=1, device_id=(b, 1 - h, w + 1), device_id_type=MESH)

    def greet(i, carry):
        pl.semaphore_signal(barrier, inc=1, device_id=chip_at(rotated(i)), device_id_type=MESH)
        return carry

    lax.fori_loop(1, chips, greet, 0)

    for lay in layers:
        frame_at = lax.broadcasted_iota(jnp.int32, (lay.frames, 1), 0)
        inside = jnp.zeros((lay.frames, 1), F32)
        for clip in range(lay.clips):
            valid = k.frame_counts[clip]
            valid = valid if lay.index == 0 else lax.div(valid, 2)
            begin = clip * lay.slot
            inside = jnp.where((frame_at >= begin) & (frame_at < begin + valid), 1.0, inside)
        height = HEIGHT if lay.index == 0 else HEIGHT // 2
        for row in range(lay.rows + 2):
            at_row = h * lay.rows + row - 1
            for col in range(lay.cols + 2):
                at_col = w * lay.cols + col - 1
                good = (at_row >= 0) & (at_row < height) & (at_col >= 0) & (at_col < height)
                lay.s.mask[row, col] = inside * good.astype(F32)

    def start_sum(at):
        pair = pltpu.make_async_remote_copy(
            src_ref=k.sums.at[at],
            dst_ref=k.pair_sums.at[at],
            send_sem=k.pair_sem.at[0, at],
            recv_sem=k.pair_sem.at[1, at],
            device_id=(b, 1 - h, w),
            device_id_type=MESH,
        )
        pair.start()
        pair.wait()
        k.chip_sums[at % 2, my_chip] = k.sums[at] + k.pair_sums[at]

        def send(i, carry):
            pltpu.make_async_remote_copy(
                src_ref=k.chip_sums.at[at % 2, my_chip],
                dst_ref=k.chip_sums.at[at % 2, my_chip],
                send_sem=k.chip_sem.at[0, at],
                recv_sem=k.chip_sem.at[1, at],
                device_id=chip_at(rotated(i)),
                device_id_type=MESH,
            ).start()
            return carry

        if chips <= 16:
            for i in range(1, chips):
                send(i, 0)
        else:
            lax.fori_loop(1, chips, send, 0)

    def end_sum(at):
        for way in (1, 0):
            others = k.chip_sums.at[at % 2, pl.ds(0, chips - 1)]
            pltpu.make_async_copy(others, others, k.chip_sem.at[way, at]).wait()
        total = k.chip_sums[at % 2, 0]
        for p in range(1, chips):
            total = total + k.chip_sums[at % 2, p]
        return total

    def halo_copies(lay, ref, at):
        src_row = jnp.where(h == 0, lay.rows, 1)
        dst_row = jnp.where(h == 0, 0, lay.rows + 1)
        rows, cols = lay.rows, lay.cols

        def remote(src, dst, way, device):
            return pltpu.make_async_remote_copy(
                src_ref=ref.at[src],
                dst_ref=ref.at[dst],
                send_sem=k.halo_sem.at[0, at, way],
                recv_sem=k.halo_sem.at[1, at, way],
                device_id=device,
                device_id_type=MESH,
            )

        all_rows, all_cols = pl.ds(1, rows), pl.ds(1, cols)
        row = remote((src_row, all_cols), (dst_row, all_cols), 0, (b, 1 - h, w))
        to_left = [
            remote((all_rows, 1), (all_rows, cols + 1), 1, (b, h, w - 1)),
            remote((src_row, 1), (dst_row, cols + 1), 2, (b, 1 - h, w - 1)),
        ]
        to_right = [
            remote((all_rows, cols), (all_rows, 0), 3, (b, h, w + 1)),
            remote((src_row, cols), (dst_row, 0), 4, (b, 1 - h, w + 1)),
        ]
        return row, to_left, to_right

    def start_halo(lay, ref, at):
        row, to_left, to_right = halo_copies(lay, ref, at)
        row.start()

        @pl.when(w > 0)
        def _():
            for copy in to_left:
                copy.start()

        @pl.when(w < n_wa - 1)
        def _():
            for copy in to_right:
                copy.start()

    def end_halo(lay, ref, at):
        row, to_left, to_right = halo_copies(lay, ref, at)
        row.wait()

        @pl.when(w > 0)
        def _():
            for copy in to_left:
                copy.wait_send()
            for copy in to_right:
                copy.wait_recv()

        @pl.when(w < n_wa - 1)
        def _():
            for copy in to_right:
                copy.wait_send()
            for copy in to_left:
                copy.wait_recv()

    def exchange(layer, number):
        begin, count = BUNDLES[number]
        half, quarter, eighth = count // 2, count // 4, count // 8
        piece, chunk = count // 16, count // 32
        stride = n_batch // OWNERS
        g = k.grads.at[layer]
        x, y = lax.rem(w, 2), lax.div(w, 2)
        pair, beside, below = (b, 1 - h, w), (b, h, w + 1 - 2 * x), (b, h, w + 2 - 4 * y)

        def copy(source, at, target, to, size, slot, device):
            return pltpu.make_async_remote_copy(
                src_ref=source.at[pl.ds(at, size)],
                dst_ref=target.at[pl.ds(to, size)],
                send_sem=k.grad_sem.at[0, layer, number, slot],
                recv_sem=k.grad_sem.at[1, layer, number, slot],
                device_id=device,
                device_id_type=MESH,
            )

        def go(copies):
            for c in copies:
                c.start()

        def end(copies):
            for c in copies:
                c.wait()

        def add(at, other, to, size):
            step = 16 if size % 16 == 0 else size

            def body(i, carry):
                mine = pl.ds(at + i * step, step)
                g[mine] = g[mine] + other[pl.ds(to + i * step, step)]
                return carry

            lax.fori_loop(0, size // step, body, 0)

        def free(slot, device):
            sem = k.free_sem.at[layer, number, slot]
            pl.semaphore_signal(sem, inc=1, device_id=device, device_id_type=MESH)

        def wait_free(slot):
            pl.semaphore_wait(k.free_sem.at[layer, number, slot], 1)

        r1, r2, r3, r4 = (r.at[layer] for r in (k.got_half, k.got_eighth, k.got_piece, k.got_chunk))
        mine = begin + h * half
        copies = [copy(g, begin + (1 - h) * half, r1, begin // 2, half, 0, pair)]
        go(copies)
        yield
        end(copies)
        free(0, pair)
        add(mine, r1, begin // 2, half)
        at_a, at_b = mine, mine + quarter
        to = begin // 4
        copies = [
            copy(g, at_a + (1 - x) * eighth, r2, to, eighth, 1, beside),
            copy(g, at_b + (1 - y) * eighth, r2, to + eighth, eighth, 2, below),
        ]
        go(copies)
        yield
        end(copies)
        at_a, at_b = at_a + x * eighth, at_b + y * eighth
        add(at_a, r2, to, eighth)
        add(at_b, r2, to + eighth, eighth)
        to = begin // 8
        copies = [
            copy(g, at_a + (1 - y) * piece, r3, to, piece, 3, below),
            copy(g, at_b + (1 - x) * piece, r3, to + piece, piece, 4, beside),
        ]
        go(copies)
        yield
        end(copies)
        free(1, below)
        free(2, beside)
        at_a, at_b = at_a + y * piece, at_b + x * piece
        add(at_a, r3, to, piece)
        add(at_b, r3, to + piece, piece)

        def chunk_at(owner):
            return (at_a, at_b)[owner // 2] + owner % 2 * chunk

        to = begin // 32
        r5 = k.got_total.at[layer]
        for owner in range(OWNERS):

            @pl.when(b != owner * stride)
            def _(owner=owner):
                pltpu.make_async_remote_copy(
                    src_ref=g.at[pl.ds(chunk_at(owner), chunk)],
                    dst_ref=r4.at[b, pl.ds(to, chunk)],
                    send_sem=k.grad_sem.at[0, layer, number, 5 + owner],
                    recv_sem=k.grad_sem.at[1, layer, number, 5],
                    device_id=(owner * stride, h, w),
                    device_id_type=MESH,
                ).start()

        yield

        def for_owner(do):
            if stride == 1:
                do()
            else:
                pl.when(lax.rem(b, stride) == 0)(do)

        rank = lax.div(b, stride)
        my_chunk = jnp.where(rank < 2, at_a, at_b) + lax.rem(rank, 2) * chunk

        def collect():
            others = r4.at[pl.ds(0, n_batch - 1), pl.ds(to, chunk)]
            pltpu.make_async_copy(others, others, k.grad_sem.at[1, layer, number, 5]).wait()
            r4[b, pl.ds(to, chunk)] = g[pl.ds(my_chunk, chunk)]
            total = r4[0, pl.ds(to, chunk)].astype(F32)
            for slot in range(1, n_batch):
                total = total + r4[slot, pl.ds(to, chunk)].astype(F32)
            g[pl.ds(my_chunk, chunk)] = total.astype(BF16)

        for_owner(collect)
        for owner in range(OWNERS):

            @pl.when(b != owner * stride)
            def _(owner=owner):
                part = g.at[pl.ds(chunk_at(owner), chunk)]
                pltpu.make_async_copy(part, part, k.grad_sem.at[0, layer, number, 5 + owner]).wait()

        def share_copy(i):
            return pltpu.make_async_remote_copy(
                src_ref=g.at[pl.ds(my_chunk, chunk)],
                dst_ref=r5.at[rank, pl.ds(to, chunk)],
                send_sem=k.grad_sem.at[0, layer, number, 9],
                recv_sem=k.grad_sem.at[1, layer, number, 9 + rank],
                device_id=(lax.rem(b + i, n_batch), h, w),
                device_id_type=MESH,
            )

        def share():
            def body(i, carry):
                share_copy(i).start()
                return carry

            lax.fori_loop(1, n_batch, body, 0)

        for_owner(share)
        yield

        def shared():
            def body(i, carry):
                share_copy(i).wait_send()
                return carry

            lax.fori_loop(1, n_batch, body, 0)

        for_owner(shared)
        for owner in range(OWNERS):

            @pl.when(b != owner * stride)
            def _(owner=owner):
                part = r5.at[owner, pl.ds(to, chunk)]
                pltpu.make_async_copy(part, part, k.grad_sem.at[1, layer, number, 9 + owner]).wait()
                g[pl.ds(chunk_at(owner), chunk)] = r5[owner, pl.ds(to, chunk)]

        copies = [
            copy(g, at_a, g, at_a, piece, 13, below),
            copy(g, at_b, g, at_b, piece, 14, beside),
        ]
        wait_free(1)
        wait_free(2)
        go(copies)
        yield
        end(copies)
        at_a, at_b = mine + x * eighth, mine + quarter + y * eighth
        copies = [
            copy(g, at_a, g, at_a, eighth, 15, beside),
            copy(g, at_b, g, at_b, eighth, 16, below),
        ]
        go(copies)
        yield
        end(copies)
        copies = [copy(g, mine, g, mine, half, 17, pair)]
        wait_free(0)
        go(copies)
        yield
        end(copies)
        target = k.weight_grads.at[layer, pl.ds(LOW_OUT if begin == LOW_AT else begin, count)]
        out = pltpu.make_async_copy(g.at[pl.ds(begin, count)], target, k.out_sem.at[layer, number])
        out.start()
        yield
        out.wait()

    exchanges = {}

    def start_exchange(layer, number):
        exchanges[layer, number] = exchange(layer, number)
        next(exchanges[layer, number])

    def progress(layer, at):
        for key in SCHEDULE.get((layer, at), ()):
            next(exchanges[key], None)

    def flat_block(lay):
        block = lay.s.block_in[...]
        return block.reshape(lay.cells, block.shape[-1])

    def store_blocks(layer, at, value):
        rows, lanes = value.shape
        for lane in range(0, lanes, 128):
            size = min(128, lanes - lane)
            blocks = pl.ds(at + lane // 128 * (rows // 16), rows // 16)
            tile = value[:, lane : lane + size].reshape(rows // 16, 16, size)
            k.grads[layer, blocks, :, 0:size] = tile

    def column_sum(value):
        return jnp.sum(value, axis=0, keepdims=True)

    def center_mask(lay, row, count=1):
        mask = lay.s.mask[pl.ds(row + 1, count), 1 : lay.cols + 1]
        return mask.reshape(count * lay.row_cells, 1)

    def shifted(lay, value):
        count = value.shape[0]
        frame_at = lax.rem(lax.broadcasted_iota(jnp.int32, (count, 1), 0), lay.slot)
        before = jnp.where(frame_at == 0, 0.0, pltpu.roll(value, 1, 0))
        after = jnp.where(frame_at == lay.slot - 1, 0.0, pltpu.roll(value, count - 1, 0))
        return before, after

    def reduce_conv(lay):
        s, at = lay.s, lay.index
        step = 2
        count = step * lay.row_cells

        def body(i, sums):
            mask = center_mask(lay, i * step, step)
            block = s.block_in[pl.ds(i * step, step)]
            block = block.reshape(count, block.shape[-1])
            if lay.index == 0:
                block = (block.astype(F32) * mask).astype(BF16)
                shape = (step, lay.cols, lay.frames, block.shape[-1])
                s.block_in[pl.ds(i * step, step)] = block.reshape(shape)
            reduced = dot(block, k.v_w_reduce[at], NT)
            projected = dot(block, k.v_w_pool[at])
            rows = pl.ds(i * step, step)
            inner = pl.ds(i * step + 1, step)
            shape = (step, lay.cols, lay.frames)
            s.first[rows] = reduced[:, :B0].reshape(shape + (B0,))
            thin = reduced[:, B0:].reshape(shape + (NARROW,))
            s.narrow[inner, 1 : lay.cols + 1] = thin
            s.border[inner, 1 : lay.cols + 1, :, 0:BP] = projected.reshape(shape + (BP,)).astype(BF16)
            s.border[inner, 1 : lay.cols + 1, :, BP:] = thin.astype(BF16)
            total, square, valid = sums
            return (
                total + column_sum(reduced),
                square + column_sum(reduced * reduced),
                valid + column_sum(mask),
            )

        zero = jnp.zeros((1, REDUCE), F32)
        return lax.fori_loop(0, lay.rows // step, body, (zero, zero, jnp.zeros((1, 1), F32)))

    def narrow_windows(lay, norm):
        s = lay.s
        average, scale, bias = norm
        rows, cols, t = lay.rows, lay.cols, lay.frames
        for row in (0, rows + 1):
            s.narrow[row] = s.border[row, :, :, BP:].astype(F32)
        for col in (0, cols + 1):
            s.narrow[1 : rows + 1, col] = s.border[1 : rows + 1, col, :, BP:].astype(F32)

        def body(row, carry):
            count = (cols + 2) * t
            z = s.narrow[row].reshape(count, NARROW)
            mask = s.mask[row].reshape(count, 1)
            value = jnp.where(mask > 0.0, softplus((z - average) * scale + bias), 0.0)
            before, after = shifted(lay, value)
            parts = (before, value, after)
            mid = jnp.concatenate([p[:, :B1R] for p in parts], axis=1)
            small = jnp.concatenate([p[:, B1R:] for p in parts], axis=1)
            s.mid_in[row] = mid.astype(BF16).reshape(cols + 2, t, 3 * B1R)
            s.small_in[row] = small.astype(BF16).reshape(cols + 2, t, 3 * B2R)
            s.box[row] = box_row(lay, s.border[row, :, :, 0:BP].astype(F32))
            return carry

        lax.fori_loop(0, rows + 2, body, 0)

    def box_row(lay, value):
        cols, t = lay.cols, lay.frames
        flat = value.reshape((cols + 2) * t, BP)
        before, after = shifted(lay, flat)
        flat = (flat + before + after).reshape(cols + 2, t, BP)
        return flat[0:cols] + flat[1 : cols + 1] + flat[2 : cols + 2]

    def box_rows(lay, row):
        box = lay.s.box
        total = box[row] + box[row + 1] + box[row + 2]
        return total.reshape(lay.row_cells, BP) * (1.0 / 27.0)

    def window(lay, ref, row, col, width):
        value = ref[pl.ds(row, lay.rows), pl.ds(col, lay.cols)]
        return value.reshape(lay.cells, width)

    def cube_conv(lay):
        s, at = lay.s, lay.index
        s.mid[:, 0:B1] = jnp.zeros((lay.cells, B1), F32)
        s.small[...] = jnp.zeros(s.small.shape, F32)

        def body(tap, carry):
            row, col = lax.div(tap, 3), lax.rem(tap, 3)
            s.mid[:, 0:B1] += dot(window(lay, s.mid_in, row, col, 3 * B1R), mid_kernel(at, tap))
            s.small[...] += dot(window(lay, s.small_in, row, col, 3 * B2R), small_kernel(at, tap))
            return carry

        lax.fori_loop(0, 9, body, 0)

    def mid_kernel(at, tap):
        return jnp.concatenate([k.v_w_mid[at, 9 * t + tap] for t in range(3)], axis=0)

    def small_kernel(at, tap):
        return jnp.concatenate([k.v_w_small[at, 9 * t + tap] for t in range(3)], axis=0)

    def second_rows(lay, row, count=1):
        cells = pl.ds(pl.multiple_of(row * lay.row_cells, lay.row_cells), count * lay.row_cells)
        return [
            ref[cells, 0:n] for ref, n in zip((lay.s.mid, lay.s.small, lay.s.pool), SECOND)
        ]

    def second_sums(lay):
        def body(row, sums):
            cells = pl.ds(pl.multiple_of(row * lay.row_cells, lay.row_cells), lay.row_cells)
            lay.s.pool[cells, :] = box_rows(lay, row)
            mask = center_mask(lay, row)
            out = []
            for (total, square), value in zip(sums, second_rows(lay, row)):
                inside = value * mask
                out.append((total + column_sum(inside), square + column_sum(inside * value)))
            return tuple(out)

        zero = tuple((jnp.zeros((1, n), F32),) * 2 for n in SECOND)
        return lax.fori_loop(0, lay.rows, body, zero)

    def put_second(at, sums):
        for which in range(2):
            for begin, part, width in zip(SECOND_AT, sums, SECOND):
                begin += which * SECOND_WIDTH
                k.sums[at, :, begin : begin + width] = part[which]

    def get_second(total, which):
        return [total[:, which * SECOND_WIDTH + a : which * SECOND_WIDTH + a + n] for a, n in zip(SECOND_AT, SECOND)]

    def put_first(at, sums):
        for which in range(2):
            k.sums[at, :, which * 512 : which * 512 + REDUCE] = sums[which]

    def get_first(total, which):
        return total[:, which * 512 : which * 512 + REDUCE]

    def second_params(k_of, at):
        row = k_of[at]
        out, begin = [], REDUCE
        for width in SECOND:
            out.append(row[:, begin : begin + width])
            begin += width
        return out

    def first_params(k_of, at):
        return k_of[at][:, :REDUCE]

    def forward(lay, at, count):
        s = lay.s
        total, square, valid = reduce_conv(lay)
        start_halo(lay, s.border, 2 * lay.index)
        put_first(at, (total, square))
        if count is None:
            k.sums[at, :, 1024:1152] = jnp.broadcast_to(valid, (1, 128))
        start_sum(at)
        end_halo(lay, s.border, 2 * lay.index)
        summed = end_sum(at)
        if count is None:
            count = summed[:, 1024:1025]
        average, inv_std, scale = batch_norm_scale(
            get_first(summed, 0), get_first(summed, 1), count, first_params(k.gain, lay.index)
        )
        first = (average, inv_std, scale, first_params(k.bias, lay.index))
        narrow_windows(lay, (average[:, B0:], scale[:, B0:], first[3][:, B0:]))
        cube_conv(lay)
        put_second(at + 1, second_sums(lay))
        start_sum(at + 1)
        summed = end_sum(at + 1)
        second = []
        for total, square, gain, bias in zip(
            get_second(summed, 0),
            get_second(summed, 1),
            second_params(k.gain, lay.index),
            second_params(k.bias, lay.index),
        ):
            second.append(batch_norm_scale(total, square, count, gain) + (bias,))
        return first, second, count

    def normalised(value, norm):
        average, inv_std, scale, bias = norm
        return (value - average) * inv_std

    def affine(value, norm):
        average, inv_std, scale, bias = norm
        return (value - average) * scale + bias

    def left_half(norm):
        return tuple(p[:, :B0] for p in norm)

    def outputs(lay, row, first, second):
        mask = center_mask(lay, row)
        z = lay.s.first[row].reshape(lay.row_cells, B0)
        parts = [softplus(affine(z, left_half(first))) * mask]
        values = second_rows(lay, row)
        parts += [softplus(affine(v, n)) * mask for v, n in zip(values, second)]
        for begin, width, v, n in zip(SECOND_AT, SECOND, values, second):
            normed = normalised(v, n).astype(BF16).reshape(lay.cols, lay.frames, width)
            lay.s.normed[row + 1, 1 : lay.cols + 1, :, begin : begin + width] = normed
        return parts

    for copy in loads[:3]:
        copy.wait()
    beside = (w > 0).astype(jnp.int32) + (w < n_wa - 1).astype(jnp.int32)
    pl.semaphore_wait(barrier, chips + beside)

    for copy in loads[3:]:
        copy.wait()
    first_one, second_one, count_one = forward(one, 0, None)

    def halve(row, carry):
        low = outputs(one, 2 * row, first_one, second_one)
        high = outputs(one, 2 * row + 1, first_one, second_one)
        begin = 0
        for p, q in zip(low, high):
            width = p.shape[-1]
            both = (p + q).reshape(two.cols, 2, one.frames, width)
            both = both[:, 0] + both[:, 1]
            for lane in range(0, width, 128):
                size = min(128, width - lane)
                k.pairs[:, begin + lane // 128, :, 0:size] = both[:, :, lane : lane + size]
            begin += -(-width // 128)
        for col in range(two.cols):
            tiles = []
            for lane in range(begin):
                even = k.pairs[col, lane, pl.ds(0, two.frames, stride=2), :]
                odd = k.pairs[col, lane, pl.ds(1, two.frames, stride=2), :]
                tiles.append((even + odd) * 0.125)
            half = (B0 + B1) // 128
            tiles[half] = tiles[half][:, : (B0 + B1) % 128]
            mean = jnp.concatenate(tiles, axis=1)
            two.s.block_in[row, col] = mean.astype(BF16)
        return carry

    lax.fori_loop(0, two.rows, halve, 0)
    start_halo(one, one.s.normed, 1)

    first_two, second_two, count_two = forward(two, 2, count_one * 0.125)

    def finish(row, carry):
        parts = outputs(two, row, first_two, second_two)
        value = jnp.concatenate(parts, axis=1).astype(BF16)
        k.block_output[row] = value.reshape(two.cols, two.frames, value.shape[-1])
        return carry

    lax.fori_loop(0, two.rows, finish, 0)
    start_halo(two, two.s.normed, 3)

    def backward(lay, out_slope, border_slope, at, first, second, count, before_end):
        s, index = lay.s, lay.index

        def second_slope(row):
            mask = center_mask(lay, row)
            slopes = out_slope(row)[1:]
            values = second_rows(lay, row)
            normed = [normalised(v, n) for v, n in zip(values, second)]
            slopes = [
                g * mask * sigmoid(m * (n[2] / n[1]) + n[3])
                for g, m, n in zip(slopes, normed, second)
            ]
            return mask, normed, slopes

        def sum_body(row, sums):
            mask, normed, slopes = second_slope(row)
            return tuple(
                (t + column_sum(g), q + column_sum(g * m))
                for (t, q), g, m in zip(sums, slopes, normed)
            )

        zero = tuple((jnp.zeros((1, n), F32),) * 2 for n in SECOND)
        put_second(at, lax.fori_loop(0, lay.rows, sum_body, zero))
        start_sum(at)
        before_end()
        progress(index, 7)
        summed = end_sum(at)
        totals = list(zip(get_second(summed, 0), get_second(summed, 1)))
        begin = REDUCE
        for (bias_grad, gain_grad), width in zip(totals, SECOND):
            k.bias_grad[index, :, begin : begin + width] = bias_grad
            k.gain_grad[index, :, begin : begin + width] = gain_grad
            begin += width

        def pre_slope(g, m, norm, total):
            return norm[2] * (g - (total[0] + m * total[1]) / count)

        def center_body(row, carry):
            mask, normed, slopes = second_slope(row)
            for a, width, g, m, n, total in zip(SECOND_AT, SECOND, slopes, normed, second, totals):
                value = (pre_slope(g, m, n, total) * mask).astype(BF16)
                s.normed[row + 1, 1 : lay.cols + 1, :, a : a + width] = value.reshape(
                    lay.cols, lay.frames, width
                )
            return carry

        lax.fori_loop(0, lay.rows, center_body, 0)

        def border_cells(row, col):
            mask = s.mask[row, col]
            normed = s.normed[row, col].astype(F32)
            slopes = border_slope(row, col)
            for a, width, g, n, total in zip(SECOND_AT, SECOND, slopes, second, totals):
                m = normed[:, a : a + width]
                g = g * sigmoid(m * (n[2] / n[1]) + n[3])
                value = jnp.where(mask > 0.0, pre_slope(g, m, n, total), 0.0)
                s.normed[row, col, :, a : a + width] = value.astype(BF16)

        def across(col, carry):
            border_cells(0, col)
            border_cells(lay.rows + 1, col)
            return carry

        lax.fori_loop(0, lay.cols + 2, across, 0)

        def along(row, carry):
            border_cells(row, 0)
            border_cells(row, lay.cols + 1)
            return carry

        lax.fori_loop(1, lay.rows + 1, along, 0)

        center = s.normed[1 : lay.rows + 1, 1 : lay.cols + 1].reshape(lay.cells, SECOND_WIDTH)
        turned_mid = center[:, 0:B1].T
        turned_small = center[:, 384:512].T

        def tap_body(tap, carry):
            row, col = lax.div(tap, 3), lax.rem(tap, 3)
            mid = dot(turned_mid, window(lay, s.mid_in, row, col, 3 * B1R)).astype(BF16)
            small = dot(turned_small, window(lay, s.small_in, row, col, 3 * B2R)).astype(BF16)
            store_blocks(index, tap * TAP_BLOCKS, mid)
            store_blocks(index, tap * TAP_BLOCKS + 80, small)
            return carry

        lax.fori_loop(0, 4, tap_body, 0)
        start_exchange(index, 0)
        lax.fori_loop(4, 9, tap_body, 0)
        start_exchange(index, 1)
        progress(index, 0)

        s.mid[...] = jnp.zeros(s.mid.shape, F32)
        s.small[:, 0 : 3 * B2R] = jnp.zeros((lay.cells, 3 * B2R), F32)

        def back_body(tap, carry):
            row, col = 2 - lax.div(tap, 3), 2 - lax.rem(tap, 3)
            slope = window(lay, s.normed, row, col, SECOND_WIDTH)
            s.mid[...] += dot(slope[:, 0:B1], mid_kernel(index, tap), NT)
            s.small[:, 0 : 3 * B2R] += dot(slope[:, 384:512], small_kernel(index, tap), NT)
            return carry

        for part in range(3):
            lax.fori_loop(3 * part, 3 * part + 3, back_body, 0)
            progress(index, 1 + part)

        def box_body(row, carry):
            s.box[row] = box_row(lay, s.normed[row, :, :, 512:640].astype(F32))
            return carry

        lax.fori_loop(0, lay.rows + 2, box_body, 0)

        def first_body(row, sums):
            cells = pl.ds(pl.multiple_of(row * lay.row_cells, lay.row_cells), lay.row_cells)
            s.projected_slope[cells, :] = box_rows(lay, row).astype(BF16)
            mid = s.mid[cells, :]
            small = s.small[cells, 0 : 3 * B2R]
            thirds = [
                jnp.concatenate(
                    [mid[:, B1R * t : B1R * (t + 1)], small[:, B2R * t : B2R * (t + 1)]], axis=1
                )
                for t in range(3)
            ]
            thin = thirds[1] + shifted(lay, thirds[2])[0] + shifted(lay, thirds[0])[1]
            mask = center_mask(lay, row)
            z = s.first[row].reshape(lay.row_cells, B0)
            z_thin = s.narrow[row + 1, 1 : lay.cols + 1].reshape(lay.row_cells, NARROW)
            normed = normalised(jnp.concatenate([z, z_thin], axis=1), first)
            g = jnp.concatenate([out_slope(row)[0], thin], axis=1)
            g = g * mask * sigmoid(normed * (first[2] / first[1]) + first[3])
            s.mid[cells, 0:REDUCE] = g
            return sums[0] + column_sum(g), sums[1] + column_sum(g * normed)

        zero = (jnp.zeros((1, REDUCE), F32),) * 2
        put_first(at + 1, lax.fori_loop(0, lay.rows, first_body, zero))
        start_sum(at + 1)

        progress(index, 4)
        store_blocks(index, LOW_AT + 196, dot(s.projected_slope[...].T, flat_block(lay)).astype(BF16))
        progress(index, 5)
        summed = end_sum(at + 1)
        total = (get_first(summed, 0), get_first(summed, 1))
        k.bias_grad[index, :, 0:REDUCE] = total[0]
        k.gain_grad[index, :, 0:REDUCE] = total[1]

        def low_body(row, carry):
            cells = pl.ds(pl.multiple_of(row * lay.row_cells, lay.row_cells), lay.row_cells)
            mask = center_mask(lay, row)
            z = s.first[row].reshape(lay.row_cells, B0)
            z_thin = s.narrow[row + 1, 1 : lay.cols + 1].reshape(lay.row_cells, NARROW)
            normed = normalised(jnp.concatenate([z, z_thin], axis=1), first)
            value = (pre_slope(s.mid[cells, 0:REDUCE], normed, first, total) * mask).astype(BF16)
            s.low[cells, :] = value
            slope = dot(value, k.v_w_reduce[index])
            slope = slope + dot(s.projected_slope[cells, :], k.v_w_pool[index], NT)
            lay.put_slope(row, slope * mask)
            return carry

        lax.fori_loop(0, lay.rows, low_body, 0)
        store_blocks(index, LOW_AT, dot(s.low[...].T, flat_block(lay)).astype(BF16))
        start_exchange(index, 2)
        progress(index, 6)

    def split(value):
        a, b_, c, d = B0, B0 + B1, B0 + B1 + B2, B0 + B1 + B2 + BP
        return [value[:, :a], value[:, a:b_], value[:, b_:c], value[:, c:d]]

    def spread_two(row, carry):
        value = k.v_out_grad[row].astype(F32).reshape(two.row_cells, k.v_out_grad.shape[-1])
        for a, part, width in zip(SECOND_AT, split(value)[1:], SECOND):
            part = part.reshape(two.cols, two.frames, width)
            k.grad_border[0, row + 1, 1 : two.cols + 1, :, a : a + width] = part.astype(BF16)
        return carry

    lax.fori_loop(0, two.rows, spread_two, 0)
    start_halo(two, k.grad_border.at[0], 4)

    def slope_two(row):
        value = k.v_out_grad[row].astype(F32).reshape(two.row_cells, k.v_out_grad.shape[-1])
        return split(value)

    def border_two(row, col):
        value = k.grad_border[0, row, col].astype(F32)
        return [value[:, a : a + n] for a, n in zip(SECOND_AT, SECOND)]

    def widen(ref, begin, value):
        width = value.shape[-1]
        for lane in range(0, width, 128):
            size = min(128, width - lane)
            for odd in range(2):
                ref[(begin + lane) // 128, pl.ds(odd, two.frames, stride=2), 0:size] = value[
                    :, lane : lane + size
                ]

    def wide(value, a, width):
        tiles = [value[..., lane // 128, :, :] for lane in range(a, a + width, 128)]
        return jnp.concatenate(tiles, axis=-1)[..., :width]

    def put_two(row, slope):
        slope = slope * 0.125
        for a, part in zip((0,) + tuple(B0 + a for a in SECOND_AT), split(slope)):
            width = part.shape[-1]
            part = part.reshape(two.cols, two.frames, width)
            for col in range(two.cols):
                widen(k.spread.at[row, col], a, part[col])
            if a >= B0:
                k.grad_border[1, row + 1, 1 : two.cols + 1, :, a - B0 : a - B0 + width] = part.astype(BF16)

    two.put_slope = put_two

    def end_two():
        end_halo(two, two.s.normed, 3)
        end_halo(two, k.grad_border.at[0], 4)

    backward(two, slope_two, border_two, 4, first_two, second_two, count_two, end_two)
    start_halo(two, k.grad_border.at[1], 5)

    def slope_one(row):
        value = k.spread[lax.div(row, 2)]
        out = []
        for a, width in zip((0,) + tuple(B0 + a for a in SECOND_AT), (B0,) + SECOND):
            part = wide(value, a, width)
            pieces = [part[col // 2] for col in range(one.cols)]
            out.append(jnp.concatenate(pieces, axis=0))
        return out

    def border_one(row, col):
        value = k.border_spread[lax.div(row + 1, 2), lax.div(col + 1, 2)]
        return [wide(value, a, n) for a, n in zip(SECOND_AT, SECOND)]

    def end_one():
        end_halo(one, one.s.normed, 1)
        end_halo(two, k.grad_border.at[1], 5)

        def widen_border(row, col):
            value = k.grad_border[1, row, col].astype(F32)
            widen(k.border_spread.at[row, col], 0, value)

        def across(col, carry):
            widen_border(0, col)
            widen_border(two.rows + 1, col)
            return carry

        lax.fori_loop(0, two.cols + 2, across, 0)

        def along(row, carry):
            widen_border(row, 0)
            widen_border(row, two.cols + 1)
            return carry

        lax.fori_loop(1, two.rows + 1, along, 0)

    def put_one(row, slope):
        k.input_grad[row] = slope.astype(BF16).reshape(one.cols, one.frames, slope.shape[-1])

    one.put_slope = put_one
    backward(one, slope_one, border_one, 6, first_one, second_one, count_one, end_one)
    for key in LAST_STEPS:
        next(exchanges[key], None)
    for steps in exchanges.values():
        for _ in steps:
            pass


def unpack_body(taps, low, mid_out, small_out, reduce_out, pool_out, unit):
    def lanes(blocks, tiles, rows, width):
        parts = []
        for tile in range(tiles):
            size = min(128, width - 128 * tile)
            part = blocks[tile * (rows // 16) : (tile + 1) * (rows // 16), :, 0:size]
            parts.append(part.reshape(rows, size))
        return parts

    @pl.when((pl.program_id(0) == 0) & (pl.program_id(1) == 0))
    def _():
        shape = unit.shape
        same = lax.broadcasted_iota(jnp.int32, shape, 0) == lax.broadcasted_iota(jnp.int32, shape, 1)
        unit[...] = same.astype(F32).astype(BF16)

    mid = jnp.concatenate(lanes(taps.at[0], 4, B1, 3 * B1R), axis=1)
    mid = dot(unit[...], mid, NT)
    small = lanes(taps.at[0, 80:88], 1, B2, 3 * B2R)[0]
    small = dot(unit[0 : 3 * B2R, 0 : 3 * B2R], small, NT)
    for t in range(3):
        mid_out[0, t, 0] = mid[B1R * t : B1R * (t + 1)]
        small_out[0, t, 0] = small[B2R * t : B2R * (t + 1)]

    @pl.when(pl.program_id(1) == 0)
    def _():
        channels = reduce_out.shape[-1]
        tiles = -(-channels // 128)
        for at, part in enumerate(lanes(low.at[0, 0:196], tiles, REDUCE, channels)):
            reduce_out[0, :, 128 * at : 128 * at + part.shape[1]] = part.astype(F32)
        for at, part in enumerate(lanes(low.at[0, 196:252], tiles, BP, channels)):
            size = part.shape[1]
            pool_out[0, 128 * at : 128 * at + size, :] = dot(unit[0:size, 0:size], part, NT)


def unpack(grads, channels):
    grid = (2, 9)
    shapes = ((2, 3, 9, B1R, B1), (2, 3, 9, B2R, B2), (2, REDUCE, channels), (2, channels, BP))
    mid_grad, small_grad, reduce_grad, pool_grad = pl.pallas_call(
        unpack_body,
        grid=grid,
        out_shape=[jax.ShapeDtypeStruct(shape, F32) for shape in shapes],
        in_specs=[
            pl.BlockSpec((1, TAP_BLOCKS, 16, 128), lambda i, j: (i, j, 0, 0)),
            pl.BlockSpec((1, 256, 16, 128), lambda i, j: (i, LOW_OUT // 256, 0, 0)),
        ],
        out_specs=[
            pl.BlockSpec((1, 3, 1, B1R, B1), lambda i, j: (i, 0, j, 0, 0)),
            pl.BlockSpec((1, 3, 1, B2R, B2), lambda i, j: (i, 0, j, 0, 0)),
            pl.BlockSpec((1, REDUCE, channels), lambda i, j: (i, 0, 0)),
            pl.BlockSpec((1, channels, BP), lambda i, j: (i, 0, 0)),
        ],
        scratch_shapes=[pltpu.VMEM((3 * B1R, 3 * B1R), BF16)],
        compiler_params=pltpu.CompilerParams(vmem_limit_bytes=40 * 1024 * 1024),
        name="unpack",
    )(grads, grads)
    return (
        jnp.swapaxes(reduce_grad, 1, 2),
        mid_grad.reshape(2, 27, B1R, B1),
        small_grad.reshape(2, 27, B2R, B2),
        pool_grad,
    )


def on_device(
    n_batch, n_wa, clip_features, frame_counts, w_reduce, w_mid, w_small, w_pool, norm_gain, norm_bias, out_grad
):
    frames, rows, cols, channels = clip_features.shape
    clips = frame_counts.shape[0]
    slot = frames // clips
    layers = (
        Layer(0, rows, cols, clips, slot),
        Layer(1, rows // 2, cols // 2, clips, slot // 2),
    )
    one, two = layers
    chips = n_batch * n_wa

    def cells_first(array):
        return array.transpose(1, 2, 0, 3)

    operands = dict(
        features=cells_first(clip_features),
        frame_counts=frame_counts,
        w_reduce=jnp.swapaxes(w_reduce, 1, 2),
        w_mid=w_mid,
        w_small=w_small,
        w_pool=w_pool,
        gain=norm_gain.reshape(2, 1, -1),
        bias=norm_bias.reshape(2, 1, -1),
        out_grad=cells_first(out_grad),
    )
    in_space = dict(frame_counts=pltpu.SMEM, gain=pltpu.VMEM, bias=pltpu.VMEM)
    out_space = dict(weight_grads=pl.ANY)
    results = dict(
        block_output=jax.ShapeDtypeStruct((two.rows, two.cols, two.frames, channels), BF16),
        input_grad=jax.ShapeDtypeStruct((rows, cols, frames, channels), BF16),
        weight_grads=jax.ShapeDtypeStruct((2, LOW_OUT + 256, 16, 128), BF16),
        gain_grad=jax.ShapeDtypeStruct(norm_gain[:, None].shape, F32),
        bias_grad=jax.ShapeDtypeStruct(norm_bias[:, None].shape, F32),
    )
    scratch = {}
    for name in ("w_reduce", "w_mid", "w_small", "w_pool", "out_grad"):
        scratch["v_" + name] = pltpu.VMEM(operands[name].shape, BF16)
    small_pad = (two.rows + 2, two.cols + 2)
    scratch.update(
        pairs=pltpu.VMEM((two.cols, (B0 + SECOND_WIDTH) // 128, one.frames, 128), F32),
        spread=pltpu.VMEM(
            (two.rows, two.cols, (B0 + SECOND_WIDTH) // 128, one.frames, 128), F32
        ),
        border_spread=pltpu.VMEM(small_pad + (SECOND_WIDTH // 128, one.frames, 128), F32),
        grad_border=pltpu.VMEM((2,) + small_pad + (two.frames, SECOND_WIDTH), BF16),
        sums=pltpu.VMEM((8, 1, SUM_WIDTH), F32),
        pair_sums=pltpu.VMEM((8, 1, SUM_WIDTH), F32),
        chip_sums=pltpu.VMEM((2, chips, 1, SUM_WIDTH), F32),
        load_sem=pltpu.SemaphoreType.DMA((6,)),
        pair_sem=pltpu.SemaphoreType.DMA((2, 8)),
        chip_sem=pltpu.SemaphoreType.DMA((2, 8)),
        halo_sem=pltpu.SemaphoreType.DMA((2, 6, 5)),
        grads=pltpu.VMEM((2, GRAD_BLOCKS, 16, 128), BF16),
        got_half=pltpu.VMEM((2, GRAD_BLOCKS // 2, 16, 128), BF16),
        got_eighth=pltpu.VMEM((2, GRAD_BLOCKS // 4, 16, 128), BF16),
        got_piece=pltpu.VMEM((2, GRAD_BLOCKS // 8, 16, 128), BF16),
        got_chunk=pltpu.VMEM((2, n_batch, GRAD_BLOCKS // 32, 16, 128), BF16),
        got_total=pltpu.VMEM((2, OWNERS, GRAD_BLOCKS // 32, 16, 128), BF16),
        free_sem=pltpu.SemaphoreType.REGULAR((2, 3, 3)),
        grad_sem=pltpu.SemaphoreType.DMA((2, 2, 3, 18)),
        out_sem=pltpu.SemaphoreType.DMA((2, 3)),
    )
    names = list(operands) + list(results) + list(scratch)
    layer_scratch = [lay.scratch(channels) for lay in layers]

    def body(*refs):
        rest = refs[len(names) :]
        for lay, parts in zip(layers, layer_scratch):
            lay.s = SimpleNamespace(**dict(zip(parts, rest[: len(parts)])))
            rest = rest[len(parts) :]
        kernel_body(names, (n_batch, n_wa, layers), refs[: len(names)])

    out = pl.pallas_call(
        body,
        out_shape=list(results.values()),
        in_specs=[pl.BlockSpec(memory_space=in_space.get(name, pl.ANY)) for name in operands],
        out_specs=[pl.BlockSpec(memory_space=out_space.get(name, pltpu.VMEM)) for name in results],
        scratch_shapes=list(scratch.values()) + [r for parts in layer_scratch for r in parts.values()],
        compiler_params=pltpu.CompilerParams(
            collective_id=0, has_side_effects=True, vmem_limit_bytes=63 * 1024 * 1024
        ),
        name="layers",
    )(*operands.values())
    out = dict(zip(results, out))

    reduce_grad, mid_grad, small_grad, pool_grad = unpack(out["weight_grads"], channels)

    return (
        out["block_output"].transpose(2, 0, 1, 3),
        out["input_grad"].transpose(2, 0, 1, 3),
        reduce_grad,
        mid_grad,
        small_grad,
        pool_grad,
        out["gain_grad"].reshape(norm_gain.shape),
        out["bias_grad"].reshape(norm_bias.shape),
    )


def solution(mesh):
    in_specs = (
        P("batch", "ha", "wa", None),
        P("batch"),
        P(),
        P(),
        P(),
        P(),
        P(),
        P(),
        P("batch", "ha", "wa", None),
    )
    out_specs = (
        P("batch", "ha", "wa", None),
        P("batch", "ha", "wa", None),
        P(),
        P(),
        P(),
        P(),
        P(),
        P(),
    )
    return jax.shard_map(
        functools.partial(on_device, mesh.shape["batch"], mesh.shape["wa"]),
        mesh=mesh,
        in_specs=in_specs,
        out_specs=out_specs,
        check_vma=False,
    )
```

```python
import functools
from types import SimpleNamespace

import jax
import jax.numpy as jnp
from jax import lax
from jax.experimental import pallas as pl
from jax.experimental.pallas import tpu as pltpu
from jax.sharding import PartitionSpec as P

HEIGHT = 14
EPSILON = 1e-05
MESH = pl.DeviceIdType.MESH
F32 = jnp.float32
BF16 = jnp.bfloat16

B0, B1R, B2R, B1, B2, BP = 256, 160, 32, 320, 128, 128
NARROW = B1R + B2R
REDUCE = B0 + NARROW
SECOND = (B1, B2, BP)
SECOND_AT = (0, 384, 512)
SECOND_WIDTH = 640
SUM_WIDTH = 1280
AXES = ("batch", "ha", "wa")

TAP_BLOCKS = 88
LOW_AT = 800
LOW_OUT = 1024
GRAD_BLOCKS = 1056
BUNDLES = ((0, 352), (352, 448), (800, 256))
OWNERS = 4

SCHEDULE = {
    (1, (5, 3)): ((1, 0),),
    (1, (5, 8)): ((1, 1),),
    (1, 7): ((1, 0),),
    (1, 8): ((1, 2), (1, 1)),
    (0, 0): ((1, 2),),
    (0, 1): ((1, 0),),
    (0, (2, 0)): ((1, 1),),
    (0, (2, 3)): ((1, 2),),
    (0, (2, 5)): ((1, 0),),
    (0, (2, 8)): ((1, 1),),
    (0, 3): ((1, 2),),
    (0, (5, 1)): ((1, 0),),
    (0, (5, 3)): ((0, 0),),
    (0, (5, 7)): ((0, 0), (1, 1)),
    (0, (5, 8)): ((0, 1),),
    (0, 7): ((1, 2),),
    (0, 8): ((0, 2), (0, 1)),
}
LAST_STEPS = (
    (1, 0),
    (0, 0),
    (0, 2),
    (1, 1),
    (0, 1),
    (1, 2),
    (1, 0),
    (0, 0),
    (0, 2),
    (1, 1),
    (0, 0),
    (0, 1),
    (1, 2),
    (1, 0),
    (0, 2),
    (0, 0),
    (1, 0),
    (1, 0),
    (1, 1),
    (0, 1),
    (1, 2),
    (1, 1),
    (0, 2),
    (0, 0),
    (1, 2),
    (1, 1),
    (1, 2),
    (0, 1),
    (0, 0),
    (0, 2),
    (0, 0),
    (0, 1),
    (0, 0),
    (0, 2),
    (0, 1),
    (0, 2),
    (0, 1),
    (0, 2),
    (0, 1),
    (0, 2),
)

NN = (((1,), (0,)), ((), ()))
NT = (((1,), (1,)), ((), ()))


def dot(a, b, dims=NN):
    return lax.dot_general(a, b, dims, preferred_element_type=F32)


def softplus(x):
    return jnp.maximum(x, 0.0) + jnp.log1p(jnp.exp(-jnp.abs(x)))


def sigmoid(x):
    return 1.0 / (1.0 + jnp.exp(-x))


def loop(count, body, init):
    return body(0, init) if count == 1 else lax.fori_loop(0, count, body, init)


class Layer:
    def __init__(self, index, rows, cols, clips, slot):
        self.index, self.rows, self.cols = index, rows, cols
        self.clips, self.slot = clips, slot
        self.frames = clips * slot
        self.cells = rows * cols * self.frames
        self.row_cells = cols * self.frames
        self.step = rows if index else 2
        self.pad_step = rows + 2 if index else 2

    def scratch(self, channels):
        r, c, t, n = self.rows, self.cols, self.frames, self.cells
        pad = (r + 2, c + 2, t)
        return dict(
            mask=pltpu.VMEM(pad + (1,), F32),
            block_in=pltpu.VMEM((r, c, t, channels), BF16),
            first=pltpu.VMEM((r, c, t, B0), F32),
            narrow=pltpu.VMEM(pad + (NARROW,), F32),
            border=pltpu.VMEM(pad + (BP + NARROW,), BF16),
            mid_in=pltpu.VMEM(pad + (3 * B1R,), BF16),
            small_in=pltpu.VMEM(pad + (3 * B2R,), BF16),
            box=pltpu.VMEM((r + 2, c, t, BP), F32),
            mid=pltpu.VMEM((n, 3 * B1R), F32),
            small=pltpu.VMEM((n, B2), F32),
            pool=pltpu.VMEM((n, BP), F32),
            normed=pltpu.VMEM(pad + (SECOND_WIDTH,), BF16),
            projected_slope=pltpu.VMEM((n, BP), BF16),
            low=pltpu.VMEM((n, REDUCE), BF16),
        )


def batch_norm_scale(total, square, count, gain):
    average = total / count
    variance = square / count - average * average
    inv_std = lax.rsqrt(variance + EPSILON)
    return average, inv_std, inv_std * gain


def kernel_body(names, sizes, refs):
    k = SimpleNamespace(**dict(zip(names, refs)))
    n_batch, n_wa, layers = sizes
    b, h, w = (lax.axis_index(a) for a in AXES)
    chips = n_batch * n_wa
    my_chip = b * n_wa + w
    one, two = layers

    def chip_at(p):
        return lax.div(p, n_wa), h, lax.rem(p, n_wa)

    def rotated(i):
        return lax.rem(my_chip + i, chips)

    def load(at, source, target):
        return pltpu.make_async_copy(source, target, k.load_sem.at[at])

    def load_features(i):
        rows = pl.ds(i * one.step, one.step)
        return pltpu.make_async_copy(k.features.at[rows], one.s.block_in.at[rows], k.feature_sem.at[i])

    def load_cubes(at, layer):
        copies = []
        for t in range(3):
            mid, small = pl.ds(B1R * t, B1R), pl.ds(B2R * t, B2R)
            copies.append(load(at + 2 * t, k.w_mid.at[layer, t], k.v_w_mid.at[layer, :, mid]))
            copies.append(load(at + 2 * t + 1, k.w_small.at[layer, t], k.v_w_small.at[layer, :, small]))
        return copies

    def load_flat(at, layer):
        return [
            load(at, k.w_reduce.at[layer], k.v_w_reduce.at[layer]),
            load(at + 1, k.w_pool.at[layer], k.v_w_pool.at[layer]),
        ]

    flat_one, flat_two = load_flat(0, 0), load_flat(2, 1)
    cubes_one, cubes_two = load_cubes(4, 0), load_cubes(10, 1)
    slope_load = load(16, k.out_grad, k.v_out_grad)
    for copy in flat_one:
        copy.start()
    for i in range(one.rows // one.step):
        load_features(i).start()
    for copy in cubes_one + [slope_load] + flat_two + cubes_two:
        copy.start()

    for lay in layers:
        s = lay.s
        for ref in (s.border, s.normed):
            for row in (0, lay.rows + 1):
                ref[row] = jnp.zeros(ref.shape[1:], ref.dtype)
            for col in (0, lay.cols + 1):
                ref[:, col] = jnp.zeros((ref.shape[0],) + ref.shape[2:], ref.dtype)
    ref = k.grad_border
    ref[...] = jnp.zeros(ref.shape, ref.dtype)
    for layer in range(2):
        for begin, end in ((9 * TAP_BLOCKS, LOW_AT), (LOW_AT + 252, GRAD_BLOCKS)):
            k.grads[layer, begin:end] = jnp.zeros((end - begin, 16, 128), BF16)
    k.sums[...] = jnp.zeros(k.sums.shape, F32)

    barrier = pltpu.get_barrier_semaphore()
    pl.semaphore_signal(barrier, inc=1, device_id=(b, 1 - h, w), device_id_type=MESH)

    @pl.when(w > 0)
    def _():
        pl.semaphore_signal(barrier, inc=1, device_id=(b, 1 - h, w - 1), device_id_type=MESH)

    @pl.when(w < n_wa - 1)
    def _():
        pl.semaphore_signal(barrier, inc=1, device_id=(b, 1 - h, w + 1), device_id_type=MESH)

    def greet(i, carry):
        pl.semaphore_signal(barrier, inc=1, device_id=chip_at(rotated(i)), device_id_type=MESH)
        return carry

    lax.fori_loop(1, chips, greet, 0)

    for lay in layers:
        frame_at = lax.broadcasted_iota(jnp.int32, (lay.frames, 1), 0)
        inside = jnp.zeros((lay.frames, 1), F32)
        for clip in range(lay.clips):
            valid = k.frame_counts[clip]
            valid = valid if lay.index == 0 else lax.div(valid, 2)
            begin = clip * lay.slot
            inside = jnp.where((frame_at >= begin) & (frame_at < begin + valid), 1.0, inside)
        height = HEIGHT if lay.index == 0 else HEIGHT // 2
        for row in range(lay.rows + 2):
            at_row = h * lay.rows + row - 1
            for col in range(lay.cols + 2):
                at_col = w * lay.cols + col - 1
                good = (at_row >= 0) & (at_row < height) & (at_col >= 0) & (at_col < height)
                lay.s.mask[row, col] = inside * good.astype(F32)

    def start_sum(at):
        pair = pltpu.make_async_remote_copy(
            src_ref=k.sums.at[at],
            dst_ref=k.pair_sums.at[at],
            send_sem=k.pair_sem.at[0, at],
            recv_sem=k.pair_sem.at[1, at],
            device_id=(b, 1 - h, w),
            device_id_type=MESH,
        )
        pair.start()
        pair.wait()
        k.chip_sums[at % 2, my_chip] = k.sums[at] + k.pair_sums[at]

        def send(i, carry):
            pltpu.make_async_remote_copy(
                src_ref=k.chip_sums.at[at % 2, my_chip],
                dst_ref=k.chip_sums.at[at % 2, my_chip],
                send_sem=k.chip_sem.at[0, at],
                recv_sem=k.chip_sem.at[1, at],
                device_id=chip_at(rotated(i)),
                device_id_type=MESH,
            ).start()
            return carry

        if chips <= 16:
            for i in range(1, chips):
                send(i, 0)
        else:
            lax.fori_loop(1, chips, send, 0)

    def end_sum(at):
        for way in (1, 0):
            others = k.chip_sums.at[at % 2, pl.ds(0, chips - 1)]
            pltpu.make_async_copy(others, others, k.chip_sem.at[way, at]).wait()
        total = k.chip_sums[at % 2, 0]
        for p in range(1, chips):
            total = total + k.chip_sums[at % 2, p]
        return total

    def halo_copies(lay, ref, at):
        src_row = jnp.where(h == 0, lay.rows, 1)
        dst_row = jnp.where(h == 0, 0, lay.rows + 1)
        rows, cols = lay.rows, lay.cols

        def remote(src, dst, way, device):
            return pltpu.make_async_remote_copy(
                src_ref=ref.at[src],
                dst_ref=ref.at[dst],
                send_sem=k.halo_sem.at[0, at, way],
                recv_sem=k.halo_sem.at[1, at, way],
                device_id=device,
                device_id_type=MESH,
            )

        all_rows, all_cols = pl.ds(1, rows), pl.ds(1, cols)
        row = remote((src_row, all_cols), (dst_row, all_cols), 0, (b, 1 - h, w))
        to_left = [
            remote((all_rows, 1), (all_rows, cols + 1), 1, (b, h, w - 1)),
            remote((src_row, 1), (dst_row, cols + 1), 2, (b, 1 - h, w - 1)),
        ]
        to_right = [
            remote((all_rows, cols), (all_rows, 0), 3, (b, h, w + 1)),
            remote((src_row, cols), (dst_row, 0), 4, (b, 1 - h, w + 1)),
        ]
        return row, to_left, to_right

    def start_halo(lay, ref, at):
        row, to_left, to_right = halo_copies(lay, ref, at)
        row.start()

        @pl.when(w > 0)
        def _():
            for copy in to_left:
                copy.start()

        @pl.when(w < n_wa - 1)
        def _():
            for copy in to_right:
                copy.start()

    def end_halo(lay, ref, at):
        row, to_left, to_right = halo_copies(lay, ref, at)
        row.wait()

        @pl.when(w > 0)
        def _():
            for copy in to_left:
                copy.wait_send()
            for copy in to_right:
                copy.wait_recv()

        @pl.when(w < n_wa - 1)
        def _():
            for copy in to_right:
                copy.wait_send()
            for copy in to_left:
                copy.wait_recv()

    def exchange(layer, number):
        begin, count = BUNDLES[number]
        half, quarter, eighth = count // 2, count // 4, count // 8
        piece, chunk = count // 16, count // 32
        stride = n_batch // OWNERS
        g = k.grads.at[layer]
        r1, r2, r3, r4, r5 = (
            r.at[layer] for r in (k.got_half, k.got_eighth, k.got_piece, k.got_chunk, k.got_total)
        )
        to_half, to_eighth, to_piece, to_chunk = begin // 2, begin // 4, begin // 8, begin // 32

        def places():
            b, h, w = (lax.axis_index(a) for a in AXES)
            x, y = lax.rem(w, 2), lax.div(w, 2)
            at = SimpleNamespace(b=b, h=h, w=w)
            at.pair, at.beside, at.below = (b, 1 - h, w), (b, h, w + 1 - 2 * x), (b, h, w + 2 - 4 * y)
            at.mine, at.other = begin + h * half, begin + (1 - h) * half
            half_a, half_b = at.mine, at.mine + quarter
            at.eighth_a, at.eighth_b = half_a + x * eighth, half_b + y * eighth
            at.a, at.b_ = at.eighth_a + y * piece, at.eighth_b + x * piece
            at.sent_a, at.sent_b = half_a + (1 - x) * eighth, half_b + (1 - y) * eighth
            at.last_a, at.last_b = at.eighth_a + (1 - y) * piece, at.eighth_b + (1 - x) * piece
            at.rank = lax.div(b, stride)
            at.chunk = jnp.where(at.rank < 2, at.a, at.b_) + lax.rem(at.rank, 2) * chunk
            at.chunks = [(at.a, at.b_)[owner // 2] + owner % 2 * chunk for owner in range(OWNERS)]
            return at

        def copy(source, at, target, to, size, slot, device):
            return pltpu.make_async_remote_copy(
                src_ref=source.at[pl.ds(at, size)],
                dst_ref=target.at[pl.ds(to, size)],
                send_sem=k.grad_sem.at[0, layer, number, slot],
                recv_sem=k.grad_sem.at[1, layer, number, slot],
                device_id=device,
                device_id_type=MESH,
            )

        def pair_copies(at):
            return [copy(g, at.other, r1, to_half, half, 0, at.pair)]

        def eighth_copies(at):
            return [
                copy(g, at.sent_a, r2, to_eighth, eighth, 1, at.beside),
                copy(g, at.sent_b, r2, to_eighth + eighth, eighth, 2, at.below),
            ]

        def piece_copies(at):
            return [
                copy(g, at.last_a, r3, to_piece, piece, 3, at.below),
                copy(g, at.last_b, r3, to_piece + piece, piece, 4, at.beside),
            ]

        def piece_returns(at):
            return [
                copy(g, at.a, g, at.a, piece, 13, at.below),
                copy(g, at.b_, g, at.b_, piece, 14, at.beside),
            ]

        def eighth_returns(at):
            return [
                copy(g, at.eighth_a, g, at.eighth_a, eighth, 15, at.beside),
                copy(g, at.eighth_b, g, at.eighth_b, eighth, 16, at.below),
            ]

        def pair_returns(at):
            return [copy(g, at.mine, g, at.mine, half, 17, at.pair)]

        def go(copies):
            for c in copies:
                c.start()

        def end(copies):
            for c in copies:
                c.wait()

        def add(at, other, to, size):
            step = 16 if size % 16 == 0 else size

            def body(i, carry):
                mine = pl.ds(at + i * step, step)
                g[mine] = g[mine] + other[pl.ds(to + i * step, step)]
                return carry

            lax.fori_loop(0, size // step, body, 0)

        def free(slot, device):
            sem = k.free_sem.at[layer, number, slot]
            pl.semaphore_signal(sem, inc=1, device_id=device, device_id_type=MESH)

        def wait_free(slot):
            pl.semaphore_wait(k.free_sem.at[layer, number, slot], 1)

        def for_owner(at, do):
            if stride == 1:
                do()
            else:
                pl.when(lax.rem(at.b, stride) == 0)(do)

        def for_others(at, do):
            for owner in range(OWNERS):
                pl.when(at.b != owner * stride)(functools.partial(do, owner))

        def share_copies(at):
            return [
                pltpu.make_async_remote_copy(
                    src_ref=g.at[pl.ds(at.chunk, chunk)],
                    dst_ref=r5.at[at.rank, pl.ds(to_chunk, chunk)],
                    send_sem=k.grad_sem.at[0, layer, number, 9],
                    recv_sem=k.grad_sem.at[1, layer, number, 9 + at.rank],
                    device_id=(lax.rem(at.b + i, n_batch), at.h, at.w),
                    device_id_type=MESH,
                )
                for i in range(1, n_batch)
            ]

        def start_pair():
            go(pair_copies(places()))

        def start_eighths():
            at = places()
            end(pair_copies(at))
            free(0, at.pair)
            add(at.mine, r1, to_half, half)
            go(eighth_copies(at))

        def start_pieces():
            at = places()
            end(eighth_copies(at))
            add(at.eighth_a, r2, to_eighth, eighth)
            add(at.eighth_b, r2, to_eighth + eighth, eighth)
            go(piece_copies(at))

        def start_chunks():
            at = places()
            end(piece_copies(at))
            free(1, at.below)
            free(2, at.beside)
            add(at.a, r3, to_piece, piece)
            add(at.b_, r3, to_piece + piece, piece)

            def send_chunk(owner):
                pltpu.make_async_remote_copy(
                    src_ref=g.at[pl.ds(at.chunks[owner], chunk)],
                    dst_ref=r4.at[at.b, pl.ds(to_chunk, chunk)],
                    send_sem=k.grad_sem.at[0, layer, number, 5 + owner],
                    recv_sem=k.grad_sem.at[1, layer, number, 5],
                    device_id=(owner * stride, at.h, at.w),
                    device_id_type=MESH,
                ).start()

            for_others(at, send_chunk)

        def share_chunk():
            at = places()

            def collect():
                others = r4.at[pl.ds(0, n_batch - 1), pl.ds(to_chunk, chunk)]
                pltpu.make_async_copy(others, others, k.grad_sem.at[1, layer, number, 5]).wait()
                r4[at.b, pl.ds(to_chunk, chunk)] = g[pl.ds(at.chunk, chunk)]
                total = r4[0, pl.ds(to_chunk, chunk)].astype(F32)
                for slot in range(1, n_batch):
                    total = total + r4[slot, pl.ds(to_chunk, chunk)].astype(F32)
                g[pl.ds(at.chunk, chunk)] = total.astype(BF16)
                go(share_copies(at))

            for_owner(at, collect)

            def sent_chunk(owner):
                part = g.at[pl.ds(at.chunks[owner], chunk)]
                pltpu.make_async_copy(part, part, k.grad_sem.at[0, layer, number, 5 + owner]).wait()

            for_others(at, sent_chunk)

        def return_pieces():
            at = places()

            def shared():
                for c in share_copies(at):
                    c.wait_send()

            for_owner(at, shared)

            def take_chunk(owner):
                part = r5.at[owner, pl.ds(to_chunk, chunk)]
                pltpu.make_async_copy(part, part, k.grad_sem.at[1, layer, number, 9 + owner]).wait()
                g[pl.ds(at.chunks[owner], chunk)] = r5[owner, pl.ds(to_chunk, chunk)]

            for_others(at, take_chunk)
            wait_free(1)
            wait_free(2)
            go(piece_returns(at))

        def return_eighths():
            at = places()
            end(piece_returns(at))
            go(eighth_returns(at))

        def return_halves():
            at = places()
            end(eighth_returns(at))
            wait_free(0)
            go(pair_returns(at))

        def result():
            target = k.weight_grads.at[layer, pl.ds(LOW_OUT if begin == LOW_AT else begin, count)]
            sem = k.out_sem.at[layer, number]
            return pltpu.make_async_copy(g.at[pl.ds(begin, count)], target, sem)

        def start_result():
            end(pair_returns(places()))

            result().start()

        def end_result():
            result().wait()

        return (
            start_pair,
            start_eighths,
            start_pieces,
            start_chunks,
            share_chunk,
            return_pieces,
            return_eighths,
            return_halves,
            start_result,
            end_result,
        )

    exchanges = {(layer, number): exchange(layer, number) for layer in range(2) for number in range(3)}
    plan, taken = {}, dict.fromkeys(exchanges, 0)
    for point, keys in list(SCHEDULE.items()) + [(None, LAST_STEPS)]:
        for key in keys:
            plan.setdefault(point, []).append(exchanges[key][taken[key]])
            taken[key] += 1
    assert all(taken[key] == len(exchanges[key]) for key in exchanges)

    def progress(*point):
        for step in plan.get(point, ()):
            step()

    def flat_block(lay):
        block = lay.s.block_in[...]
        return block.reshape(lay.cells, block.shape[-1])

    def store_blocks(layer, at, value):
        rows, lanes = value.shape
        for lane in range(0, lanes, 128):
            size = min(128, lanes - lane)
            blocks = pl.ds(at + lane // 128 * (rows // 16), rows // 16)
            tile = value[:, lane : lane + size].reshape(rows // 16, 16, size)
            k.grads[layer, blocks, :, 0:size] = tile

    def column_sum(value):
        return jnp.sum(value, axis=0, keepdims=True)

    def center_mask(lay, row, count=1):
        mask = lay.s.mask[pl.ds(row + 1, count), 1 : lay.cols + 1]
        return mask.reshape(count * lay.row_cells, 1)

    def shifted(lay, value):
        count = value.shape[0]
        frame_at = lax.rem(lax.broadcasted_iota(jnp.int32, (count, 1), 0), lay.slot)
        before = jnp.where(frame_at == 0, 0.0, pltpu.roll(value, 1, 0))
        after = jnp.where(frame_at == lay.slot - 1, 0.0, pltpu.roll(value, count - 1, 0))
        return before, after

    def cells_of(lay, i):
        size = lay.step * lay.row_cells
        return pl.ds(i * size if isinstance(i, int) else pl.multiple_of(i * size, size), size)

    def reduce_conv(lay):
        s, at, step = lay.s, lay.index, lay.step
        count = step * lay.row_cells

        def body(i, sums):
            mask = center_mask(lay, i * step, step)
            if lay.index == 0:
                load_features(i).wait()
            block = s.block_in[pl.ds(i * step, step)]
            block = block.reshape(count, block.shape[-1])
            if lay.index == 0:
                block = (block.astype(F32) * mask).astype(BF16)
                shape = (step, lay.cols, lay.frames, block.shape[-1])
                s.block_in[pl.ds(i * step, step)] = block.reshape(shape)
            reduced = dot(block, k.v_w_reduce[at], NT)
            projected = dot(block, k.v_w_pool[at])
            rows = pl.ds(i * step, step)
            inner = pl.ds(i * step + 1, step)
            shape = (step, lay.cols, lay.frames)
            s.first[rows] = reduced[:, :B0].reshape(shape + (B0,))
            thin = reduced[:, B0:].reshape(shape + (NARROW,))
            s.narrow[inner, 1 : lay.cols + 1] = thin
            s.border[inner, 1 : lay.cols + 1, :, 0:BP] = projected.reshape(shape + (BP,)).astype(BF16)
            s.border[inner, 1 : lay.cols + 1, :, BP:] = thin.astype(BF16)
            total, square, valid = sums
            return (
                total + column_sum(reduced),
                square + column_sum(reduced * reduced),
                valid + column_sum(mask),
            )

        zero = jnp.zeros((1, REDUCE), F32)
        return loop(lay.rows // step, body, (zero, zero, jnp.zeros((1, 1), F32)))

    def narrow_windows(lay, norm):
        s = lay.s
        average, scale, bias = norm
        rows, cols, t, step = lay.rows, lay.cols, lay.frames, lay.pad_step
        for row in (0, rows + 1):
            s.narrow[row] = s.border[row, :, :, BP:].astype(F32)
        for col in (0, cols + 1):
            s.narrow[1 : rows + 1, col] = s.border[1 : rows + 1, col, :, BP:].astype(F32)

        def body(i, carry):
            at = pl.ds(i * step, step)
            count = step * (cols + 2) * t
            z = s.narrow[at].reshape(count, NARROW)
            mask = s.mask[at].reshape(count, 1)
            value = jnp.where(mask > 0.0, softplus((z - average) * scale + bias), 0.0)
            before, after = shifted(lay, value)
            parts = (before, value, after)
            mid = jnp.concatenate([p[:, :B1R] for p in parts], axis=1)
            small = jnp.concatenate([p[:, B1R:] for p in parts], axis=1)
            s.mid_in[at] = mid.astype(BF16).reshape(step, cols + 2, t, 3 * B1R)
            s.small_in[at] = small.astype(BF16).reshape(step, cols + 2, t, 3 * B2R)
            s.box[at] = box_row(lay, s.border[at, :, :, 0:BP].astype(F32))
            return carry

        loop((rows + 2) // step, body, 0)

    def box_row(lay, value):
        cols, t, step = lay.cols, lay.frames, lay.pad_step
        flat = value.reshape(step * (cols + 2) * t, BP)
        before, after = shifted(lay, flat)
        flat = (flat + before + after).reshape(step, cols + 2, t, BP)
        return flat[:, 0:cols] + flat[:, 1 : cols + 1] + flat[:, 2 : cols + 2]

    def box_rows(lay, row):
        box, step = lay.s.box, lay.step
        total = box[pl.ds(row, step)] + box[pl.ds(row + 1, step)] + box[pl.ds(row + 2, step)]
        return total.reshape(step * lay.row_cells, BP) * (1.0 / 27.0)

    def window(lay, ref, row, col, width):
        value = ref[pl.ds(row, lay.rows), pl.ds(col, lay.cols)]
        return value.reshape(lay.cells, width)

    def taps(lay, body, at=None):
        if lay.index:
            for tap in range(9):
                body(tap, 0)
                progress(1, (at, tap))
            return

        def with_progress(tap, carry):
            body(tap, carry)
            for some in range(9):
                if (0, (at, some)) in SCHEDULE:

                    @pl.when(tap == some)
                    def _(some=some):
                        progress(0, (at, some))

            return carry

        lax.fori_loop(0, 9, with_progress, 0)

    def tap_at(tap):
        return (tap // 3, tap % 3) if isinstance(tap, int) else (lax.div(tap, 3), lax.rem(tap, 3))

    def cube_conv(lay):
        s, at = lay.s, lay.index
        s.mid[:, 0:B1] = jnp.zeros((lay.cells, B1), F32)
        s.small[...] = jnp.zeros(s.small.shape, F32)

        def body(tap, carry):
            row, col = tap_at(tap)
            s.mid[:, 0:B1] += dot(window(lay, s.mid_in, row, col, 3 * B1R), k.v_w_mid[at, tap])
            s.small[...] += dot(window(lay, s.small_in, row, col, 3 * B2R), k.v_w_small[at, tap])
            return carry

        taps(lay, body)

    def second_rows(lay, i):
        cells = cells_of(lay, i)
        return [
            ref[cells, 0:n] for ref, n in zip((lay.s.mid, lay.s.small, lay.s.pool), SECOND)
        ]

    def second_sums(lay):
        def body(i, sums):
            lay.s.pool[cells_of(lay, i), :] = box_rows(lay, i * lay.step)
            mask = center_mask(lay, i * lay.step, lay.step)
            out = []
            for (total, square), value in zip(sums, second_rows(lay, i)):
                inside = value * mask
                out.append((total + column_sum(inside), square + column_sum(inside * value)))
            return tuple(out)

        zero = tuple((jnp.zeros((1, n), F32),) * 2 for n in SECOND)
        return loop(lay.rows // lay.step, body, zero)

    def put_second(at, sums):
        for which in range(2):
            for begin, part, width in zip(SECOND_AT, sums, SECOND):
                begin += which * SECOND_WIDTH
                k.sums[at, :, begin : begin + width] = part[which]

    def get_second(total, which):
        return [total[:, which * SECOND_WIDTH + a : which * SECOND_WIDTH + a + n] for a, n in zip(SECOND_AT, SECOND)]

    def put_first(at, sums):
        for which in range(2):
            k.sums[at, :, which * 512 : which * 512 + REDUCE] = sums[which]

    def get_first(total, which):
        return total[:, which * 512 : which * 512 + REDUCE]

    def second_params(k_of, at):
        row = k_of[at]
        out, begin = [], REDUCE
        for width in SECOND:
            out.append(row[:, begin : begin + width])
            begin += width
        return out

    def first_params(k_of, at):
        return k_of[at][:, :REDUCE]

    def forward(lay, at, count, cubes, before, meanwhile):
        s = lay.s
        total, square, valid = reduce_conv(lay)
        before()
        start_halo(lay, s.border, 2 * lay.index)
        put_first(at, (total, square))
        if count is None:
            k.sums[at, :, 1024:1152] = jnp.broadcast_to(valid, (1, 128))
        start_sum(at)
        meanwhile()
        end_halo(lay, s.border, 2 * lay.index)
        for copy in cubes:
            copy.wait()
        summed = end_sum(at)
        if count is None:
            count = summed[:, 1024:1025]
        gain = first_params(k.gain, lay.index)
        first = batch_norm_scale(get_first(summed, 0), get_first(summed, 1), count, gain)
        first += (first_params(k.bias, lay.index), gain)
        narrow_windows(lay, (first[0][:, B0:], first[2][:, B0:], first[3][:, B0:]))
        cube_conv(lay)
        put_second(at + 1, second_sums(lay))
        start_sum(at + 1)
        summed = end_sum(at + 1)
        second = []
        for total, square, gain, bias in zip(
            get_second(summed, 0),
            get_second(summed, 1),
            second_params(k.gain, lay.index),
            second_params(k.bias, lay.index),
        ):
            second.append(batch_norm_scale(total, square, count, gain) + (bias, gain))
        return first, second, count

    def normalised(value, norm):
        average, inv_std, scale, bias, gain = norm
        return (value - average) * inv_std

    def affine(value, norm):
        average, inv_std, scale, bias, gain = norm
        return (value - average) * scale + bias

    def left_half(norm):
        return tuple(p[:, :B0] for p in norm)

    def outputs(lay, i, first, second):
        mask = center_mask(lay, i * lay.step, lay.step)
        z = lay.s.first[pl.ds(i * lay.step, lay.step)].reshape(lay.step * lay.row_cells, B0)
        parts = [softplus(affine(z, left_half(first))) * mask]
        parts += [softplus(affine(v, n)) * mask for v, n in zip(second_rows(lay, i), second)]
        return parts

    def put_normed(lay, second):
        def body(i, carry):
            inner = pl.ds(i * lay.step + 1, lay.step)
            for begin, width, v, n in zip(SECOND_AT, SECOND, second_rows(lay, i), second):
                normed = normalised(v, n).astype(BF16)
                normed = normed.reshape(lay.step, lay.cols, lay.frames, width)
                lay.s.normed[inner, 1 : lay.cols + 1, :, begin : begin + width] = normed
            return carry

        loop(lay.rows // lay.step, body, 0)

    for copy in flat_one:
        copy.wait()

    def wait_barrier():
        beside = (w > 0).astype(jnp.int32) + (w < n_wa - 1).astype(jnp.int32)
        pl.semaphore_wait(barrier, chips + beside)

    def spread_two():
        slope_load.wait()
        for a, part, width in zip(SECOND_AT, slope_two(0)[1:], SECOND):
            part = part.reshape(two.rows, two.cols, two.frames, width).astype(BF16)
            k.grad_border[0, 1 : two.rows + 1, 1 : two.cols + 1, :, a : a + width] = part
        start_halo(two, k.grad_border.at[0], 4)

    def split(value):
        a, b_, c, d = B0, B0 + B1, B0 + B1 + B2, B0 + B1 + B2 + BP
        return [value[:, :a], value[:, a:b_], value[:, b_:c], value[:, c:d]]

    def slope_two(i):
        value = k.v_out_grad[...].astype(F32)
        return split(value.reshape(two.cells, value.shape[-1]))

    first_one, second_one, count_one = forward(one, 0, None, cubes_one, wait_barrier, spread_two)

    def halve(row, carry):
        begin = 0
        for p in outputs(one, row, first_one, second_one):
            width = p.shape[-1]
            both = p.reshape(2, two.cols, 2, one.frames, width)
            both = both[0, :, 0] + both[0, :, 1] + both[1, :, 0] + both[1, :, 1]
            for lane in range(0, width, 128):
                size = min(128, width - lane)
                k.pairs[:, begin + lane // 128, :, 0:size] = both[:, :, lane : lane + size]
            begin += -(-width // 128)
        for col in range(two.cols):
            tiles = []
            for lane in range(begin):
                even = k.pairs[col, lane, pl.ds(0, two.frames, stride=2), :]
                odd = k.pairs[col, lane, pl.ds(1, two.frames, stride=2), :]
                tiles.append((even + odd) * 0.125)
            half = (B0 + B1) // 128
            tiles[half] = tiles[half][:, : (B0 + B1) % 128]
            mean = jnp.concatenate(tiles, axis=1)
            two.s.block_in[row, col] = mean.astype(BF16)
        return carry

    lax.fori_loop(0, two.rows, halve, 0)

    for copy in flat_two:
        copy.wait()

    def share_normed():
        put_normed(one, second_one)
        start_halo(one, one.s.normed, 1)

    first_two, second_two, count_two = forward(
        two, 2, count_one * 0.125, cubes_two, lambda: None, share_normed
    )

    def backward(lay, out_slope, border_slope, at, first, second, count, before_end):
        s, index, step = lay.s, lay.index, lay.step
        chunks = lay.rows // step
        per_cell = 1.0 / count

        def second_slope(i):
            mask = center_mask(lay, i * step, step)
            values = second_rows(lay, i)
            normed = [normalised(v, n) for v, n in zip(values, second)]
            slopes = [
                g * mask * sigmoid(m * n[4] + n[3])
                for g, m, n in zip(out_slope(i)[1:], normed, second)
            ]
            return mask, normed, slopes

        def sum_body(i, sums):
            mask, normed, slopes = second_slope(i)
            return tuple(
                (t + column_sum(g), q + column_sum(g * m))
                for (t, q), g, m in zip(sums, slopes, normed)
            )

        zero = tuple((jnp.zeros((1, n), F32),) * 2 for n in SECOND)
        put_second(at, loop(chunks, sum_body, zero))
        start_sum(at)
        before_end()
        progress(index, 0)
        summed = end_sum(at)
        totals = list(zip(get_second(summed, 0), get_second(summed, 1)))
        begin = REDUCE
        for (bias_grad, gain_grad), width in zip(totals, SECOND):
            k.bias_grad[index, :, begin : begin + width] = bias_grad
            k.gain_grad[index, :, begin : begin + width] = gain_grad
            begin += width
        totals = [(t * per_cell, q * per_cell) for t, q in totals]

        def pre_slope(g, m, norm, total):
            return norm[2] * (g - (total[0] + m * total[1]))

        def center_body(i, carry):
            mask, normed, slopes = second_slope(i)
            inner = pl.ds(i * step + 1, step)
            for a, width, g, m, n, total in zip(SECOND_AT, SECOND, slopes, normed, second, totals):
                value = (pre_slope(g, m, n, total) * mask).astype(BF16)
                s.normed[inner, 1 : lay.cols + 1, :, a : a + width] = value.reshape(
                    step, lay.cols, lay.frames, width
                )
            return carry

        loop(chunks, center_body, 0)

        def border_cells(where, slopes):
            mask = s.mask[where]
            cells = mask.shape[0]
            mask = mask.reshape(cells * lay.frames, 1)
            normed = s.normed[where].astype(F32).reshape(cells * lay.frames, SECOND_WIDTH)
            for a, width, g, n, total in zip(SECOND_AT, SECOND, slopes, second, totals):
                m = normed[:, a : a + width]
                g = g * sigmoid(m * n[4] + n[3])
                value = jnp.where(mask > 0.0, pre_slope(g, m, n, total), 0.0).astype(BF16)
                s.normed[where + (slice(None), slice(a, a + width))] = value.reshape(
                    cells, lay.frames, width
                )

        border_cells((jnp.where(h == 0, lay.rows + 1, 0), slice(None)), border_slope(True, None))
        for col in (0, lay.cols + 1):
            border_cells((slice(1, lay.rows + 1), col), border_slope(False, col > 0))

        progress(index, 1)
        s.mid[...] = jnp.zeros(s.mid.shape, F32)
        s.small[:, 0 : 3 * B2R] = jnp.zeros((lay.cells, 3 * B2R), F32)

        def back_body(tap, carry):
            row, col = tap_at(tap)
            slope = window(lay, s.normed, 2 - row, 2 - col, SECOND_WIDTH)
            s.mid[...] += dot(slope[:, 0:B1], k.v_w_mid[index, tap], NT)
            s.small[:, 0 : 3 * B2R] += dot(slope[:, 384:512], k.v_w_small[index, tap], NT)
            return carry

        taps(lay, back_body, 2)

        def box_body(i, carry):
            at = pl.ds(i * lay.pad_step, lay.pad_step)
            s.box[at] = box_row(lay, s.normed[at, :, :, 512:640].astype(F32))
            return carry

        loop((lay.rows + 2) // lay.pad_step, box_body, 0)
        progress(index, 3)

        def first_normed(i):
            size = step * lay.row_cells
            z = s.first[pl.ds(i * step, step)].reshape(size, B0)
            z_thin = s.narrow[pl.ds(i * step + 1, step), 1 : lay.cols + 1].reshape(size, NARROW)
            return normalised(jnp.concatenate([z, z_thin], axis=1), first)

        def first_body(i, sums):
            cells = cells_of(lay, i)
            s.projected_slope[cells, :] = box_rows(lay, i * step).astype(BF16)
            mid = s.mid[cells, :]
            small = s.small[cells, 0 : 3 * B2R]
            thirds = [
                jnp.concatenate(
                    [mid[:, B1R * t : B1R * (t + 1)], small[:, B2R * t : B2R * (t + 1)]], axis=1
                )
                for t in range(3)
            ]
            thin = thirds[1] + shifted(lay, thirds[2])[0] + shifted(lay, thirds[0])[1]
            mask = center_mask(lay, i * step, step)
            normed = first_normed(i)
            g = jnp.concatenate([out_slope(i)[0], thin], axis=1)
            g = g * mask * sigmoid(normed * first[4] + first[3])
            s.mid[cells, 0:REDUCE] = g
            return sums[0] + column_sum(g), sums[1] + column_sum(g * normed)

        zero = (jnp.zeros((1, REDUCE), F32),) * 2
        put_first(at + 1, loop(chunks, first_body, zero))
        start_sum(at + 1)

        progress(index, 4)

        center = s.normed[1 : lay.rows + 1, 1 : lay.cols + 1].reshape(lay.cells, SECOND_WIDTH)
        turned_mid = center[:, 0:B1].T
        turned_small = center[:, 384:512].T

        def tap_body(tap, carry):
            row, col = tap_at(tap)
            mid = dot(turned_mid, window(lay, s.mid_in, row, col, 3 * B1R)).astype(BF16)
            small = dot(turned_small, window(lay, s.small_in, row, col, 3 * B2R)).astype(BF16)
            store_blocks(index, tap * TAP_BLOCKS, mid)
            store_blocks(index, tap * TAP_BLOCKS + 80, small)
            return carry

        taps(lay, tap_body, 5)
        store_blocks(index, LOW_AT + 196, dot(s.projected_slope[...].T, flat_block(lay)).astype(BF16))
        progress(index, 6)
        summed = end_sum(at + 1)
        total = (get_first(summed, 0), get_first(summed, 1))
        k.bias_grad[index, :, 0:REDUCE] = total[0]
        k.gain_grad[index, :, 0:REDUCE] = total[1]

        total = (total[0] * per_cell, total[1] * per_cell)

        def low_body(i, carry):
            cells = cells_of(lay, i)
            mask = center_mask(lay, i * step, step)
            normed = first_normed(i)
            value = (pre_slope(s.mid[cells, 0:REDUCE], normed, first, total) * mask).astype(BF16)
            s.low[cells, :] = value
            slope = dot(value, k.v_w_reduce[index])
            slope = slope + dot(s.projected_slope[cells, :], k.v_w_pool[index], NT)
            lay.put_slope(i, slope * mask)
            return carry

        loop(chunks, low_body, 0)
        progress(index, 7)
        store_blocks(index, LOW_AT, dot(s.low[...].T, flat_block(lay)).astype(BF16))
        progress(index, 8)

    def widen(ref, begin, value):
        width = value.shape[-1]
        for lane in range(0, width, 128):
            size = min(128, width - lane)
            for odd in range(2):
                ref[(begin + lane) // 128, pl.ds(odd, two.frames, stride=2), 0:size] = value[
                    :, lane : lane + size
                ]

    def wide(value, a, width):
        tiles = [value[..., lane // 128, :, :] for lane in range(a, a + width, 128)]
        return jnp.concatenate(tiles, axis=-1)[..., :width]

    def put_two(i, slope):
        slope = slope * 0.125
        for a, part in zip((0,) + tuple(B0 + a for a in SECOND_AT), split(slope)):
            width = part.shape[-1]
            part = part.reshape(two.rows, two.cols, two.frames, width)
            for row in range(two.rows):
                for col in range(two.cols):
                    widen(k.spread.at[row, col], a, part[row, col])
            if a >= B0:
                inner = (slice(1, two.rows + 1), slice(1, two.cols + 1), slice(None))
                k.grad_border[(1,) + inner + (slice(a - B0, a - B0 + width),)] = part.astype(BF16)

    two.put_slope = put_two

    def side(lay, across, last):
        if across:
            return (jnp.where(h == 0, lay.rows + 1, 0), slice(None))
        return (slice(1, lay.rows + 1), lay.cols + 1 if last else 0)

    def border_two(across, last):
        value = k.grad_border[(0,) + side(two, across, last)].astype(F32)
        value = value.reshape(value.shape[0] * two.frames, SECOND_WIDTH)
        return [value[:, a : a + n] for a, n in zip(SECOND_AT, SECOND)]

    def end_two():
        put_normed(two, second_two)
        start_halo(two, two.s.normed, 3)
        value = jnp.concatenate(outputs(two, 0, first_two, second_two), axis=1).astype(BF16)
        k.block_output[...] = value.reshape(k.block_output.shape)
        end_halo(two, two.s.normed, 3)
        end_halo(two, k.grad_border.at[0], 4)

    backward(two, slope_two, border_two, 4, first_two, second_two, count_two, end_two)
    start_halo(two, k.grad_border.at[1], 5)

    def slope_one(i):
        value = k.spread[i]
        out = []
        for a, width in zip((0,) + tuple(B0 + a for a in SECOND_AT), (B0,) + SECOND):
            part = wide(value, a, width)
            pieces = [part[col // 2] for col in range(one.cols)]
            out.append(jnp.concatenate(pieces * one.step, axis=0))
        return out

    def border_one(across, last):
        where = side(two, across, last)
        value = k.border_spread[where] if across else k.border_spread[:, where[1]]
        cells = range(one.cols + 2) if across else range(1, one.rows + 1)
        out = []
        for a, n in zip(SECOND_AT, SECOND):
            part = wide(value, a, n)
            out.append(jnp.concatenate([part[(cell + 1) // 2] for cell in cells], axis=0))
        return out

    def end_one():
        end_halo(one, one.s.normed, 1)
        end_halo(two, k.grad_border.at[1], 5)
        places = [(side(two, True, None)[0], col) for col in range(two.cols + 2)]
        places += [(row, col) for row in range(1, two.rows + 1) for col in (0, two.cols + 1)]
        for row, col in places:
            widen(k.border_spread.at[row, col], 0, k.grad_border[1, row, col].astype(F32))

    def put_one(i, slope):
        shape = (one.step, one.cols, one.frames, slope.shape[-1])
        k.input_grad[pl.ds(i * one.step, one.step)] = slope.astype(BF16).reshape(shape)

    one.put_slope = put_one
    backward(one, slope_one, border_one, 6, first_one, second_one, count_one, end_one)
    for step in plan[None]:
        step()


def unpack_body(taps, low, mid_out, small_out, reduce_out, pool_out, unit):
    def lanes(blocks, tiles, rows, width):
        parts = []
        for tile in range(tiles):
            size = min(128, width - 128 * tile)
            part = blocks[tile * (rows // 16) : (tile + 1) * (rows // 16), :, 0:size]
            parts.append(part.reshape(rows, size))
        return parts

    @pl.when((pl.program_id(0) == 0) & (pl.program_id(1) == 0))
    def _():
        shape = unit.shape
        same = lax.broadcasted_iota(jnp.int32, shape, 0) == lax.broadcasted_iota(jnp.int32, shape, 1)
        unit[...] = same.astype(F32).astype(BF16)

    mid = jnp.concatenate(lanes(taps.at[0], 4, B1, 3 * B1R), axis=1)
    mid = dot(unit[...], mid, NT)
    small = lanes(taps.at[0, 80:88], 1, B2, 3 * B2R)[0]
    small = dot(unit[0 : 3 * B2R, 0 : 3 * B2R], small, NT)
    for t in range(3):
        mid_out[0, t, 0] = mid[B1R * t : B1R * (t + 1)]
        small_out[0, t, 0] = small[B2R * t : B2R * (t + 1)]

    @pl.when(pl.program_id(1) == 0)
    def _():
        channels = reduce_out.shape[-1]
        tiles = -(-channels // 128)
        for at, part in enumerate(lanes(low.at[0, 0:196], tiles, REDUCE, channels)):
            reduce_out[0, :, 128 * at : 128 * at + part.shape[1]] = part.astype(F32)
        for at, part in enumerate(lanes(low.at[0, 196:252], tiles, BP, channels)):
            size = part.shape[1]
            pool_out[0, 128 * at : 128 * at + size, :] = dot(unit[0:size, 0:size], part, NT)


def unpack(grads, channels):
    grid = (2, 9)
    shapes = ((2, 3, 9, B1R, B1), (2, 3, 9, B2R, B2), (2, REDUCE, channels), (2, channels, BP))
    mid_grad, small_grad, reduce_grad, pool_grad = pl.pallas_call(
        unpack_body,
        grid=grid,
        out_shape=[jax.ShapeDtypeStruct(shape, F32) for shape in shapes],
        in_specs=[
            pl.BlockSpec((1, TAP_BLOCKS, 16, 128), lambda i, j: (i, j, 0, 0)),
            pl.BlockSpec((1, 256, 16, 128), lambda i, j: (i, LOW_OUT // 256, 0, 0)),
        ],
        out_specs=[
            pl.BlockSpec((1, 3, 1, B1R, B1), lambda i, j: (i, 0, j, 0, 0)),
            pl.BlockSpec((1, 3, 1, B2R, B2), lambda i, j: (i, 0, j, 0, 0)),
            pl.BlockSpec((1, REDUCE, channels), lambda i, j: (i, 0, 0)),
            pl.BlockSpec((1, channels, BP), lambda i, j: (i, 0, 0)),
        ],
        scratch_shapes=[pltpu.VMEM((3 * B1R, 3 * B1R), BF16)],
        compiler_params=pltpu.CompilerParams(vmem_limit_bytes=40 * 1024 * 1024),
        name="unpack",
    )(grads, grads)
    return (
        jnp.swapaxes(reduce_grad, 1, 2),
        mid_grad.reshape(2, 27, B1R, B1),
        small_grad.reshape(2, 27, B2R, B2),
        pool_grad,
    )


def on_device(
    n_batch, n_wa, clip_features, frame_counts, w_reduce, w_mid, w_small, w_pool, norm_gain, norm_bias, out_grad
):
    frames, rows, cols, channels = clip_features.shape
    clips = frame_counts.shape[0]
    slot = frames // clips
    layers = (
        Layer(0, rows, cols, clips, slot),
        Layer(1, rows // 2, cols // 2, clips, slot // 2),
    )
    one, two = layers
    chips = n_batch * n_wa

    def cells_first(array):
        return array.transpose(1, 2, 0, 3)

    operands = dict(
        features=cells_first(clip_features),
        frame_counts=frame_counts,
        w_reduce=jnp.swapaxes(w_reduce, 1, 2),
        w_mid=w_mid.reshape(2, 3, 9, B1R, B1),
        w_small=w_small.reshape(2, 3, 9, B2R, B2),
        w_pool=w_pool,
        gain=norm_gain.reshape(2, 1, -1),
        bias=norm_bias.reshape(2, 1, -1),
        out_grad=cells_first(out_grad),
    )
    in_space = dict(frame_counts=pltpu.SMEM, gain=pltpu.VMEM, bias=pltpu.VMEM)
    out_space = dict(weight_grads=pl.ANY)
    results = dict(
        block_output=jax.ShapeDtypeStruct((two.rows, two.cols, two.frames, channels), BF16),
        input_grad=jax.ShapeDtypeStruct((rows, cols, frames, channels), BF16),
        weight_grads=jax.ShapeDtypeStruct((2, LOW_OUT + 256, 16, 128), BF16),
        gain_grad=jax.ShapeDtypeStruct(norm_gain[:, None].shape, F32),
        bias_grad=jax.ShapeDtypeStruct(norm_bias[:, None].shape, F32),
    )
    scratch = {}
    for name in ("w_reduce", "w_pool", "out_grad"):
        scratch["v_" + name] = pltpu.VMEM(operands[name].shape, BF16)
    scratch.update(
        v_w_mid=pltpu.VMEM((2, 9, 3 * B1R, B1), BF16),
        v_w_small=pltpu.VMEM((2, 9, 3 * B2R, B2), BF16),
    )
    small_pad = (two.rows + 2, two.cols + 2)
    scratch.update(
        pairs=pltpu.VMEM((two.cols, (B0 + SECOND_WIDTH) // 128, one.frames, 128), F32),
        spread=pltpu.VMEM(
            (two.rows, two.cols, (B0 + SECOND_WIDTH) // 128, one.frames, 128), F32
        ),
        border_spread=pltpu.VMEM(small_pad + (SECOND_WIDTH // 128, one.frames, 128), F32),
        grad_border=pltpu.VMEM((2,) + small_pad + (two.frames, SECOND_WIDTH), BF16),
        sums=pltpu.VMEM((8, 1, SUM_WIDTH), F32),
        pair_sums=pltpu.VMEM((8, 1, SUM_WIDTH), F32),
        chip_sums=pltpu.VMEM((2, chips, 1, SUM_WIDTH), F32),
        load_sem=pltpu.SemaphoreType.DMA((17,)),
        feature_sem=pltpu.SemaphoreType.DMA((one.rows // one.step,)),
        pair_sem=pltpu.SemaphoreType.DMA((2, 8)),
        chip_sem=pltpu.SemaphoreType.DMA((2, 8)),
        halo_sem=pltpu.SemaphoreType.DMA((2, 6, 5)),
        grads=pltpu.VMEM((2, GRAD_BLOCKS, 16, 128), BF16),
        got_half=pltpu.VMEM((2, GRAD_BLOCKS // 2, 16, 128), BF16),
        got_eighth=pltpu.VMEM((2, GRAD_BLOCKS // 4, 16, 128), BF16),
        got_piece=pltpu.VMEM((2, GRAD_BLOCKS // 8, 16, 128), BF16),
        got_chunk=pltpu.VMEM((2, n_batch, GRAD_BLOCKS // 32, 16, 128), BF16),
        got_total=pltpu.VMEM((2, OWNERS, GRAD_BLOCKS // 32, 16, 128), BF16),
        free_sem=pltpu.SemaphoreType.REGULAR((2, 3, 3)),
        grad_sem=pltpu.SemaphoreType.DMA((2, 2, 3, 18)),
        out_sem=pltpu.SemaphoreType.DMA((2, 3)),
    )
    names = list(operands) + list(results) + list(scratch)
    layer_scratch = [lay.scratch(channels) for lay in layers]

    def body(*refs):
        rest = refs[len(names) :]
        for lay, parts in zip(layers, layer_scratch):
            lay.s = SimpleNamespace(**dict(zip(parts, rest[: len(parts)])))
            rest = rest[len(parts) :]
        kernel_body(names, (n_batch, n_wa, layers), refs[: len(names)])

    out = pl.pallas_call(
        body,
        out_shape=list(results.values()),
        in_specs=[pl.BlockSpec(memory_space=in_space.get(name, pl.ANY)) for name in operands],
        out_specs=[pl.BlockSpec(memory_space=out_space.get(name, pltpu.VMEM)) for name in results],
        scratch_shapes=list(scratch.values()) + [r for parts in layer_scratch for r in parts.values()],
        compiler_params=pltpu.CompilerParams(
            collective_id=0, has_side_effects=True, vmem_limit_bytes=63 * 1024 * 1024
        ),
        name="layers",
    )(*operands.values())
    out = dict(zip(results, out))

    reduce_grad, mid_grad, small_grad, pool_grad = unpack(out["weight_grads"], channels)

    return (
        out["block_output"].transpose(2, 0, 1, 3),
        out["input_grad"].transpose(2, 0, 1, 3),
        reduce_grad,
        mid_grad,
        small_grad,
        pool_grad,
        out["gain_grad"].reshape(norm_gain.shape),
        out["bias_grad"].reshape(norm_bias.shape),
    )


def solution(mesh):
    in_specs = (
        P("batch", "ha", "wa", None),
        P("batch"),
        P(),
        P(),
        P(),
        P(),
        P(),
        P(),
        P("batch", "ha", "wa", None),
    )
    out_specs = (
        P("batch", "ha", "wa", None),
        P("batch", "ha", "wa", None),
        P(),
        P(),
        P(),
        P(),
        P(),
        P(),
    )
    return jax.shard_map(
        functools.partial(on_device, mesh.shape["batch"], mesh.shape["wa"]),
        mesh=mesh,
        in_specs=in_specs,
        out_specs=out_specs,
        check_vma=False,
    )
```

```python
import functools
from types import SimpleNamespace

import jax
import jax.numpy as jnp
from jax import lax
from jax.experimental import pallas as pl
from jax.experimental.pallas import tpu as pltpu
from jax.sharding import PartitionSpec as P

HEIGHT = 14
EPSILON = 1e-05
MESH = pl.DeviceIdType.MESH
F32 = jnp.float32
BF16 = jnp.bfloat16

B0, B1R, B2R, B1, B2, BP = 256, 160, 32, 320, 128, 128
NARROW = B1R + B2R
REDUCE = B0 + NARROW
SECOND = (B1, B2, BP)
SECOND_AT = (0, 384, 512)
SECOND_WIDTH = 640
SUM_WIDTH = 1280
AXES = ("batch", "ha", "wa")

TAP_BLOCKS = 88
LOW_AT = 800
LOW_OUT = 1024
GRAD_BLOCKS = 1056
BUNDLES = ((0, 352), (352, 448), (800, 256))
OWNERS = 4

SCHEDULE = {
    (1, (5, 3)): ((1, 0),),
    (1, (5, 8)): ((1, 1),),
    (1, 6): ((1, 0),),
    (1, 8): ((1, 2),),
    (0, 0): ((1, 1), (1, 2), (1, 0),),
    (0, 1): ((1, 1),),
    (0, (5, 2)): ((1, 2),),
    (0, (5, 3)): ((0, 0),),
    (0, (5, 4)): ((1, 0),),
    (0, (5, 6)): ((0, 0), (1, 1),),
    (0, (5, 8)): ((0, 1), (1, 2),),
    (0, (2, 3)): ((0, 1), (1, 0),),
    (0, (2, 4)): ((0, 0),),
    (0, (2, 8)): ((1, 1),),
    (0, 4): ((1, 2), (0, 1),),
    (0, 6): ((0, 0), (1, 0),),
    (0, 7): ((0, 1),),
    (0, 8): ((0, 2),),
}
EARLY_TAPS = (9, 0)
LAST_STEPS = (
    (1, 0),
    (1, 1),
    (0, 2),
    (1, 2),
    (0, 0),
    (1, 0),
    (1, 1),
    (1, 0),
    (0, 1),
    (0, 2),
    (1, 0),
    (1, 2),
    (0, 0),
    (1, 1),
    (0, 2),
    (0, 1),
    (1, 1),
    (1, 2),
    (1, 1),
    (0, 0),
    (1, 2),
    (0, 2),
    (0, 1),
    (1, 2),
    (0, 0),
    (0, 2),
    (0, 0),
    (0, 1),
    (0, 0),
    (0, 2),
    (0, 1),
    (0, 1),
    (0, 2),
    (0, 2),
    (0, 2),
)

NORMED_AT = ((0,), (1,), (2,), (3,), ())

NN = (((1,), (0,)), ((), ()))
NT = (((1,), (1,)), ((), ()))


def dot(a, b, dims=NN):
    return lax.dot_general(a, b, dims, preferred_element_type=F32)


def softplus(x):
    return jnp.maximum(x, 0.0) + jnp.log1p(jnp.exp(-jnp.abs(x)))


def sigmoid(x):
    return 1.0 / (1.0 + jnp.exp(-x))


def loop(count, body, init):
    return body(0, init) if count == 1 else lax.fori_loop(0, count, body, init)


class Layer:
    def __init__(self, index, rows, cols, clips, slot):
        self.index, self.rows, self.cols = index, rows, cols
        self.clips, self.slot = clips, slot
        self.frames = clips * slot
        self.cells = rows * cols * self.frames
        self.row_cells = cols * self.frames
        self.step = rows if index else 2
        self.pad_step = rows + 2 if index else 2

    def scratch(self, channels):
        r, c, t, n = self.rows, self.cols, self.frames, self.cells
        pad = (r + 2, c + 2, t)
        return dict(
            mask=pltpu.VMEM(pad + (1,), F32),
            block_in=pltpu.VMEM((r, c, t, channels), BF16),
            first=pltpu.VMEM((r, c, t, B0), F32),
            narrow=pltpu.VMEM(pad + (NARROW,), F32),
            border=pltpu.VMEM(pad + (BP + NARROW,), BF16),
            mid_in=pltpu.VMEM(pad + (3 * B1R,), BF16),
            small_in=pltpu.VMEM(pad + (3 * B2R,), BF16),
            box=pltpu.VMEM((r + 2, c, t, BP), F32),
            mid=pltpu.VMEM((n, 3 * B1R), F32),
            small=pltpu.VMEM((n, B2), F32),
            pool=pltpu.VMEM((n, BP), F32),
            normed=pltpu.VMEM(pad + (SECOND_WIDTH,), BF16),
            projected_slope=pltpu.VMEM((n, BP), BF16),
            low=pltpu.VMEM((n, REDUCE), BF16),
        )


def batch_norm_scale(total, square, count, gain):
    average = total / count
    variance = square / count - average * average
    inv_std = lax.rsqrt(variance + EPSILON)
    return average, inv_std, inv_std * gain


def kernel_body(names, sizes, refs):
    k = SimpleNamespace(**dict(zip(names, refs)))
    n_batch, n_wa, layers = sizes
    b, h, w = (lax.axis_index(a) for a in AXES)
    chips = n_batch * n_wa
    my_chip = b * n_wa + w
    one, two = layers

    def chip_at(p):
        return lax.div(p, n_wa), h, lax.rem(p, n_wa)

    def rotated(i):
        return lax.rem(my_chip + i, chips)

    def load(at, source, target):
        return pltpu.make_async_copy(source, target, k.load_sem.at[at])

    def load_features(i):
        rows = pl.ds(i * one.step, one.step)
        return pltpu.make_async_copy(
            k.features.at[:, rows], k.input_grad.at[:, rows], k.feature_sem.at[i]
        )

    def load_cubes(at, layer):
        copies = []
        for t in range(3):
            mid, small = pl.ds(B1R * t, B1R), pl.ds(B2R * t, B2R)
            copies.append(load(at + 2 * t, k.w_mid.at[layer, t], k.v_w_mid.at[layer, :, mid]))
            copies.append(load(at + 2 * t + 1, k.w_small.at[layer, t], k.v_w_small.at[layer, :, small]))
        return copies

    def load_flat(at, layer):
        return [
            load(at, k.w_reduce.at[layer], k.v_w_reduce.at[layer]),
            load(at + 1, k.w_pool.at[layer], k.v_w_pool.at[layer]),
        ]

    flat_one, flat_two = load_flat(0, 0), load_flat(2, 1)
    cubes_one, cubes_two = load_cubes(4, 0), load_cubes(10, 1)
    slope_load = load(16, k.out_grad, k.v_out_grad)
    for copy in flat_one:
        copy.start()
    for i in range(one.rows // one.step):
        load_features(i).start()
    for lay in layers:
        s = lay.s
        for ref in (s.border, s.normed):
            for row in (0, lay.rows + 1):
                ref[row] = jnp.zeros(ref.shape[1:], ref.dtype)
            for col in (0, lay.cols + 1):
                ref[:, col] = jnp.zeros((ref.shape[0],) + ref.shape[2:], ref.dtype)
    ref = k.grad_border
    ref[...] = jnp.zeros(ref.shape, ref.dtype)
    for layer in range(2):
        for begin, end in ((9 * TAP_BLOCKS, LOW_AT), (LOW_AT + 252, GRAD_BLOCKS)):
            k.grads[layer, begin:end] = jnp.zeros((end - begin, 16, 128), BF16)
    k.sums[...] = jnp.zeros(k.sums.shape, F32)

    barrier = pltpu.get_barrier_semaphore()
    pl.semaphore_signal(barrier, inc=1, device_id=(b, 1 - h, w), device_id_type=MESH)

    @pl.when(w > 0)
    def _():
        pl.semaphore_signal(barrier, inc=1, device_id=(b, 1 - h, w - 1), device_id_type=MESH)

    @pl.when(w < n_wa - 1)
    def _():
        pl.semaphore_signal(barrier, inc=1, device_id=(b, 1 - h, w + 1), device_id_type=MESH)

    def greet(i, carry):
        pl.semaphore_signal(barrier, inc=1, device_id=chip_at(rotated(i)), device_id_type=MESH)
        return carry

    lax.fori_loop(1, chips, greet, 0)

    for lay in layers:
        frame_at = lax.broadcasted_iota(jnp.int32, (lay.frames, 1), 0)
        inside = jnp.zeros((lay.frames, 1), F32)
        for clip in range(lay.clips):
            valid = k.frame_counts[clip]
            valid = valid if lay.index == 0 else lax.div(valid, 2)
            begin = clip * lay.slot
            inside = jnp.where((frame_at >= begin) & (frame_at < begin + valid), 1.0, inside)
        height = HEIGHT if lay.index == 0 else HEIGHT // 2
        for row in range(lay.rows + 2):
            at_row = h * lay.rows + row - 1
            for col in range(lay.cols + 2):
                at_col = w * lay.cols + col - 1
                good = (at_row >= 0) & (at_row < height) & (at_col >= 0) & (at_col < height)
                lay.s.mask[row, col] = inside * good.astype(F32)

    def start_sum(at):
        pair = pltpu.make_async_remote_copy(
            src_ref=k.sums.at[at],
            dst_ref=k.pair_sums.at[at],
            send_sem=k.pair_sem.at[0, at],
            recv_sem=k.pair_sem.at[1, at],
            device_id=(b, 1 - h, w),
            device_id_type=MESH,
        )
        pair.start()
        pair.wait()
        k.chip_sums[at % 2, my_chip] = k.sums[at] + k.pair_sums[at]

        def send(i, carry):
            pltpu.make_async_remote_copy(
                src_ref=k.chip_sums.at[at % 2, my_chip],
                dst_ref=k.chip_sums.at[at % 2, my_chip],
                send_sem=k.chip_sem.at[0, at],
                recv_sem=k.chip_sem.at[1, at],
                device_id=chip_at(rotated(i)),
                device_id_type=MESH,
            ).start()
            return carry

        if chips <= 16:
            for i in range(1, chips):
                send(i, 0)
        else:
            lax.fori_loop(1, chips, send, 0)

    def end_sum(at):
        for way in (1, 0):
            others = k.chip_sums.at[at % 2, pl.ds(0, chips - 1)]
            pltpu.make_async_copy(others, others, k.chip_sem.at[way, at]).wait()
        total = k.chip_sums[at % 2, 0]
        for p in range(1, chips):
            total = total + k.chip_sums[at % 2, p]
        return total

    def halo_copies(lay, ref, at):
        src_row = jnp.where(h == 0, lay.rows, 1)
        dst_row = jnp.where(h == 0, 0, lay.rows + 1)
        rows, cols = lay.rows, lay.cols

        def remote(src, dst, way, device):
            return lambda: pltpu.make_async_remote_copy(
                src_ref=ref.at[src],
                dst_ref=ref.at[dst],
                send_sem=k.halo_sem.at[0, at, way],
                recv_sem=k.halo_sem.at[1, at, way],
                device_id=device,
                device_id_type=MESH,
            )

        all_rows, all_cols = pl.ds(1, rows), pl.ds(1, cols)
        row = remote((src_row, all_cols), (dst_row, all_cols), 0, (b, 1 - h, w))
        to_left = [
            remote((all_rows, 1), (all_rows, cols + 1), 1, (b, h, w - 1)),
            remote((src_row, 1), (dst_row, cols + 1), 2, (b, 1 - h, w - 1)),
        ]
        to_right = [
            remote((all_rows, cols), (all_rows, 0), 3, (b, h, w + 1)),
            remote((src_row, cols), (dst_row, 0), 4, (b, 1 - h, w + 1)),
        ]
        return row, to_left, to_right

    def normed_copies():
        ref, rows, cols = one.s.normed, one.rows, one.cols
        half = rows // 2
        src_row = jnp.where(h == 0, rows, 1)
        dst_row = jnp.where(h == 0, 0, rows + 1)

        def remote(part, slot, src, dst, device):
            return lambda: pltpu.make_async_remote_copy(
                src_ref=ref.at[src],
                dst_ref=ref.at[dst],
                send_sem=k.normed_sem.at[0, part, slot],
                recv_sem=k.normed_sem.at[1, part, slot],
                device_id=device,
                device_id_type=MESH,
            )

        parts = []
        for part in range(4):
            left, low = part < 2, part % 2 == 0
            src, dst = (1, cols + 1) if left else (cols, 0)
            way = w - 1 if left else w + 1
            run = pl.ds(1 if low else 1 + half, half)
            copies = [remote(part, 0, (run, src), (run, dst), (b, h, way))]
            if low:
                copies.append(remote(part, 1, (src_row, src), (dst_row, dst), (b, 1 - h, way)))
            parts.append((w > 0 if left else w < n_wa - 1, w < n_wa - 1 if left else w > 0, copies))
        inner = pl.ds(1, cols)
        row = remote(0, 2, (src_row, inner), (dst_row, inner), (b, 1 - h, w))
        return row, parts

    def start_normed(*which):
        row, parts = normed_copies()
        if 0 in which:
            row().start()
        for part in which:
            sends, _, copies = parts[part]

            @pl.when(sends)
            def _(copies=copies):
                for copy in copies:
                    copy().start()

    def end_normed():
        row, parts = normed_copies()
        row().wait()
        for sends, receives, copies in parts:

            @pl.when(sends)
            def _(copies=copies):
                for copy in copies:
                    copy().wait_send()

            @pl.when(receives)
            def _(copies=copies):
                for copy in copies:
                    copy().wait_recv()

    def start_halo(lay, ref, at, first=True, last=True):
        row, to_left, to_right = halo_copies(lay, ref, at)
        if first:
            row().start()

            @pl.when(w > 0)
            def _():
                for copy in to_left:
                    copy().start()

        if last:

            @pl.when(w < n_wa - 1)
            def _():
                for copy in to_right:
                    copy().start()

    def end_halo(lay, ref, at, rows=True, cols=True):
        row, to_left, to_right = halo_copies(lay, ref, at)
        if rows:
            row().wait()
        if not cols:
            return

        @pl.when(w > 0)
        def _():
            for copy in to_left:
                copy().wait_send()
            for copy in to_right:
                copy().wait_recv()

        @pl.when(w < n_wa - 1)
        def _():
            for copy in to_right:
                copy().wait_send()
            for copy in to_left:
                copy().wait_recv()

    def exchange(layer, number):
        begin, count = BUNDLES[number]
        half, quarter, eighth = count // 2, count // 4, count // 8
        piece, chunk = count // 16, count // 32
        stride = n_batch // OWNERS
        g = k.grads.at[layer]
        r1, r2, r3, r4, r5 = (
            r.at[layer] for r in (k.got_half, k.got_eighth, k.got_piece, k.got_chunk, k.got_total)
        )
        to_half, to_eighth, to_piece, to_chunk = begin // 2, begin // 4, begin // 8, begin // 32

        def places():
            b, h, w = (lax.axis_index(a) for a in AXES)
            x, y = lax.rem(w, 2), lax.div(w, 2)
            at = SimpleNamespace(b=b, h=h, w=w)
            at.pair, at.beside, at.below = (b, 1 - h, w), (b, h, w + 1 - 2 * x), (b, h, w + 2 - 4 * y)
            at.mine, at.other = begin + h * half, begin + (1 - h) * half
            half_a, half_b = at.mine, at.mine + quarter
            at.eighth_a, at.eighth_b = half_a + x * eighth, half_b + y * eighth
            at.a, at.b_ = at.eighth_a + y * piece, at.eighth_b + x * piece
            at.sent_a, at.sent_b = half_a + (1 - x) * eighth, half_b + (1 - y) * eighth
            at.last_a, at.last_b = at.eighth_a + (1 - y) * piece, at.eighth_b + (1 - x) * piece
            at.rank = lax.div(b, stride)
            at.chunk = jnp.where(at.rank < 2, at.a, at.b_) + lax.rem(at.rank, 2) * chunk
            at.chunks = [(at.a, at.b_)[owner // 2] + owner % 2 * chunk for owner in range(OWNERS)]
            return at

        def copy(source, at, target, to, size, slot, device):
            return pltpu.make_async_remote_copy(
                src_ref=source.at[pl.ds(at, size)],
                dst_ref=target.at[pl.ds(to, size)],
                send_sem=k.grad_sem.at[0, layer, number, slot],
                recv_sem=k.grad_sem.at[1, layer, number, slot],
                device_id=device,
                device_id_type=MESH,
            )

        def pair_copies(at):
            return [copy(g, at.other, r1, to_half, half, 0, at.pair)]

        def eighth_copies(at):
            return [
                copy(g, at.sent_a, r2, to_eighth, eighth, 1, at.beside),
                copy(g, at.sent_b, r2, to_eighth + eighth, eighth, 2, at.below),
            ]

        def piece_copies(at):
            return [
                copy(g, at.last_a, r3, to_piece, piece, 3, at.below),
                copy(g, at.last_b, r3, to_piece + piece, piece, 4, at.beside),
            ]

        def piece_returns(at):
            return [
                copy(g, at.a, g, at.a, piece, 13, at.below),
                copy(g, at.b_, g, at.b_, piece, 14, at.beside),
            ]

        def eighth_returns(at):
            return [
                copy(g, at.eighth_a, g, at.eighth_a, eighth, 15, at.beside),
                copy(g, at.eighth_b, g, at.eighth_b, eighth, 16, at.below),
            ]

        def pair_returns(at):
            return [copy(g, at.mine, g, at.mine, half, 17, at.pair)]

        def go(copies):
            for c in copies:
                c.start()

        def end(copies):
            for c in copies:
                c.wait()

        def add(at, other, to, size):
            step = 16 if size % 16 == 0 else size

            def body(i, carry):
                mine = pl.ds(at + i * step, step)
                g[mine] = g[mine] + other[pl.ds(to + i * step, step)]
                return carry

            lax.fori_loop(0, size // step, body, 0)

        def free(slot, device):
            sem = k.free_sem.at[layer, number, slot]
            pl.semaphore_signal(sem, inc=1, device_id=device, device_id_type=MESH)

        def wait_free(slot):
            pl.semaphore_wait(k.free_sem.at[layer, number, slot], 1)

        def for_owner(at, do):
            if stride == 1:
                do()
            else:
                pl.when(lax.rem(at.b, stride) == 0)(do)

        def for_others(at, do):
            for owner in range(OWNERS):
                pl.when(at.b != owner * stride)(functools.partial(do, owner))

        def share_copies(at):
            return [
                pltpu.make_async_remote_copy(
                    src_ref=g.at[pl.ds(at.chunk, chunk)],
                    dst_ref=r5.at[at.rank, pl.ds(to_chunk, chunk)],
                    send_sem=k.grad_sem.at[0, layer, number, 9],
                    recv_sem=k.grad_sem.at[1, layer, number, 9 + at.rank],
                    device_id=(lax.rem(at.b + i, n_batch), at.h, at.w),
                    device_id_type=MESH,
                )
                for i in range(1, n_batch)
            ]

        def start_pair():
            go(pair_copies(places()))

        def start_eighths():
            at = places()
            end(pair_copies(at))
            free(0, at.pair)
            add(at.mine, r1, to_half, half)
            go(eighth_copies(at))

        def start_pieces():
            at = places()
            end(eighth_copies(at))
            add(at.eighth_a, r2, to_eighth, eighth)
            add(at.eighth_b, r2, to_eighth + eighth, eighth)
            go(piece_copies(at))

        def start_chunks():
            at = places()
            end(piece_copies(at))
            free(1, at.below)
            free(2, at.beside)
            add(at.a, r3, to_piece, piece)
            add(at.b_, r3, to_piece + piece, piece)

            def send_chunk(owner):
                pltpu.make_async_remote_copy(
                    src_ref=g.at[pl.ds(at.chunks[owner], chunk)],
                    dst_ref=r4.at[at.b, pl.ds(to_chunk, chunk)],
                    send_sem=k.grad_sem.at[0, layer, number, 5 + owner],
                    recv_sem=k.grad_sem.at[1, layer, number, 5],
                    device_id=(owner * stride, at.h, at.w),
                    device_id_type=MESH,
                ).start()

            for_others(at, send_chunk)

        def share_chunk():
            at = places()

            def collect():
                others = r4.at[pl.ds(0, n_batch - 1), pl.ds(to_chunk, chunk)]
                pltpu.make_async_copy(others, others, k.grad_sem.at[1, layer, number, 5]).wait()
                r4[at.b, pl.ds(to_chunk, chunk)] = g[pl.ds(at.chunk, chunk)]
                total = r4[0, pl.ds(to_chunk, chunk)].astype(F32)
                for slot in range(1, n_batch):
                    total = total + r4[slot, pl.ds(to_chunk, chunk)].astype(F32)
                g[pl.ds(at.chunk, chunk)] = total.astype(BF16)
                go(share_copies(at))

            for_owner(at, collect)

            def sent_chunk(owner):
                part = g.at[pl.ds(at.chunks[owner], chunk)]
                pltpu.make_async_copy(part, part, k.grad_sem.at[0, layer, number, 5 + owner]).wait()

            for_others(at, sent_chunk)

        def return_pieces():
            at = places()

            def shared():
                for c in share_copies(at):
                    c.wait_send()

            for_owner(at, shared)

            def take_chunk(owner):
                part = r5.at[owner, pl.ds(to_chunk, chunk)]
                pltpu.make_async_copy(part, part, k.grad_sem.at[1, layer, number, 9 + owner]).wait()
                g[pl.ds(at.chunks[owner], chunk)] = r5[owner, pl.ds(to_chunk, chunk)]

            for_others(at, take_chunk)
            wait_free(1)
            wait_free(2)
            go(piece_returns(at))

        def return_eighths():
            at = places()
            end(piece_returns(at))
            go(eighth_returns(at))

        def return_halves():
            at = places()
            end(eighth_returns(at))
            wait_free(0)
            go(pair_returns(at))

        def result():
            target = k.weight_grads.at[layer, pl.ds(LOW_OUT if begin == LOW_AT else begin, count)]
            sem = k.out_sem.at[layer, number]
            return pltpu.make_async_copy(g.at[pl.ds(begin, count)], target, sem)

        def start_result():
            end(pair_returns(places()))

            result().start()

        def end_result():
            result().wait()

        return (
            start_pair,
            start_eighths,
            start_pieces,
            start_chunks,
            share_chunk,
            return_pieces,
            return_eighths,
            return_halves,
            start_result,
            end_result,
        )

    exchanges = {(layer, number): exchange(layer, number) for layer in range(2) for number in range(3)}
    plan, taken = {}, dict.fromkeys(exchanges, 0)
    for point, keys in list(SCHEDULE.items()) + [(None, LAST_STEPS)]:
        for key in keys:
            plan.setdefault(point, []).append(exchanges[key][taken[key]])
            taken[key] += 1
    assert all(taken[key] == len(exchanges[key]) for key in exchanges)

    def progress(*point):
        for step in plan.get(point, ()):
            step()

    def flat_block(lay):
        block = lay.s.block_in[...]
        return block.reshape(lay.cells, block.shape[-1])

    def store_blocks(layer, at, value):
        rows, lanes = value.shape
        for lane in range(0, lanes, 128):
            size = min(128, lanes - lane)
            blocks = pl.ds(at + lane // 128 * (rows // 16), rows // 16)
            tile = value[:, lane : lane + size].reshape(rows // 16, 16, size)
            k.grads[layer, blocks, :, 0:size] = tile

    def column_sum(value):
        return jnp.sum(value, axis=0, keepdims=True)

    def center_mask(lay, row, count=1):
        mask = lay.s.mask[pl.ds(row + 1, count), 1 : lay.cols + 1]
        return mask.reshape(count * lay.row_cells, 1)

    def shifted(lay, value):
        count = value.shape[0]
        frame_at = lax.rem(lax.broadcasted_iota(jnp.int32, (count, 1), 0), lay.slot)
        before = jnp.where(frame_at == 0, 0.0, pltpu.roll(value, 1, 0))
        after = jnp.where(frame_at == lay.slot - 1, 0.0, pltpu.roll(value, count - 1, 0))
        return before, after

    def reorder(lay, value, cells_first):
        size, cols, frames = lay.row_cells, lay.cols, lay.frames
        to = lax.broadcasted_iota(jnp.int32, (size, size), 0)
        source = lax.broadcasted_iota(jnp.int32, (size, size), 1)
        if cells_first:
            wanted = lax.rem(to, frames) * cols + lax.div(to, frames)
        else:
            wanted = lax.rem(to, cols) * frames + lax.div(to, cols)
        swap = (source == wanted).astype(F32).astype(BF16)
        return dot(swap, value.reshape(size, value.shape[-1]))

    def cells_of(lay, i):
        size = lay.step * lay.row_cells
        return pl.ds(i * size if isinstance(i, int) else pl.multiple_of(i * size, size), size)

    def reduce_conv(lay):
        s, at, step = lay.s, lay.index, lay.step
        count = step * lay.row_cells

        def body(i, sums):
            mask = center_mask(lay, i * step, step)
            if lay.index == 0:
                load_features(i).wait()
            if lay.index == 0:
                block = [reorder(lay, k.input_grad[:, i * step + row], True) for row in range(step)]
                block = (jnp.concatenate(block, axis=0) * mask).astype(BF16)
                shape = (step, lay.cols, lay.frames, block.shape[-1])
                s.block_in[pl.ds(i * step, step)] = block.reshape(shape)
            else:
                block = s.block_in[pl.ds(i * step, step)]
                block = block.reshape(count, block.shape[-1])
            reduced = dot(block, k.v_w_reduce[at], NT)
            projected = dot(block, k.v_w_pool[at])
            rows = pl.ds(i * step, step)
            inner = pl.ds(i * step + 1, step)
            shape = (step, lay.cols, lay.frames)
            s.first[rows] = reduced[:, :B0].reshape(shape + (B0,))
            thin = reduced[:, B0:].reshape(shape + (NARROW,))
            s.narrow[inner, 1 : lay.cols + 1] = thin
            s.border[inner, 1 : lay.cols + 1, :, 0:BP] = projected.reshape(shape + (BP,)).astype(BF16)
            s.border[inner, 1 : lay.cols + 1, :, BP:] = thin.astype(BF16)
            total, square, valid = sums
            return (
                total + column_sum(reduced),
                square + column_sum(reduced * reduced),
                valid + column_sum(mask),
            )

        zero = jnp.zeros((1, REDUCE), F32)
        return loop(lay.rows // step, body, (zero, zero, jnp.zeros((1, 1), F32)))

    def narrow_cells(lay, norm, where):
        s = lay.s
        average, scale, bias = norm
        z = s.narrow[where]
        shape = z.shape[:-1]
        z = z.reshape(-1, NARROW)
        mask = s.mask[where].reshape(-1, 1)
        value = jnp.where(mask > 0.0, softplus((z - average) * scale + bias), 0.0)
        before, after = shifted(lay, value)
        parts = (before, value, after)
        mid = jnp.concatenate([p[:, :B1R] for p in parts], axis=1)
        small = jnp.concatenate([p[:, B1R:] for p in parts], axis=1)
        s.mid_in[where] = mid.astype(BF16).reshape(shape + (3 * B1R,))
        s.small_in[where] = small.astype(BF16).reshape(shape + (3 * B2R,))

    def narrow_center(lay, norm):
        s, step = lay.s, lay.pad_step
        inner = slice(1, lay.cols + 1)
        for row in (0, lay.rows + 1):
            s.narrow[row, inner] = s.border[row, inner, :, BP:].astype(F32)

        def body(i, carry):
            narrow_cells(lay, norm, (pl.ds(i * step, step), inner))
            return carry

        loop((lay.rows + 2) // step, body, 0)

    def narrow_sides(lay, norm):
        s, step = lay.s, lay.pad_step
        for col in (0, lay.cols + 1):
            s.narrow[:, col] = s.border[:, col, :, BP:].astype(F32)
            narrow_cells(lay, norm, (slice(None), col))

        def body(i, carry):
            at = pl.ds(i * step, step)
            s.box[at] = box_row(lay, s.border[at, :, :, 0:BP].astype(F32))
            return carry

        loop((lay.rows + 2) // step, body, 0)

    def box_row(lay, value):
        cols, t, step = lay.cols, lay.frames, lay.pad_step
        flat = value.reshape(step * (cols + 2) * t, BP)
        before, after = shifted(lay, flat)
        flat = (flat + before + after).reshape(step, cols + 2, t, BP)
        return flat[:, 0:cols] + flat[:, 1 : cols + 1] + flat[:, 2 : cols + 2]

    def box_rows(lay, row):
        box, step = lay.s.box, lay.step
        total = box[pl.ds(row, step)] + box[pl.ds(row + 1, step)] + box[pl.ds(row + 2, step)]
        return total.reshape(step * lay.row_cells, BP) * (1.0 / 27.0)

    def window(lay, ref, row, col, width):
        value = ref[pl.ds(row, lay.rows), pl.ds(col, lay.cols)]
        return value.reshape(lay.cells, width)

    def taps(lay, body, at, begin=0, end=9):
        if lay.index:
            for tap in range(begin, end):
                body(tap, 0)
                progress(1, (at, tap))
            return

        def with_progress(tap, carry):
            body(tap, carry)
            for some in range(begin, end):
                if (0, (at, some)) in SCHEDULE:

                    @pl.when(tap == some)
                    def _(some=some):
                        progress(0, (at, some))

            return carry

        lax.fori_loop(begin, end, with_progress, 0)

    def tap_at(tap):
        return (tap // 3, tap % 3) if isinstance(tap, int) else (lax.div(tap, 3), lax.rem(tap, 3))

    def cube_conv(lay, meanwhile):
        s, at = lay.s, lay.index
        s.mid[:, 0:B1] = jnp.zeros((lay.cells, B1), F32)
        s.small[...] = jnp.zeros(s.small.shape, F32)

        def body(tap, carry):
            row, col = tap_at(tap)
            s.mid[:, 0:B1] += dot(window(lay, s.mid_in, row, col, 3 * B1R), k.v_w_mid[at, tap])
            s.small[...] += dot(window(lay, s.small_in, row, col, 3 * B2R), k.v_w_small[at, tap])
            return carry

        def inner_tap(i):
            return 3 * i + 1

        def outer_tap(i):
            return 3 * (i // 2) + 2 * (i % 2) if isinstance(i, int) else 3 * lax.div(i, 2) + 2 * lax.rem(i, 2)

        for count, to_tap in ((3, inner_tap), (6, outer_tap)):
            if lay.index:
                for i in range(count):
                    body(to_tap(i), 0)
            else:
                lax.fori_loop(0, count, lambda i, carry, to_tap=to_tap: body(to_tap(i), carry), 0)
            if to_tap is inner_tap:
                meanwhile()

    def second_rows(lay, i):
        cells = cells_of(lay, i)
        return [
            ref[cells, 0:n] for ref, n in zip((lay.s.mid, lay.s.small, lay.s.pool), SECOND)
        ]

    def second_sums(lay):
        def body(i, sums):
            lay.s.pool[cells_of(lay, i), :] = box_rows(lay, i * lay.step)
            mask = center_mask(lay, i * lay.step, lay.step)
            out = []
            for (total, square), value in zip(sums, second_rows(lay, i)):
                inside = value * mask
                out.append((total + column_sum(inside), square + column_sum(inside * value)))
            return tuple(out)

        zero = tuple((jnp.zeros((1, n), F32),) * 2 for n in SECOND)
        return loop(lay.rows // lay.step, body, zero)

    def put_second(at, sums):
        for which in range(2):
            for begin, part, width in zip(SECOND_AT, sums, SECOND):
                begin += which * SECOND_WIDTH
                k.sums[at, :, begin : begin + width] = part[which]

    def get_second(total, which):
        return [total[:, which * SECOND_WIDTH + a : which * SECOND_WIDTH + a + n] for a, n in zip(SECOND_AT, SECOND)]

    def put_first(at, sums):
        for which in range(2):
            k.sums[at, :, which * 512 : which * 512 + REDUCE] = sums[which]

    def get_first(total, which):
        return total[:, which * 512 : which * 512 + REDUCE]

    def second_params(k_of, at):
        row = k_of[at : at + 1, :]
        out, begin = [], REDUCE
        for width in SECOND:
            out.append(row[:, begin : begin + width])
            begin += width
        return out

    def first_params(k_of, at):
        return k_of[at : at + 1, 0:REDUCE]

    def forward(lay, at, count, cubes, before, first_idle, after_first, in_conv, second_idle):
        s = lay.s
        total, square, valid = reduce_conv(lay)
        before()
        put_first(at, (total, square))
        if count is None:
            k.sums[at, :, 1024:1152] = jnp.broadcast_to(valid, (1, 128))
        start_sum(at)
        start_halo(lay, s.border, 2 * lay.index)
        first_idle()
        end_halo(lay, s.border, 2 * lay.index, cols=False)
        for copy in cubes:
            copy.wait()
        summed = end_sum(at)
        if count is None:
            count = summed[:, 1024:1025]
        gain = first_params(k.gain, lay.index)
        first = batch_norm_scale(get_first(summed, 0), get_first(summed, 1), count, gain)
        first += (first_params(k.bias, lay.index), gain)
        after_first()
        thin = (first[0][:, B0:], first[2][:, B0:], first[3][:, B0:])
        narrow_center(lay, thin)

        def sides():
            end_halo(lay, s.border, 2 * lay.index, rows=False)
            narrow_sides(lay, thin)
            in_conv()

        cube_conv(lay, sides)
        put_second(at + 1, second_sums(lay))
        start_sum(at + 1)
        second_idle()
        summed = end_sum(at + 1)
        second = []
        for total, square, gain, bias in zip(
            get_second(summed, 0),
            get_second(summed, 1),
            second_params(k.gain, lay.index),
            second_params(k.bias, lay.index),
        ):
            second.append(batch_norm_scale(total, square, count, gain) + (bias, gain))
        return first, second, count

    def normalised(value, norm):
        average, inv_std, scale, bias, gain = norm
        return (value - average) * inv_std

    def affine(value, norm):
        average, inv_std, scale, bias, gain = norm
        return (value - average) * scale + bias

    def left_half(norm):
        return tuple(p[:, :B0] for p in norm)

    def outputs(lay, i, first, second):
        mask = center_mask(lay, i * lay.step, lay.step)
        z = lay.s.first[pl.ds(i * lay.step, lay.step)].reshape(lay.step * lay.row_cells, B0)
        parts = [softplus(affine(z, left_half(first))) * mask]
        parts += [softplus(affine(v, n)) * mask for v, n in zip(second_rows(lay, i), second)]
        return parts

    def put_normed(lay, second):
        def body(i, carry):
            inner = pl.ds(i * lay.step + 1, lay.step)
            for begin, width, v, n in zip(SECOND_AT, SECOND, second_rows(lay, i), second):
                normed = normalised(v, n).astype(BF16)
                normed = normed.reshape(lay.step, lay.cols, lay.frames, width)
                lay.s.normed[inner, 1 : lay.cols + 1, :, begin : begin + width] = normed
            return carry

        loop(lay.rows // lay.step, body, 0)

    for copy in flat_one:
        copy.wait()

    def wait_barrier():
        for copy in cubes_one + [slope_load] + flat_two + cubes_two:
            copy.start()
        beside = (w > 0).astype(jnp.int32) + (w < n_wa - 1).astype(jnp.int32)
        pl.semaphore_wait(barrier, chips + beside)

    def spread_two():
        slope_load.wait()
        for row in range(two.rows):
            k.slopes[pl.ds(row * two.row_cells, two.row_cells), :] = reorder(
                two, k.v_out_grad[:, row], True
            ).astype(BF16)
        for a, part, width in zip(SECOND_AT, slope_two(0)[1:], SECOND):
            part = part.reshape(two.rows, two.cols, two.frames, width).astype(BF16)
            k.grad_border[0, 1 : two.rows + 1, 1 : two.cols + 1, :, a : a + width] = part
        start_halo(two, k.grad_border.at[0], 4)

    def nothing():
        return None

    def split(value):
        a, b_, c, d = B0, B0 + B1, B0 + B1 + B2, B0 + B1 + B2 + BP
        return [value[:, :a], value[:, a:b_], value[:, b_:c], value[:, c:d]]

    def slope_two(i):
        return split(k.slopes[...].astype(F32))

    first_one, second_one, count_one = forward(
        one, 0, None, cubes_one, wait_barrier, nothing, nothing, spread_two, nothing
    )

    def halve(row, carry):
        begin = 0
        for p in outputs(one, row, first_one, second_one):
            width = p.shape[-1]
            both = p.reshape(2, two.cols, 2, one.frames, width)
            both = both[0, :, 0] + both[0, :, 1] + both[1, :, 0] + both[1, :, 1]
            for lane in range(0, width, 128):
                size = min(128, width - lane)
                k.pairs[:, begin + lane // 128, :, 0:size] = both[:, :, lane : lane + size]
            begin += -(-width // 128)
        for col in range(two.cols):
            tiles = []
            for lane in range(begin):
                even = k.pairs[col, lane, pl.ds(0, two.frames, stride=2), :]
                odd = k.pairs[col, lane, pl.ds(1, two.frames, stride=2), :]
                tiles.append((even + odd) * 0.125)
            half = (B0 + B1) // 128
            tiles[half] = tiles[half][:, : (B0 + B1) % 128]
            mean = jnp.concatenate(tiles, axis=1)
            two.s.block_in[row, col] = mean.astype(BF16)
        return carry

    put_normed(one, second_one)
    start_normed(*NORMED_AT[0])
    lax.fori_loop(0, two.rows, halve, 0)

    for copy in flat_two:
        copy.wait()

    def share_normed():
        start_normed(*NORMED_AT[1])

    def share_third():
        start_normed(*NORMED_AT[2])

    def share_rest():
        start_normed(*NORMED_AT[3])

    first_two, second_two, count_two = forward(
        two, 2, count_one * 0.125, cubes_two, nothing, share_normed, share_third, nothing, share_rest
    )

    def backward(lay, out_slope, border_slope, at, first, second, count, before_end, after_end, before_low):
        s, index, step = lay.s, lay.index, lay.step
        chunks = lay.rows // step
        per_cell = 1.0 / count

        def second_slope(i):
            mask = center_mask(lay, i * step, step)
            values = second_rows(lay, i)
            normed = [normalised(v, n) for v, n in zip(values, second)]
            slopes = [
                g * mask * sigmoid(m * n[4] + n[3])
                for g, m, n in zip(out_slope(i)[1:], normed, second)
            ]
            return mask, normed, slopes

        def sum_body(i, sums):
            mask, normed, slopes = second_slope(i)
            return tuple(
                (t + column_sum(g), q + column_sum(g * m))
                for (t, q), g, m in zip(sums, slopes, normed)
            )

        zero = tuple((jnp.zeros((1, n), F32),) * 2 for n in SECOND)
        put_second(at, loop(chunks, sum_body, zero))
        start_sum(at)
        before_end()
        progress(index, 0)
        summed = end_sum(at)
        after_end()
        totals = list(zip(get_second(summed, 0), get_second(summed, 1)))
        begin = REDUCE
        for (bias_grad, gain_grad), width in zip(totals, SECOND):
            k.bias_grad[index : index + 1, begin : begin + width] = bias_grad
            k.gain_grad[index : index + 1, begin : begin + width] = gain_grad
            begin += width
        totals = [(t * per_cell, q * per_cell) for t, q in totals]

        def pre_slope(g, m, norm, total):
            return norm[2] * (g - (total[0] + m * total[1]))

        def center_body(i, carry):
            mask, normed, slopes = second_slope(i)
            inner = pl.ds(i * step + 1, step)
            for a, width, g, m, n, total in zip(SECOND_AT, SECOND, slopes, normed, second, totals):
                value = (pre_slope(g, m, n, total) * mask).astype(BF16)
                s.normed[inner, 1 : lay.cols + 1, :, a : a + width] = value.reshape(
                    step, lay.cols, lay.frames, width
                )
            return carry

        loop(chunks, center_body, 0)

        def border_cells(where, slopes):
            mask = s.mask[where]
            cells = mask.shape[0]
            mask = mask.reshape(cells * lay.frames, 1)
            normed = s.normed[where].astype(F32).reshape(cells * lay.frames, SECOND_WIDTH)
            for a, width, g, n, total in zip(SECOND_AT, SECOND, slopes, second, totals):
                m = normed[:, a : a + width]
                g = g * sigmoid(m * n[4] + n[3])
                value = jnp.where(mask > 0.0, pre_slope(g, m, n, total), 0.0).astype(BF16)
                s.normed[where + (slice(None), slice(a, a + width))] = value.reshape(
                    cells, lay.frames, width
                )

        border_cells((jnp.where(h == 0, lay.rows + 1, 0), slice(None)), border_slope(True, None))
        for col in (0, lay.cols + 1):
            border_cells((slice(1, lay.rows + 1), col), border_slope(False, col > 0))

        progress(index, 1)

        center = s.normed[1 : lay.rows + 1, 1 : lay.cols + 1].reshape(lay.cells, SECOND_WIDTH)
        turned_mid = center[:, 0:B1].T
        turned_small = center[:, 384:512].T

        def tap_body(tap, carry):
            row, col = tap_at(tap)
            mid = dot(turned_mid, window(lay, s.mid_in, row, col, 3 * B1R)).astype(BF16)
            small = dot(turned_small, window(lay, s.small_in, row, col, 3 * B2R)).astype(BF16)
            store_blocks(index, tap * TAP_BLOCKS, mid)
            store_blocks(index, tap * TAP_BLOCKS + 80, small)
            return carry

        taps(lay, tap_body, 5, 0, EARLY_TAPS[index])

        s.mid[...] = jnp.zeros(s.mid.shape, F32)
        s.small[:, 0 : 3 * B2R] = jnp.zeros((lay.cells, 3 * B2R), F32)

        def back_body(tap, carry):
            row, col = tap_at(tap)
            slope = window(lay, s.normed, 2 - row, 2 - col, SECOND_WIDTH)
            s.mid[...] += dot(slope[:, 0:B1], k.v_w_mid[index, tap], NT)
            s.small[:, 0 : 3 * B2R] += dot(slope[:, 384:512], k.v_w_small[index, tap], NT)
            return carry

        taps(lay, back_body, 2)

        def box_body(i, carry):
            at = pl.ds(i * lay.pad_step, lay.pad_step)
            s.box[at] = box_row(lay, s.normed[at, :, :, 512:640].astype(F32))
            return carry

        loop((lay.rows + 2) // lay.pad_step, box_body, 0)
        progress(index, 3)

        def first_normed(i):
            size = step * lay.row_cells
            z = s.first[pl.ds(i * step, step)].reshape(size, B0)
            z_thin = s.narrow[pl.ds(i * step + 1, step), 1 : lay.cols + 1].reshape(size, NARROW)
            return normalised(jnp.concatenate([z, z_thin], axis=1), first)

        def first_body(i, sums):
            cells = cells_of(lay, i)
            s.projected_slope[cells, :] = box_rows(lay, i * step).astype(BF16)
            mid = s.mid[cells, :]
            small = s.small[cells, 0 : 3 * B2R]
            thirds = [
                jnp.concatenate(
                    [mid[:, B1R * t : B1R * (t + 1)], small[:, B2R * t : B2R * (t + 1)]], axis=1
                )
                for t in range(3)
            ]
            thin = thirds[1] + shifted(lay, thirds[2])[0] + shifted(lay, thirds[0])[1]
            mask = center_mask(lay, i * step, step)
            normed = first_normed(i)
            g = jnp.concatenate([out_slope(i)[0], thin], axis=1)
            g = g * mask * sigmoid(normed * first[4] + first[3])
            s.mid[cells, 0:REDUCE] = g
            return sums[0] + column_sum(g), sums[1] + column_sum(g * normed)

        zero = (jnp.zeros((1, REDUCE), F32),) * 2
        put_first(at + 1, loop(chunks, first_body, zero))
        start_sum(at + 1)

        progress(index, 4)

        taps(lay, tap_body, 5, EARLY_TAPS[index])
        store_blocks(index, LOW_AT + 196, dot(s.projected_slope[...].T, flat_block(lay)).astype(BF16))
        progress(index, 6)
        summed = end_sum(at + 1)
        total = (get_first(summed, 0), get_first(summed, 1))
        k.bias_grad[index : index + 1, 0:REDUCE] = total[0]
        k.gain_grad[index : index + 1, 0:REDUCE] = total[1]

        total = (total[0] * per_cell, total[1] * per_cell)

        def low_body(i, carry):
            cells = cells_of(lay, i)
            mask = center_mask(lay, i * step, step)
            value = pre_slope(s.mid[cells, 0:REDUCE], first_normed(i), first, total) * mask
            s.low[cells, :] = value.astype(BF16)
            return carry

        loop(chunks, low_body, 0)
        before_low()
        progress(index, 7)
        store_blocks(index, LOW_AT, dot(s.low[...].T, flat_block(lay)).astype(BF16))
        progress(index, 8)

    def widen(ref, begin, value):
        width = value.shape[-1]
        for lane in range(0, width, 128):
            size = min(128, width - lane)
            for odd in range(2):
                ref[(begin + lane) // 128, pl.ds(odd, two.frames, stride=2), 0:size] = value[
                    :, lane : lane + size
                ]

    def wide(value, a, width):
        tiles = [value[..., lane // 128, :, :] for lane in range(a, a + width, 128)]
        return jnp.concatenate(tiles, axis=-1)[..., :width]

    def put_two(i, slope):
        slope = slope * 0.125
        for a, part in zip((0,) + tuple(B0 + a for a in SECOND_AT), split(slope)):
            width = part.shape[-1]
            part = part.reshape(two.rows, two.cols, two.frames, width)
            for row in range(two.rows):
                for col in range(two.cols):
                    widen(k.spread.at[row, col], a, part[row, col])
            if a >= B0:
                inner = (slice(1, two.rows + 1), slice(1, two.cols + 1), slice(None))
                k.grad_border[(1,) + inner + (slice(a - B0, a - B0 + width),)] = part.astype(BF16)

    def input_slope(lay, low, projected):
        slope = dot(low, k.v_w_reduce[lay.index])
        return slope + dot(projected, k.v_w_pool[lay.index], NT)

    def low_two():
        mask = center_mask(two, 0, two.rows)
        put_two(0, input_slope(two, two.s.low[...], two.s.projected_slope[...]) * mask)

    def side(lay, across, last):
        if across:
            return (jnp.where(h == 0, lay.rows + 1, 0), slice(None))
        return (slice(1, lay.rows + 1), lay.cols + 1 if last else 0)

    def border_two(across, last):
        value = k.grad_border[(0,) + side(two, across, last)].astype(F32)
        value = value.reshape(value.shape[0] * two.frames, SECOND_WIDTH)
        return [value[:, a : a + n] for a, n in zip(SECOND_AT, SECOND)]

    def end_two():
        put_normed(two, second_two)
        start_halo(two, two.s.normed, 3)
        value = jnp.concatenate(outputs(two, 0, first_two, second_two), axis=1).astype(BF16)
        for row in range(two.rows):
            part = reorder(two, value[row * two.row_cells : (row + 1) * two.row_cells], False)
            k.block_output[:, row] = part.reshape(two.frames, two.cols, -1).astype(BF16)
        end_halo(two, two.s.normed, 3)
        end_halo(two, k.grad_border.at[0], 4)

    def after_two():
        start_normed(*NORMED_AT[4])

    backward(two, slope_two, border_two, 4, first_two, second_two, count_two, end_two, after_two, low_two)
    start_halo(two, k.grad_border.at[1], 5)

    def slope_one(i):
        value = k.spread[i]
        out = []
        for a, width in zip((0,) + tuple(B0 + a for a in SECOND_AT), (B0,) + SECOND):
            part = wide(value, a, width)
            pieces = [part[col // 2] for col in range(one.cols)]
            out.append(jnp.concatenate(pieces * one.step, axis=0))
        return out

    def border_one(across, last):
        where = side(two, across, last)
        value = k.border_spread[where] if across else k.border_spread[:, where[1]]
        cells = range(one.cols + 2) if across else range(1, one.rows + 1)
        out = []
        for a, n in zip(SECOND_AT, SECOND):
            part = wide(value, a, n)
            out.append(jnp.concatenate([part[(cell + 1) // 2] for cell in cells], axis=0))
        return out

    def end_one():
        end_normed()
        end_halo(two, k.grad_border.at[1], 5)
        places = [(side(two, True, None)[0], col) for col in range(two.cols + 2)]
        places += [(row, col) for row in range(1, two.rows + 1) for col in (0, two.cols + 1)]
        for row, col in places:
            widen(k.border_spread.at[row, col], 0, k.grad_border[1, row, col].astype(F32))

    backward(one, slope_one, border_one, 6, first_one, second_one, count_one, end_one, nothing, nothing)

    def input_row(row, carry):
        cells = pl.ds(pl.multiple_of(row * one.row_cells, one.row_cells), one.row_cells)
        low = reorder(one, one.s.low[cells, :], False).astype(BF16)
        projected = one.s.projected_slope[cells, :].astype(F32) * center_mask(one, row)
        projected = reorder(one, projected.astype(BF16), False).astype(BF16)
        slope = input_slope(one, low, projected)
        k.input_grad[:, row] = slope.reshape(one.frames, one.cols, -1).astype(BF16)
        return carry

    lax.fori_loop(0, one.rows, input_row, 0)
    for step in plan[None]:
        step()


UNPACK_TAPS = 3


def unpack_body(taps, low, mid_out, small_out, reduce_out, pool_out):
    def lanes(blocks, tiles, rows, width):
        parts = []
        for tile in range(tiles):
            size = min(128, width - 128 * tile)
            part = blocks[tile * (rows // 16) : (tile + 1) * (rows // 16), :, 0:size]
            parts.append(part.reshape(rows, size))
        return jnp.concatenate(parts, axis=1)

    def tap_body(tap, carry):
        blocks = taps.at[0, pl.ds(tap * TAP_BLOCKS, TAP_BLOCKS)]
        mid = lanes(blocks, 4, B1, 3 * B1R).T.astype(F32)
        small = lanes(blocks.at[80:88], 1, B2, 3 * B2R).T.astype(F32)
        for t in range(3):
            mid_out[0, t, tap] = mid[B1R * t : B1R * (t + 1)]
            small_out[0, t, tap] = small[B2R * t : B2R * (t + 1)]
        return carry

    lax.fori_loop(0, UNPACK_TAPS, tap_body, 0)

    @pl.when(pl.program_id(1) == 0)
    def _():
        channels = reduce_out.shape[-1]
        tiles = -(-channels // 128)
        reduce_out[0] = lanes(low.at[0, 0:196], tiles, REDUCE, channels).astype(F32)
        pool_out[0] = lanes(low.at[0, 196:252], tiles, BP, channels).T.astype(F32)


def unpack(grads, channels):
    n = UNPACK_TAPS
    shapes = ((2, 3, 9, B1R, B1), (2, 3, 9, B2R, B2), (2, REDUCE, channels), (2, channels, BP))
    mid_grad, small_grad, reduce_grad, pool_grad = pl.pallas_call(
        unpack_body,
        grid=(2, 9 // n),
        out_shape=[jax.ShapeDtypeStruct(shape, F32) for shape in shapes],
        in_specs=[
            pl.BlockSpec((1, n * TAP_BLOCKS, 16, 128), lambda i, j: (i, j, 0, 0)),
            pl.BlockSpec((1, 256, 16, 128), lambda i, j: (i, LOW_OUT // 256, 0, 0)),
        ],
        out_specs=[
            pl.BlockSpec((1, 3, n, B1R, B1), lambda i, j: (i, 0, j, 0, 0)),
            pl.BlockSpec((1, 3, n, B2R, B2), lambda i, j: (i, 0, j, 0, 0)),
            pl.BlockSpec((1, REDUCE, channels), lambda i, j: (i, 0, 0)),
            pl.BlockSpec((1, channels, BP), lambda i, j: (i, 0, 0)),
        ],
        compiler_params=pltpu.CompilerParams(vmem_limit_bytes=60 * 1024 * 1024),
        name="unpack",
    )(grads, grads)
    return (
        jnp.swapaxes(reduce_grad, 1, 2),
        mid_grad.reshape(2, 27, B1R, B1),
        small_grad.reshape(2, 27, B2R, B2),
        pool_grad,
    )


def on_device(
    n_batch, n_wa, clip_features, frame_counts, w_reduce, w_mid, w_small, w_pool, norm_gain, norm_bias, out_grad
):
    frames, rows, cols, channels = clip_features.shape
    clips = frame_counts.shape[0]
    slot = frames // clips
    layers = (
        Layer(0, rows, cols, clips, slot),
        Layer(1, rows // 2, cols // 2, clips, slot // 2),
    )
    one, two = layers
    chips = n_batch * n_wa

    operands = dict(
        features=clip_features,
        frame_counts=frame_counts,
        w_reduce=jnp.swapaxes(w_reduce, 1, 2),
        w_mid=w_mid.reshape(2, 3, 9, B1R, B1),
        w_small=w_small.reshape(2, 3, 9, B2R, B2),
        w_pool=w_pool,
        gain=norm_gain,
        bias=norm_bias,
        out_grad=out_grad,
    )
    in_space = dict(frame_counts=pltpu.SMEM, gain=pltpu.VMEM, bias=pltpu.VMEM)
    out_space = dict(weight_grads=pl.ANY)
    results = dict(
        block_output=jax.ShapeDtypeStruct(out_grad.shape, BF16),
        input_grad=jax.ShapeDtypeStruct(clip_features.shape, BF16),
        weight_grads=jax.ShapeDtypeStruct((2, LOW_OUT + 256, 16, 128), BF16),
        gain_grad=jax.ShapeDtypeStruct(norm_gain.shape, F32),
        bias_grad=jax.ShapeDtypeStruct(norm_bias.shape, F32),
    )
    scratch = {}
    for name in ("w_reduce", "w_pool", "out_grad"):
        scratch["v_" + name] = pltpu.VMEM(operands[name].shape, BF16)
    scratch.update(
        v_w_mid=pltpu.VMEM((2, 9, 3 * B1R, B1), BF16),
        v_w_small=pltpu.VMEM((2, 9, 3 * B2R, B2), BF16),
    )
    small_pad = (two.rows + 2, two.cols + 2)
    scratch.update(
        slopes=pltpu.VMEM((two.cells, channels), BF16),
        pairs=pltpu.VMEM((two.cols, (B0 + SECOND_WIDTH) // 128, one.frames, 128), F32),
        spread=pltpu.VMEM(
            (two.rows, two.cols, (B0 + SECOND_WIDTH) // 128, one.frames, 128), F32
        ),
        border_spread=pltpu.VMEM(small_pad + (SECOND_WIDTH // 128, one.frames, 128), F32),
        grad_border=pltpu.VMEM((2,) + small_pad + (two.frames, SECOND_WIDTH), BF16),
        sums=pltpu.VMEM((8, 1, SUM_WIDTH), F32),
        pair_sums=pltpu.VMEM((8, 1, SUM_WIDTH), F32),
        chip_sums=pltpu.VMEM((2, chips, 1, SUM_WIDTH), F32),
        load_sem=pltpu.SemaphoreType.DMA((17,)),
        feature_sem=pltpu.SemaphoreType.DMA((one.rows // one.step,)),
        pair_sem=pltpu.SemaphoreType.DMA((2, 8)),
        chip_sem=pltpu.SemaphoreType.DMA((2, 8)),
        normed_sem=pltpu.SemaphoreType.DMA((2, 4, 3)),
        halo_sem=pltpu.SemaphoreType.DMA((2, 6, 5)),
        grads=pltpu.VMEM((2, GRAD_BLOCKS, 16, 128), BF16),
        got_half=pltpu.VMEM((2, GRAD_BLOCKS // 2, 16, 128), BF16),
        got_eighth=pltpu.VMEM((2, GRAD_BLOCKS // 4, 16, 128), BF16),
        got_piece=pltpu.VMEM((2, GRAD_BLOCKS // 8, 16, 128), BF16),
        got_chunk=pltpu.VMEM((2, n_batch, GRAD_BLOCKS // 32, 16, 128), BF16),
        got_total=pltpu.VMEM((2, OWNERS, GRAD_BLOCKS // 32, 16, 128), BF16),
        free_sem=pltpu.SemaphoreType.REGULAR((2, 3, 3)),
        grad_sem=pltpu.SemaphoreType.DMA((2, 2, 3, 18)),
        out_sem=pltpu.SemaphoreType.DMA((2, 3)),
    )
    names = list(operands) + list(results) + list(scratch)
    layer_scratch = [lay.scratch(channels) for lay in layers]

    def body(*refs):
        rest = refs[len(names) :]
        for lay, parts in zip(layers, layer_scratch):
            lay.s = SimpleNamespace(**dict(zip(parts, rest[: len(parts)])))
            rest = rest[len(parts) :]
        kernel_body(names, (n_batch, n_wa, layers), refs[: len(names)])

    out = pl.pallas_call(
        body,
        out_shape=list(results.values()),
        in_specs=[pl.BlockSpec(memory_space=in_space.get(name, pl.ANY)) for name in operands],
        out_specs=[pl.BlockSpec(memory_space=out_space.get(name, pltpu.VMEM)) for name in results],
        scratch_shapes=list(scratch.values()) + [r for parts in layer_scratch for r in parts.values()],
        compiler_params=pltpu.CompilerParams(
            collective_id=0, has_side_effects=True, vmem_limit_bytes=63 * 1024 * 1024
        ),
        name="layers",
    )(*operands.values())
    out = dict(zip(results, out))

    reduce_grad, mid_grad, small_grad, pool_grad = unpack(out["weight_grads"], channels)

    return (
        out["block_output"],
        out["input_grad"],
        reduce_grad,
        mid_grad,
        small_grad,
        pool_grad,
        out["gain_grad"],
        out["bias_grad"],
    )


def solution(mesh):
    in_specs = (
        P("batch", "ha", "wa", None),
        P("batch"),
        P(),
        P(),
        P(),
        P(),
        P(),
        P(),
        P("batch", "ha", "wa", None),
    )
    out_specs = (
        P("batch", "ha", "wa", None),
        P("batch", "ha", "wa", None),
        P(),
        P(),
        P(),
        P(),
        P(),
        P(),
    )
    return jax.shard_map(
        functools.partial(on_device, mesh.shape["batch"], mesh.shape["wa"]),
        mesh=mesh,
        in_specs=in_specs,
        out_specs=out_specs,
        check_vma=False,
    )
```

```python
import functools
from types import SimpleNamespace

import jax
import jax.numpy as jnp
from jax import lax
from jax.experimental import pallas as pl
from jax.experimental.pallas import tpu as pltpu
from jax.sharding import PartitionSpec as P

HEIGHT = 14
EPSILON = 1e-05
MESH = pl.DeviceIdType.MESH
F32 = jnp.float32
BF16 = jnp.bfloat16

B0, B1R, B2R, B1, B2, BP = 256, 160, 32, 320, 128, 128
NARROW = B1R + B2R
REDUCE = B0 + NARROW
SECOND = (B1, B2, BP)
SECOND_AT = (0, 384, 512)
SECOND_WIDTH = 640
SUM_WIDTH = 1280
AXES = ("batch", "ha", "wa")

TAP_BLOCKS = 88
LOW_AT = 800
LOW_OUT = 1024
GRAD_BLOCKS = 1056
BUNDLES = ((0, 352), (352, 448), (800, 256))
OWNERS = 4

SCHEDULE = {
    (1, (5, 3)): ((1, 0),),
    (1, (5, 8)): ((1, 1),),
    (1, 6): ((1, 0),),
    (1, 8): ((1, 2),),
    (0, 0): ((1, 1), (1, 0),),
    (0, (5, 0)): ((1, 1),),
    (0, (5, 1)): ((1, 2), (1, 0),),
    (0, (5, 3)): ((0, 0),),
    (0, (5, 5)): ((1, 1),),
    (0, (5, 6)): ((0, 0),),
    (0, (5, 8)): ((0, 1), (1, 2),),
    (0, (2, 0)): ((1, 0),),
    (0, (2, 2)): ((0, 1),),
    (0, (2, 5)): ((1, 1), (1, 2),),
    (0, (2, 7)): ((0, 0),),
    (0, (2, 8)): ((1, 0),),
    (0, 4): ((0, 1),),
    (0, 6): ((0, 0), (1, 1), (1, 0), (1, 2),),
    (0, 8): ((0, 2), (0, 1), (0, 2), (1, 1), (0, 0),),
}
EARLY_TAPS = (9, 0)
LAST_STEPS = (
    (1, 2),
    (1, 0),
    (1, 0),
    (0, 2),
    (0, 1),
    (1, 0),
    (0, 0),
    (1, 1),
    (1, 2),
    (0, 2),
    (1, 1),
    (0, 1),
    (0, 0),
    (1, 2),
    (0, 2),
    (0, 1),
    (1, 2),
    (1, 1),
    (0, 0),
    (0, 2),
    (0, 0),
    (1, 2),
    (0, 1),
    (0, 2),
    (0, 1),
    (0, 0),
    (0, 1),
    (0, 2),
    (0, 2),
    (0, 2),
)

NORMED_AT = ((0,), (1,), (2,), (3,), ())

NN = (((1,), (0,)), ((), ()))
NT = (((1,), (1,)), ((), ()))


def dot(a, b, dims=NN):
    return lax.dot_general(a, b, dims, preferred_element_type=F32)


def softplus(x):
    return jnp.maximum(x, 0.0) + jnp.log(1.0 + jnp.exp(-jnp.abs(x)))


def sigmoid(x):
    return 1.0 / (1.0 + jnp.exp(-x))


def loop(count, body, init):
    return body(0, init) if count == 1 else lax.fori_loop(0, count, body, init)


class Layer:
    def __init__(self, index, rows, cols, clips, slot):
        self.index, self.rows, self.cols = index, rows, cols
        self.clips, self.slot = clips, slot
        self.frames = clips * slot
        self.cells = rows * cols * self.frames
        self.row_cells = cols * self.frames
        self.step = rows if index else 2
        self.pad_step = rows + 2 if index else 2

    def scratch(self, channels):
        r, c, t, n = self.rows, self.cols, self.frames, self.cells
        pad = (r + 2, c + 2, t)
        return dict(
            mask=pltpu.VMEM(pad + (1,), F32),
            block_in=pltpu.VMEM((r, c, t, channels), BF16),
            first=pltpu.VMEM((r, c, t, B0), F32),
            narrow=pltpu.VMEM(pad + (NARROW,), F32),
            border=pltpu.VMEM(pad + (BP + NARROW,), BF16),
            mid_in=pltpu.VMEM(pad + (3 * B1R,), BF16),
            small_in=pltpu.VMEM(pad + (3 * B2R,), BF16),
            box=pltpu.VMEM((r + 2, c, t, BP), F32),
            mid=pltpu.VMEM((n, 3 * B1R), F32),
            small=pltpu.VMEM((n, B2), F32),
            pool=pltpu.VMEM((n, BP), F32),
            normed=pltpu.VMEM(pad + (SECOND_WIDTH,), BF16),
            projected_slope=pltpu.VMEM((n, BP), BF16),
            low=pltpu.VMEM((n, REDUCE), BF16),
        )


def batch_norm_scale(total, square, count, gain):
    average = total / count
    variance = square / count - average * average
    inv_std = lax.rsqrt(variance + EPSILON)
    return average, inv_std, inv_std * gain


def kernel_body(names, sizes, refs):
    k = SimpleNamespace(**dict(zip(names, refs)))
    n_batch, n_wa, layers = sizes
    b, h, w = (lax.axis_index(a) for a in AXES)
    chips = n_batch * n_wa
    my_chip = b * n_wa + w
    one, two = layers

    def chip_at(p):
        return lax.div(p, n_wa), h, lax.rem(p, n_wa)

    def rotated(i):
        return lax.rem(my_chip + i, chips)

    def load(at, source, target):
        return pltpu.make_async_copy(source, target, k.load_sem.at[at])

    def load_features(i):
        rows = pl.ds(i * one.step, one.step)
        return pltpu.make_async_copy(
            k.features.at[:, rows], k.input_grad.at[:, rows], k.feature_sem.at[i]
        )

    def load_cubes(at, layer):
        copies = []
        for t in range(3):
            mid, small = pl.ds(B1R * t, B1R), pl.ds(B2R * t, B2R)
            copies.append(load(at + 2 * t, k.w_mid.at[layer, t], k.v_w_mid.at[layer, :, mid]))
            copies.append(load(at + 2 * t + 1, k.w_small.at[layer, t], k.v_w_small.at[layer, :, small]))
        return copies

    def load_flat(at, layer):
        return [
            load(at, k.w_reduce.at[layer], k.v_w_reduce.at[layer]),
            load(at + 1, k.w_pool.at[layer], k.v_w_pool.at[layer]),
        ]

    flat_one, flat_two = load_flat(0, 0), load_flat(2, 1)
    cubes_one, cubes_two = load_cubes(4, 0), load_cubes(10, 1)
    slope_load = load(16, k.out_grad, k.v_out_grad)
    for copy in flat_one:
        copy.start()
    for i in range(one.rows // one.step):
        load_features(i).start()
    for lay in layers:
        s = lay.s
        for ref in (s.border, s.normed):
            for row in (0, lay.rows + 1):
                ref[row] = jnp.zeros(ref.shape[1:], ref.dtype)
            for col in (0, lay.cols + 1):
                ref[:, col] = jnp.zeros((ref.shape[0],) + ref.shape[2:], ref.dtype)
    ref = k.grad_border
    ref[...] = jnp.zeros(ref.shape, ref.dtype)
    for layer in range(2):
        for begin, end in ((9 * TAP_BLOCKS, LOW_AT), (LOW_AT + 252, GRAD_BLOCKS)):
            k.grads[layer, begin:end] = jnp.zeros((end - begin, 16, 128), BF16)
    k.sums[...] = jnp.zeros(k.sums.shape, F32)

    barrier = pltpu.get_barrier_semaphore()
    pl.semaphore_signal(barrier, inc=1, device_id=(b, 1 - h, w), device_id_type=MESH)

    @pl.when(w > 0)
    def _():
        pl.semaphore_signal(barrier, inc=1, device_id=(b, 1 - h, w - 1), device_id_type=MESH)

    @pl.when(w < n_wa - 1)
    def _():
        pl.semaphore_signal(barrier, inc=1, device_id=(b, 1 - h, w + 1), device_id_type=MESH)

    def greet(i, carry):
        pl.semaphore_signal(barrier, inc=1, device_id=chip_at(rotated(i)), device_id_type=MESH)
        return carry

    lax.fori_loop(1, chips, greet, 0)

    for lay in layers:
        frame_at = lax.broadcasted_iota(jnp.int32, (lay.frames, 1), 0)
        inside = jnp.zeros((lay.frames, 1), F32)
        for clip in range(lay.clips):
            valid = k.frame_counts[clip]
            valid = valid if lay.index == 0 else lax.div(valid, 2)
            begin = clip * lay.slot
            inside = jnp.where((frame_at >= begin) & (frame_at < begin + valid), 1.0, inside)
        height = HEIGHT if lay.index == 0 else HEIGHT // 2
        for row in range(lay.rows + 2):
            at_row = h * lay.rows + row - 1
            for col in range(lay.cols + 2):
                at_col = w * lay.cols + col - 1
                good = (at_row >= 0) & (at_row < height) & (at_col >= 0) & (at_col < height)
                lay.s.mask[row, col] = inside * good.astype(F32)

    def start_sum(at):
        pair = pltpu.make_async_remote_copy(
            src_ref=k.sums.at[at],
            dst_ref=k.pair_sums.at[at],
            send_sem=k.pair_sem.at[0, at],
            recv_sem=k.pair_sem.at[1, at],
            device_id=(b, 1 - h, w),
            device_id_type=MESH,
        )
        pair.start()
        pair.wait()
        k.chip_sums[at % 2, my_chip] = k.sums[at] + k.pair_sums[at]

        def send(i, carry):
            pltpu.make_async_remote_copy(
                src_ref=k.chip_sums.at[at % 2, my_chip],
                dst_ref=k.chip_sums.at[at % 2, my_chip],
                send_sem=k.chip_sem.at[0, at],
                recv_sem=k.chip_sem.at[1, at],
                device_id=chip_at(rotated(i)),
                device_id_type=MESH,
            ).start()
            return carry

        if chips <= 16:
            for i in range(1, chips):
                send(i, 0)
        else:
            lax.fori_loop(1, chips, send, 0)

    def end_sum(at):
        for way in (1, 0):
            others = k.chip_sums.at[at % 2, pl.ds(0, chips - 1)]
            pltpu.make_async_copy(others, others, k.chip_sem.at[way, at]).wait()
        total = k.chip_sums[at % 2, 0]
        for p in range(1, chips):
            total = total + k.chip_sums[at % 2, p]
        return total

    def halo_copies(lay, ref, at):
        src_row = jnp.where(h == 0, lay.rows, 1)
        dst_row = jnp.where(h == 0, 0, lay.rows + 1)
        rows, cols = lay.rows, lay.cols

        def remote(src, dst, way, device):
            return lambda: pltpu.make_async_remote_copy(
                src_ref=ref.at[src],
                dst_ref=ref.at[dst],
                send_sem=k.halo_sem.at[0, at, way],
                recv_sem=k.halo_sem.at[1, at, way],
                device_id=device,
                device_id_type=MESH,
            )

        all_rows, all_cols = pl.ds(1, rows), pl.ds(1, cols)
        row = remote((src_row, all_cols), (dst_row, all_cols), 0, (b, 1 - h, w))
        to_left = [
            remote((all_rows, 1), (all_rows, cols + 1), 1, (b, h, w - 1)),
            remote((src_row, 1), (dst_row, cols + 1), 2, (b, 1 - h, w - 1)),
        ]
        to_right = [
            remote((all_rows, cols), (all_rows, 0), 3, (b, h, w + 1)),
            remote((src_row, cols), (dst_row, 0), 4, (b, 1 - h, w + 1)),
        ]
        return row, to_left, to_right

    def normed_copies():
        ref, rows, cols = one.s.normed, one.rows, one.cols
        half = rows // 2
        src_row = jnp.where(h == 0, rows, 1)
        dst_row = jnp.where(h == 0, 0, rows + 1)

        def remote(part, slot, src, dst, device):
            return lambda: pltpu.make_async_remote_copy(
                src_ref=ref.at[src],
                dst_ref=ref.at[dst],
                send_sem=k.normed_sem.at[0, part, slot],
                recv_sem=k.normed_sem.at[1, part, slot],
                device_id=device,
                device_id_type=MESH,
            )

        parts = []
        for part in range(4):
            left, low = part < 2, part % 2 == 0
            src, dst = (1, cols + 1) if left else (cols, 0)
            way = w - 1 if left else w + 1
            run = pl.ds(1 if low else 1 + half, half)
            copies = [remote(part, 0, (run, src), (run, dst), (b, h, way))]
            if low:
                copies.append(remote(part, 1, (src_row, src), (dst_row, dst), (b, 1 - h, way)))
            parts.append((w > 0 if left else w < n_wa - 1, w < n_wa - 1 if left else w > 0, copies))
        inner = pl.ds(1, cols)
        row = remote(0, 2, (src_row, inner), (dst_row, inner), (b, 1 - h, w))
        return row, parts

    def start_normed(*which):
        row, parts = normed_copies()
        if 0 in which:
            row().start()
        for part in which:
            sends, _, copies = parts[part]

            @pl.when(sends)
            def _(copies=copies):
                for copy in copies:
                    copy().start()

    def end_normed():
        row, parts = normed_copies()
        row().wait()
        for sends, receives, copies in parts:

            @pl.when(sends)
            def _(copies=copies):
                for copy in copies:
                    copy().wait_send()

            @pl.when(receives)
            def _(copies=copies):
                for copy in copies:
                    copy().wait_recv()

    def start_halo(lay, ref, at, first=True, last=True):
        row, to_left, to_right = halo_copies(lay, ref, at)
        if first:
            row().start()

            @pl.when(w > 0)
            def _():
                for copy in to_left:
                    copy().start()

        if last:

            @pl.when(w < n_wa - 1)
            def _():
                for copy in to_right:
                    copy().start()

    def end_halo(lay, ref, at, rows=True, cols=True):
        row, to_left, to_right = halo_copies(lay, ref, at)
        if rows:
            row().wait()
        if not cols:
            return

        @pl.when(w > 0)
        def _():
            for copy in to_left:
                copy().wait_send()
            for copy in to_right:
                copy().wait_recv()

        @pl.when(w < n_wa - 1)
        def _():
            for copy in to_right:
                copy().wait_send()
            for copy in to_left:
                copy().wait_recv()

    def exchange(layer, number):
        begin, count = BUNDLES[number]
        half, quarter, eighth = count // 2, count // 4, count // 8
        piece, chunk = count // 16, count // 32
        stride = n_batch // OWNERS
        g = k.grads.at[layer]
        r1, r2, r3, r4, r5 = (
            r.at[layer] for r in (k.got_half, k.got_eighth, k.got_piece, k.got_chunk, k.got_total)
        )
        to_half, to_eighth, to_piece, to_chunk = begin // 2, begin // 4, begin // 8, begin // 32

        def places():
            b, h, w = (lax.axis_index(a) for a in AXES)
            x, y = lax.rem(w, 2), lax.div(w, 2)
            at = SimpleNamespace(b=b, h=h, w=w)
            at.pair, at.beside, at.below = (b, 1 - h, w), (b, h, w + 1 - 2 * x), (b, h, w + 2 - 4 * y)
            at.mine, at.other = begin + h * half, begin + (1 - h) * half
            half_a, half_b = at.mine, at.mine + quarter
            at.eighth_a, at.eighth_b = half_a + x * eighth, half_b + y * eighth
            at.a, at.b_ = at.eighth_a + y * piece, at.eighth_b + x * piece
            at.sent_a, at.sent_b = half_a + (1 - x) * eighth, half_b + (1 - y) * eighth
            at.last_a, at.last_b = at.eighth_a + (1 - y) * piece, at.eighth_b + (1 - x) * piece
            at.rank = lax.div(b, stride)
            at.chunk = jnp.where(at.rank < 2, at.a, at.b_) + lax.rem(at.rank, 2) * chunk
            at.chunks = [(at.a, at.b_)[owner // 2] + owner % 2 * chunk for owner in range(OWNERS)]
            return at

        def copy(source, at, target, to, size, slot, device):
            return pltpu.make_async_remote_copy(
                src_ref=source.at[pl.ds(at, size)],
                dst_ref=target.at[pl.ds(to, size)],
                send_sem=k.grad_sem.at[0, layer, number, slot],
                recv_sem=k.grad_sem.at[1, layer, number, slot],
                device_id=device,
                device_id_type=MESH,
            )

        def pair_copies(at):
            return [copy(g, at.other, r1, to_half, half, 0, at.pair)]

        def eighth_copies(at):
            return [
                copy(g, at.sent_a, r2, to_eighth, eighth, 1, at.beside),
                copy(g, at.sent_b, r2, to_eighth + eighth, eighth, 2, at.below),
            ]

        def piece_copies(at):
            return [
                copy(g, at.last_a, r3, to_piece, piece, 3, at.below),
                copy(g, at.last_b, r3, to_piece + piece, piece, 4, at.beside),
            ]

        def piece_returns(at):
            return [
                copy(g, at.a, g, at.a, piece, 13, at.below),
                copy(g, at.b_, g, at.b_, piece, 14, at.beside),
            ]

        def eighth_returns(at):
            return [
                copy(g, at.eighth_a, g, at.eighth_a, eighth, 15, at.beside),
                copy(g, at.eighth_b, g, at.eighth_b, eighth, 16, at.below),
            ]

        def pair_returns(at):
            return [copy(g, at.mine, g, at.mine, half, 17, at.pair)]

        def go(copies):
            for c in copies:
                c.start()

        def end(copies):
            for c in copies:
                c.wait()

        def add(at, other, to, size):
            step = 16 if size % 16 == 0 else size

            def body(i, carry):
                mine = pl.ds(at + i * step, step)
                g[mine] = g[mine] + other[pl.ds(to + i * step, step)]
                return carry

            lax.fori_loop(0, size // step, body, 0)

        def free(slot, device):
            sem = k.free_sem.at[layer, number, slot]
            pl.semaphore_signal(sem, inc=1, device_id=device, device_id_type=MESH)

        def wait_free(slot):
            pl.semaphore_wait(k.free_sem.at[layer, number, slot], 1)

        def for_owner(at, do):
            if stride == 1:
                do()
            else:
                pl.when(lax.rem(at.b, stride) == 0)(do)

        def for_others(at, do):
            for owner in range(OWNERS):
                pl.when(at.b != owner * stride)(functools.partial(do, owner))

        def share_copies(at):
            return [
                pltpu.make_async_remote_copy(
                    src_ref=g.at[pl.ds(at.chunk, chunk)],
                    dst_ref=r5.at[at.rank, pl.ds(to_chunk, chunk)],
                    send_sem=k.grad_sem.at[0, layer, number, 9],
                    recv_sem=k.grad_sem.at[1, layer, number, 9 + at.rank],
                    device_id=(lax.rem(at.b + i, n_batch), at.h, at.w),
                    device_id_type=MESH,
                )
                for i in range(1, n_batch)
            ]

        def start_pair():
            go(pair_copies(places()))

        def start_eighths():
            at = places()
            end(pair_copies(at))
            free(0, at.pair)
            add(at.mine, r1, to_half, half)
            go(eighth_copies(at))

        def start_pieces():
            at = places()
            end(eighth_copies(at))
            add(at.eighth_a, r2, to_eighth, eighth)
            add(at.eighth_b, r2, to_eighth + eighth, eighth)
            go(piece_copies(at))

        def start_chunks():
            at = places()
            end(piece_copies(at))
            free(1, at.below)
            free(2, at.beside)
            add(at.a, r3, to_piece, piece)
            add(at.b_, r3, to_piece + piece, piece)

            def send_chunk(owner):
                pltpu.make_async_remote_copy(
                    src_ref=g.at[pl.ds(at.chunks[owner], chunk)],
                    dst_ref=r4.at[at.b, pl.ds(to_chunk, chunk)],
                    send_sem=k.grad_sem.at[0, layer, number, 5 + owner],
                    recv_sem=k.grad_sem.at[1, layer, number, 5],
                    device_id=(owner * stride, at.h, at.w),
                    device_id_type=MESH,
                ).start()

            for_others(at, send_chunk)

        def share_chunk():
            at = places()

            def collect():
                others = r4.at[pl.ds(0, n_batch - 1), pl.ds(to_chunk, chunk)]
                pltpu.make_async_copy(others, others, k.grad_sem.at[1, layer, number, 5]).wait()
                r4[at.b, pl.ds(to_chunk, chunk)] = g[pl.ds(at.chunk, chunk)]
                total = r4[0, pl.ds(to_chunk, chunk)].astype(F32)
                for slot in range(1, n_batch):
                    total = total + r4[slot, pl.ds(to_chunk, chunk)].astype(F32)
                g[pl.ds(at.chunk, chunk)] = total.astype(BF16)
                go(share_copies(at))

            for_owner(at, collect)

            def sent_chunk(owner):
                part = g.at[pl.ds(at.chunks[owner], chunk)]
                pltpu.make_async_copy(part, part, k.grad_sem.at[0, layer, number, 5 + owner]).wait()

            for_others(at, sent_chunk)

        def return_pieces():
            at = places()

            def shared():
                for c in share_copies(at):
                    c.wait_send()

            for_owner(at, shared)

            def take_chunk(owner):
                part = r5.at[owner, pl.ds(to_chunk, chunk)]
                pltpu.make_async_copy(part, part, k.grad_sem.at[1, layer, number, 9 + owner]).wait()
                g[pl.ds(at.chunks[owner], chunk)] = r5[owner, pl.ds(to_chunk, chunk)]

            for_others(at, take_chunk)
            wait_free(1)
            wait_free(2)
            go(piece_returns(at))

        def return_eighths():
            at = places()
            end(piece_returns(at))
            go(eighth_returns(at))

        def return_halves():
            at = places()
            end(eighth_returns(at))
            wait_free(0)
            go(pair_returns(at))

        def result():
            target = k.weight_grads.at[layer, pl.ds(LOW_OUT if begin == LOW_AT else begin, count)]
            sem = k.out_sem.at[layer, number]
            return pltpu.make_async_copy(g.at[pl.ds(begin, count)], target, sem)

        def start_result():
            end(pair_returns(places()))

            result().start()

        def end_result():
            result().wait()

        return (
            start_pair,
            start_eighths,
            start_pieces,
            start_chunks,
            share_chunk,
            return_pieces,
            return_eighths,
            return_halves,
            start_result,
            end_result,
        )

    exchanges = {(layer, number): exchange(layer, number) for layer in range(2) for number in range(3)}
    plan, taken = {}, dict.fromkeys(exchanges, 0)
    for point, keys in list(SCHEDULE.items()) + [(None, LAST_STEPS)]:
        for key in keys:
            plan.setdefault(point, []).append(exchanges[key][taken[key]])
            taken[key] += 1
    assert all(taken[key] == len(exchanges[key]) for key in exchanges)

    def progress(*point):
        for step in plan.get(point, ()):
            step()

    def flat_block(lay):
        block = lay.s.block_in[...]
        return block.reshape(lay.cells, block.shape[-1])

    def store_blocks(layer, at, value):
        rows, lanes = value.shape
        for lane in range(0, lanes, 128):
            size = min(128, lanes - lane)
            blocks = pl.ds(at + lane // 128 * (rows // 16), rows // 16)
            tile = value[:, lane : lane + size].reshape(rows // 16, 16, size)
            k.grads[layer, blocks, :, 0:size] = tile

    def column_sum(value):
        return jnp.sum(value, axis=0, keepdims=True)

    def center_mask(lay, row, count=1):
        mask = lay.s.mask[pl.ds(row + 1, count), 1 : lay.cols + 1]
        return mask.reshape(count * lay.row_cells, 1)

    def shifted(lay, value):
        count = value.shape[0]
        frame_at = lax.rem(lax.broadcasted_iota(jnp.int32, (count, 1), 0), lay.slot)
        before = jnp.where(frame_at == 0, 0.0, pltpu.roll(value, 1, 0))
        after = jnp.where(frame_at == lay.slot - 1, 0.0, pltpu.roll(value, count - 1, 0))
        return before, after

    def reorder(lay, value, cells_first):
        size, cols, frames = lay.row_cells, lay.cols, lay.frames
        to = lax.broadcasted_iota(jnp.int32, (size, size), 0)
        source = lax.broadcasted_iota(jnp.int32, (size, size), 1)
        if cells_first:
            wanted = lax.rem(to, frames) * cols + lax.div(to, frames)
        else:
            wanted = lax.rem(to, cols) * frames + lax.div(to, cols)
        swap = (source == wanted).astype(F32).astype(BF16)
        return dot(swap, value.reshape(size, value.shape[-1]))

    def cells_of(lay, i):
        size = lay.step * lay.row_cells
        return pl.ds(i * size if isinstance(i, int) else pl.multiple_of(i * size, size), size)

    def reduce_conv(lay):
        s, at, step = lay.s, lay.index, lay.step
        count = step * lay.row_cells

        def body(i, sums):
            mask = center_mask(lay, i * step, step)
            if lay.index == 0:
                load_features(i).wait()
            if lay.index == 0:
                block = [reorder(lay, k.input_grad[:, i * step + row], True) for row in range(step)]
                block = (jnp.concatenate(block, axis=0) * mask).astype(BF16)
                shape = (step, lay.cols, lay.frames, block.shape[-1])
                s.block_in[pl.ds(i * step, step)] = block.reshape(shape)
            else:
                block = s.block_in[pl.ds(i * step, step)]
                block = block.reshape(count, block.shape[-1])
            reduced = dot(block, k.v_w_reduce[at], NT)
            projected = dot(block, k.v_w_pool[at])
            rows = pl.ds(i * step, step)
            inner = pl.ds(i * step + 1, step)
            shape = (step, lay.cols, lay.frames)
            s.first[rows] = reduced[:, :B0].reshape(shape + (B0,))
            thin = reduced[:, B0:].reshape(shape + (NARROW,))
            s.narrow[inner, 1 : lay.cols + 1] = thin
            s.border[inner, 1 : lay.cols + 1, :, 0:BP] = projected.reshape(shape + (BP,)).astype(BF16)
            s.border[inner, 1 : lay.cols + 1, :, BP:] = thin.astype(BF16)
            total, square, valid = sums
            return (
                total + column_sum(reduced),
                square + column_sum(reduced * reduced),
                valid + column_sum(mask),
            )

        zero = jnp.zeros((1, REDUCE), F32)
        return loop(lay.rows // step, body, (zero, zero, jnp.zeros((1, 1), F32)))

    def narrow_cells(lay, norm, where):
        s = lay.s
        average, scale, bias = norm
        z = s.narrow[where]
        shape = z.shape[:-1]
        z = z.reshape(-1, NARROW)
        mask = s.mask[where].reshape(-1, 1)
        value = jnp.where(mask > 0.0, softplus((z - average) * scale + bias), 0.0)
        before, after = shifted(lay, value)
        parts = (before, value, after)
        mid = jnp.concatenate([p[:, :B1R] for p in parts], axis=1)
        small = jnp.concatenate([p[:, B1R:] for p in parts], axis=1)
        s.mid_in[where] = mid.astype(BF16).reshape(shape + (3 * B1R,))
        s.small_in[where] = small.astype(BF16).reshape(shape + (3 * B2R,))

    def narrow_center(lay, norm):
        s, step = lay.s, lay.pad_step
        inner = slice(1, lay.cols + 1)
        for row in (0, lay.rows + 1):
            s.narrow[row, inner] = s.border[row, inner, :, BP:].astype(F32)

        def body(i, carry):
            narrow_cells(lay, norm, (pl.ds(i * step, step), inner))
            return carry

        loop((lay.rows + 2) // step, body, 0)

    def narrow_sides(lay, norm):
        s, step = lay.s, lay.pad_step
        for col in (0, lay.cols + 1):
            s.narrow[:, col] = s.border[:, col, :, BP:].astype(F32)
            narrow_cells(lay, norm, (slice(None), col))

        def body(i, carry):
            at = pl.ds(i * step, step)
            s.box[at] = box_row(lay, s.border[at, :, :, 0:BP].astype(F32))
            return carry

        loop((lay.rows + 2) // step, body, 0)

    def box_row(lay, value):
        cols, t, step = lay.cols, lay.frames, lay.pad_step
        flat = value.reshape(step * (cols + 2) * t, BP)
        before, after = shifted(lay, flat)
        flat = (flat + before + after).reshape(step, cols + 2, t, BP)
        return flat[:, 0:cols] + flat[:, 1 : cols + 1] + flat[:, 2 : cols + 2]

    def box_rows(lay, row):
        box, step = lay.s.box, lay.step
        total = box[pl.ds(row, step)] + box[pl.ds(row + 1, step)] + box[pl.ds(row + 2, step)]
        return total.reshape(step * lay.row_cells, BP) * (1.0 / 27.0)

    def window(lay, ref, row, col, width):
        value = ref[pl.ds(row, lay.rows), pl.ds(col, lay.cols)]
        return value.reshape(lay.cells, width)

    def taps(lay, body, at, begin=0, end=9):
        if lay.index:
            for tap in range(begin, end):
                body(tap, 0)
                progress(1, (at, tap))
            return

        def with_progress(tap, carry):
            body(tap, carry)
            for some in range(begin, end):
                if (0, (at, some)) in SCHEDULE:

                    @pl.when(tap == some)
                    def _(some=some):
                        progress(0, (at, some))

            return carry

        lax.fori_loop(begin, end, with_progress, 0)

    def tap_at(tap):
        return (tap // 3, tap % 3) if isinstance(tap, int) else (lax.div(tap, 3), lax.rem(tap, 3))

    def cube_conv(lay, meanwhile):
        s, at = lay.s, lay.index
        s.mid[:, 0:B1] = jnp.zeros((lay.cells, B1), F32)
        s.small[...] = jnp.zeros(s.small.shape, F32)

        def body(tap, carry):
            row, col = tap_at(tap)
            s.mid[:, 0:B1] += dot(window(lay, s.mid_in, row, col, 3 * B1R), k.v_w_mid[at, tap])
            s.small[...] += dot(window(lay, s.small_in, row, col, 3 * B2R), k.v_w_small[at, tap])
            return carry

        def inner_tap(i):
            return 3 * i + 1

        def outer_tap(i):
            return 3 * (i // 2) + 2 * (i % 2) if isinstance(i, int) else 3 * lax.div(i, 2) + 2 * lax.rem(i, 2)

        for count, to_tap in ((3, inner_tap), (6, outer_tap)):
            if lay.index:
                for i in range(count):
                    body(to_tap(i), 0)
            else:
                lax.fori_loop(0, count, lambda i, carry, to_tap=to_tap: body(to_tap(i), carry), 0)
            if to_tap is inner_tap:
                meanwhile()

    def second_rows(lay, i):
        cells = cells_of(lay, i)
        return [
            ref[cells, 0:n] for ref, n in zip((lay.s.mid, lay.s.small, lay.s.pool), SECOND)
        ]

    def second_sums(lay):
        def body(i, sums):
            lay.s.pool[cells_of(lay, i), :] = box_rows(lay, i * lay.step)
            mask = center_mask(lay, i * lay.step, lay.step)
            out = []
            for (total, square), value in zip(sums, second_rows(lay, i)):
                inside = value * mask
                out.append((total + column_sum(inside), square + column_sum(inside * value)))
            return tuple(out)

        zero = tuple((jnp.zeros((1, n), F32),) * 2 for n in SECOND)
        return loop(lay.rows // lay.step, body, zero)

    def put_second(at, sums):
        for which in range(2):
            for begin, part, width in zip(SECOND_AT, sums, SECOND):
                begin += which * SECOND_WIDTH
                k.sums[at, :, begin : begin + width] = part[which]

    def get_second(total, which):
        return [total[:, which * SECOND_WIDTH + a : which * SECOND_WIDTH + a + n] for a, n in zip(SECOND_AT, SECOND)]

    def put_first(at, sums):
        for which in range(2):
            k.sums[at, :, which * 512 : which * 512 + REDUCE] = sums[which]

    def get_first(total, which):
        return total[:, which * 512 : which * 512 + REDUCE]

    def second_params(k_of, at):
        row = k_of[at : at + 1, :]
        out, begin = [], REDUCE
        for width in SECOND:
            out.append(row[:, begin : begin + width])
            begin += width
        return out

    def first_params(k_of, at):
        return k_of[at : at + 1, 0:REDUCE]

    def forward(lay, at, count, cubes, before, first_idle, after_first, in_conv, second_idle):
        s = lay.s
        total, square, valid = reduce_conv(lay)
        before()
        put_first(at, (total, square))
        if count is None:
            k.sums[at, :, 1024:1152] = jnp.broadcast_to(valid, (1, 128))
        start_sum(at)
        start_halo(lay, s.border, 2 * lay.index)
        first_idle()
        end_halo(lay, s.border, 2 * lay.index, cols=False)
        for copy in cubes:
            copy.wait()
        summed = end_sum(at)
        if count is None:
            count = summed[:, 1024:1025]
        gain = first_params(k.gain, lay.index)
        first = batch_norm_scale(get_first(summed, 0), get_first(summed, 1), count, gain)
        first += (first_params(k.bias, lay.index), gain)
        after_first()
        thin = (first[0][:, B0:], first[2][:, B0:], first[3][:, B0:])
        narrow_center(lay, thin)

        def sides():
            end_halo(lay, s.border, 2 * lay.index, rows=False)
            narrow_sides(lay, thin)
            in_conv()

        cube_conv(lay, sides)
        put_second(at + 1, second_sums(lay))
        start_sum(at + 1)
        second_idle()
        summed = end_sum(at + 1)
        second = []
        for total, square, gain, bias in zip(
            get_second(summed, 0),
            get_second(summed, 1),
            second_params(k.gain, lay.index),
            second_params(k.bias, lay.index),
        ):
            second.append(batch_norm_scale(total, square, count, gain) + (bias, gain))
        return first, second, count

    def normalised(value, norm):
        average, inv_std, scale, bias, gain = norm
        return (value - average) * inv_std

    def affine(value, norm):
        average, inv_std, scale, bias, gain = norm
        return (value - average) * scale + bias

    def left_half(norm):
        return tuple(p[:, :B0] for p in norm)

    def outputs(lay, i, first, second):
        mask = center_mask(lay, i * lay.step, lay.step)
        z = lay.s.first[pl.ds(i * lay.step, lay.step)].reshape(lay.step * lay.row_cells, B0)
        parts = [softplus(affine(z, left_half(first))) * mask]
        parts += [softplus(affine(v, n)) * mask for v, n in zip(second_rows(lay, i), second)]
        return parts

    def put_normed(lay, second):
        def body(i, carry):
            inner = pl.ds(i * lay.step + 1, lay.step)
            for begin, width, v, n in zip(SECOND_AT, SECOND, second_rows(lay, i), second):
                normed = normalised(v, n).astype(BF16)
                normed = normed.reshape(lay.step, lay.cols, lay.frames, width)
                lay.s.normed[inner, 1 : lay.cols + 1, :, begin : begin + width] = normed
            return carry

        loop(lay.rows // lay.step, body, 0)

    for copy in flat_one:
        copy.wait()

    def wait_barrier():
        for copy in cubes_one + [slope_load] + flat_two + cubes_two:
            copy.start()
        beside = (w > 0).astype(jnp.int32) + (w < n_wa - 1).astype(jnp.int32)
        pl.semaphore_wait(barrier, chips + beside)

    def spread_two():
        slope_load.wait()
        for row in range(two.rows):
            k.slopes[pl.ds(row * two.row_cells, two.row_cells), :] = reorder(
                two, k.v_out_grad[:, row], True
            ).astype(BF16)
        for a, part, width in zip(SECOND_AT, slope_two(0)[1:], SECOND):
            part = part.reshape(two.rows, two.cols, two.frames, width).astype(BF16)
            k.grad_border[0, 1 : two.rows + 1, 1 : two.cols + 1, :, a : a + width] = part
        start_halo(two, k.grad_border.at[0], 4)

    def nothing():
        return None

    def split(value):
        a, b_, c, d = B0, B0 + B1, B0 + B1 + B2, B0 + B1 + B2 + BP
        return [value[:, :a], value[:, a:b_], value[:, b_:c], value[:, c:d]]

    def slope_two(i):
        return split(k.slopes[...].astype(F32))

    first_one, second_one, count_one = forward(
        one, 0, None, cubes_one, wait_barrier, nothing, nothing, spread_two, nothing
    )

    def halve(row, carry):
        begin = 0
        for p in outputs(one, row, first_one, second_one):
            width = p.shape[-1]
            both = p.reshape(2, two.cols, 2, one.frames, width)
            both = both[0, :, 0] + both[0, :, 1] + both[1, :, 0] + both[1, :, 1]
            for lane in range(0, width, 128):
                size = min(128, width - lane)
                k.pairs[:, begin + lane // 128, :, 0:size] = both[:, :, lane : lane + size]
            begin += -(-width // 128)
        for col in range(two.cols):
            tiles = []
            for lane in range(begin):
                even = k.pairs[col, lane, pl.ds(0, two.frames, stride=2), :]
                odd = k.pairs[col, lane, pl.ds(1, two.frames, stride=2), :]
                tiles.append((even + odd) * 0.125)
            half = (B0 + B1) // 128
            tiles[half] = tiles[half][:, : (B0 + B1) % 128]
            mean = jnp.concatenate(tiles, axis=1)
            two.s.block_in[row, col] = mean.astype(BF16)
        return carry

    put_normed(one, second_one)
    start_normed(*NORMED_AT[0])
    lax.fori_loop(0, two.rows, halve, 0)

    for copy in flat_two:
        copy.wait()

    def share_normed():
        start_normed(*NORMED_AT[1])

    def share_third():
        start_normed(*NORMED_AT[2])

    def share_rest():
        start_normed(*NORMED_AT[3])

    first_two, second_two, count_two = forward(
        two, 2, count_one * 0.125, cubes_two, nothing, share_normed, share_third, nothing, share_rest
    )

    def level(lay, begin, end):
        return softplus(k.bias[lay.index : lay.index + 1, begin:end]).astype(BF16).astype(F32)

    def center_windows(lay):
        mid, small = level(lay, B0, B0 + B1R), level(lay, B0 + B1R, REDUCE)
        mid, small = (jnp.concatenate([v] * 3, axis=1) for v in (mid, small))
        s, step = lay.s, lay.pad_step

        def body(i, carry):
            at = pl.ds(i * step, step)
            for ref, value in ((s.mid_in, mid), (s.small_in, small)):
                shape = (step,) + ref.shape[1:]
                part = ref[at].reshape(-1, shape[-1]).astype(F32) - value
                ref[at] = part.astype(BF16).reshape(shape)
            return carry

        loop((lay.rows + 2) // step, body, 0)

    def centered_block(lay):
        if lay.index == 0:
            return flat_block(lay)
        value = jnp.concatenate([level(one, 0, B0), level(one, REDUCE, k.bias.shape[1])], axis=1)
        return (flat_block(lay).astype(F32) - value).astype(BF16)

    def backward(lay, out_slope, border_slope, at, first, second, count, before_end, after_end, before_low):
        s, index, step = lay.s, lay.index, lay.step
        chunks = lay.rows // step
        per_cell = 1.0 / count

        def second_slope(i):
            mask = center_mask(lay, i * step, step)
            values = second_rows(lay, i)
            normed = [normalised(v, n) for v, n in zip(values, second)]
            slopes = [
                g * mask * sigmoid(m * n[4] + n[3])
                for g, m, n in zip(out_slope(i)[1:], normed, second)
            ]
            return mask, normed, slopes

        def sum_body(i, sums):
            mask, normed, slopes = second_slope(i)
            return tuple(
                (t + column_sum(g), q + column_sum(g * m))
                for (t, q), g, m in zip(sums, slopes, normed)
            )

        zero = tuple((jnp.zeros((1, n), F32),) * 2 for n in SECOND)
        put_second(at, loop(chunks, sum_body, zero))
        start_sum(at)
        before_end()
        center_windows(lay)
        progress(index, 0)
        summed = end_sum(at)
        after_end()
        totals = list(zip(get_second(summed, 0), get_second(summed, 1)))
        begin = REDUCE
        for (bias_grad, gain_grad), width in zip(totals, SECOND):
            k.bias_grad[index : index + 1, begin : begin + width] = bias_grad
            k.gain_grad[index : index + 1, begin : begin + width] = gain_grad
            begin += width
        totals = [(t * per_cell, q * per_cell) for t, q in totals]

        def pre_slope(g, m, norm, total):
            return norm[2] * (g - (total[0] + m * total[1]))

        def center_body(i, carry):
            mask, normed, slopes = second_slope(i)
            inner = pl.ds(i * step + 1, step)
            for a, width, g, m, n, total in zip(SECOND_AT, SECOND, slopes, normed, second, totals):
                value = (pre_slope(g, m, n, total) * mask).astype(BF16)
                s.normed[inner, 1 : lay.cols + 1, :, a : a + width] = value.reshape(
                    step, lay.cols, lay.frames, width
                )
            return carry

        loop(chunks, center_body, 0)

        def border_cells(where, slopes):
            mask = s.mask[where]
            cells = mask.shape[0]
            mask = mask.reshape(cells * lay.frames, 1)
            normed = s.normed[where].astype(F32).reshape(cells * lay.frames, SECOND_WIDTH)
            for a, width, g, n, total in zip(SECOND_AT, SECOND, slopes, second, totals):
                m = normed[:, a : a + width]
                g = g * sigmoid(m * n[4] + n[3])
                value = jnp.where(mask > 0.0, pre_slope(g, m, n, total), 0.0).astype(BF16)
                s.normed[where + (slice(None), slice(a, a + width))] = value.reshape(
                    cells, lay.frames, width
                )

        border_cells((jnp.where(h == 0, lay.rows + 1, 0), slice(None)), border_slope(True, None))
        for col in (0, lay.cols + 1):
            border_cells((slice(1, lay.rows + 1), col), border_slope(False, col > 0))

        progress(index, 1)

        center = s.normed[1 : lay.rows + 1, 1 : lay.cols + 1].reshape(lay.cells, SECOND_WIDTH)
        turned_mid = center[:, 0:B1].T
        turned_small = center[:, 384:512].T

        def tap_body(tap, carry):
            row, col = tap_at(tap)
            mid = dot(turned_mid, window(lay, s.mid_in, row, col, 3 * B1R)).astype(BF16)
            small = dot(turned_small, window(lay, s.small_in, row, col, 3 * B2R)).astype(BF16)
            store_blocks(index, tap * TAP_BLOCKS, mid)
            store_blocks(index, tap * TAP_BLOCKS + 80, small)
            return carry

        taps(lay, tap_body, 5, 0, EARLY_TAPS[index])

        s.mid[...] = jnp.zeros(s.mid.shape, F32)
        s.small[:, 0 : 3 * B2R] = jnp.zeros((lay.cells, 3 * B2R), F32)

        def back_body(tap, carry):
            row, col = tap_at(tap)
            slope = window(lay, s.normed, 2 - row, 2 - col, SECOND_WIDTH)
            s.mid[...] += dot(slope[:, 0:B1], k.v_w_mid[index, tap], NT)
            s.small[:, 0 : 3 * B2R] += dot(slope[:, 384:512], k.v_w_small[index, tap], NT)
            return carry

        taps(lay, back_body, 2)

        def box_body(i, carry):
            at = pl.ds(i * lay.pad_step, lay.pad_step)
            s.box[at] = box_row(lay, s.normed[at, :, :, 512:640].astype(F32))
            return carry

        loop((lay.rows + 2) // lay.pad_step, box_body, 0)
        progress(index, 3)

        def first_normed(i):
            size = step * lay.row_cells
            z = s.first[pl.ds(i * step, step)].reshape(size, B0)
            z_thin = s.narrow[pl.ds(i * step + 1, step), 1 : lay.cols + 1].reshape(size, NARROW)
            return normalised(jnp.concatenate([z, z_thin], axis=1), first)

        def first_body(i, sums):
            cells = cells_of(lay, i)
            s.projected_slope[cells, :] = box_rows(lay, i * step).astype(BF16)
            mid = s.mid[cells, :]
            small = s.small[cells, 0 : 3 * B2R]
            thirds = [
                jnp.concatenate(
                    [mid[:, B1R * t : B1R * (t + 1)], small[:, B2R * t : B2R * (t + 1)]], axis=1
                )
                for t in range(3)
            ]
            thin = thirds[1] + shifted(lay, thirds[2])[0] + shifted(lay, thirds[0])[1]
            mask = center_mask(lay, i * step, step)
            normed = first_normed(i)
            g = jnp.concatenate([out_slope(i)[0], thin], axis=1)
            g = g * mask * sigmoid(normed * first[4] + first[3])
            s.mid[cells, 0:REDUCE] = g
            return sums[0] + column_sum(g), sums[1] + column_sum(g * normed)

        zero = (jnp.zeros((1, REDUCE), F32),) * 2
        put_first(at + 1, loop(chunks, first_body, zero))
        start_sum(at + 1)

        progress(index, 4)

        taps(lay, tap_body, 5, EARLY_TAPS[index])
        store_blocks(index, LOW_AT + 196, dot(s.projected_slope[...].T, flat_block(lay)).astype(BF16))
        progress(index, 6)
        summed = end_sum(at + 1)
        total = (get_first(summed, 0), get_first(summed, 1))
        k.bias_grad[index : index + 1, 0:REDUCE] = total[0]
        k.gain_grad[index : index + 1, 0:REDUCE] = total[1]

        total = (total[0] * per_cell, total[1] * per_cell)

        def low_body(i, carry):
            cells = cells_of(lay, i)
            mask = center_mask(lay, i * step, step)
            value = pre_slope(s.mid[cells, 0:REDUCE], first_normed(i), first, total) * mask
            s.low[cells, :] = value.astype(BF16)
            return carry

        loop(chunks, low_body, 0)
        before_low()
        progress(index, 7)
        store_blocks(index, LOW_AT, dot(s.low[...].T, centered_block(lay)).astype(BF16))
        progress(index, 8)

    def widen(ref, begin, value):
        width = value.shape[-1]
        for lane in range(0, width, 128):
            size = min(128, width - lane)
            for odd in range(2):
                ref[(begin + lane) // 128, pl.ds(odd, two.frames, stride=2), 0:size] = value[
                    :, lane : lane + size
                ]

    def wide(value, a, width):
        tiles = [value[..., lane // 128, :, :] for lane in range(a, a + width, 128)]
        return jnp.concatenate(tiles, axis=-1)[..., :width]

    def put_two(i, slope):
        slope = slope * 0.125
        for a, part in zip((0,) + tuple(B0 + a for a in SECOND_AT), split(slope)):
            width = part.shape[-1]
            part = part.reshape(two.rows, two.cols, two.frames, width)
            for row in range(two.rows):
                for col in range(two.cols):
                    widen(k.spread.at[row, col], a, part[row, col])
            if a >= B0:
                inner = (slice(1, two.rows + 1), slice(1, two.cols + 1), slice(None))
                k.grad_border[(1,) + inner + (slice(a - B0, a - B0 + width),)] = part.astype(BF16)

    def input_slope(lay, low, projected):
        slope = dot(low, k.v_w_reduce[lay.index])
        return slope + dot(projected, k.v_w_pool[lay.index], NT)

    def low_two():
        mask = center_mask(two, 0, two.rows)
        put_two(0, input_slope(two, two.s.low[...], two.s.projected_slope[...]) * mask)

    def side(lay, across, last):
        if across:
            return (jnp.where(h == 0, lay.rows + 1, 0), slice(None))
        return (slice(1, lay.rows + 1), lay.cols + 1 if last else 0)

    def border_two(across, last):
        value = k.grad_border[(0,) + side(two, across, last)].astype(F32)
        value = value.reshape(value.shape[0] * two.frames, SECOND_WIDTH)
        return [value[:, a : a + n] for a, n in zip(SECOND_AT, SECOND)]

    def end_two():
        put_normed(two, second_two)
        start_halo(two, two.s.normed, 3)
        value = jnp.concatenate(outputs(two, 0, first_two, second_two), axis=1).astype(BF16)
        for row in range(two.rows):
            part = reorder(two, value[row * two.row_cells : (row + 1) * two.row_cells], False)
            k.block_output[:, row] = part.reshape(two.frames, two.cols, -1).astype(BF16)
        end_halo(two, two.s.normed, 3)
        end_halo(two, k.grad_border.at[0], 4)

    def after_two():
        start_normed(*NORMED_AT[4])

    backward(two, slope_two, border_two, 4, first_two, second_two, count_two, end_two, after_two, low_two)
    start_halo(two, k.grad_border.at[1], 5)

    def slope_one(i):
        value = k.spread[i]
        out = []
        for a, width in zip((0,) + tuple(B0 + a for a in SECOND_AT), (B0,) + SECOND):
            part = wide(value, a, width)
            pieces = [part[col // 2] for col in range(one.cols)]
            out.append(jnp.concatenate(pieces * one.step, axis=0))
        return out

    def border_one(across, last):
        where = side(two, across, last)
        value = k.border_spread[where] if across else k.border_spread[:, where[1]]
        cells = range(one.cols + 2) if across else range(1, one.rows + 1)
        out = []
        for a, n in zip(SECOND_AT, SECOND):
            part = wide(value, a, n)
            out.append(jnp.concatenate([part[(cell + 1) // 2] for cell in cells], axis=0))
        return out

    def end_one():
        end_normed()
        end_halo(two, k.grad_border.at[1], 5)
        places = [(side(two, True, None)[0], col) for col in range(two.cols + 2)]
        places += [(row, col) for row in range(1, two.rows + 1) for col in (0, two.cols + 1)]
        for row, col in places:
            widen(k.border_spread.at[row, col], 0, k.grad_border[1, row, col].astype(F32))

    backward(one, slope_one, border_one, 6, first_one, second_one, count_one, end_one, nothing, nothing)

    def input_row(row, carry):
        cells = pl.ds(pl.multiple_of(row * one.row_cells, one.row_cells), one.row_cells)
        low = reorder(one, one.s.low[cells, :], False).astype(BF16)
        projected = one.s.projected_slope[cells, :].astype(F32) * center_mask(one, row)
        projected = reorder(one, projected.astype(BF16), False).astype(BF16)
        slope = input_slope(one, low, projected)
        k.input_grad[:, row] = slope.reshape(one.frames, one.cols, -1).astype(BF16)
        return carry

    lax.fori_loop(0, one.rows, input_row, 0)
    for step in plan[None]:
        step()


UNPACK_TAPS = 3


def unpack_body(taps, low, gain, bias, mid_out, small_out, reduce_out, pool_out, gain_out, bias_out):
    def lanes(blocks, tiles, rows, width):
        parts = []
        for tile in range(tiles):
            size = min(128, width - 128 * tile)
            part = blocks[tile * (rows // 16) : (tile + 1) * (rows // 16), :, 0:size]
            parts.append(part.reshape(rows, size))
        return jnp.concatenate(parts, axis=1)

    def tap_body(tap, carry):
        blocks = taps.at[0, pl.ds(tap * TAP_BLOCKS, TAP_BLOCKS)]
        mid = lanes(blocks, 4, B1, 3 * B1R).T.astype(F32)
        small = lanes(blocks.at[80:88], 1, B2, 3 * B2R).T.astype(F32)
        for t in range(3):
            mid_out[0, t, tap] = mid[B1R * t : B1R * (t + 1)]
            small_out[0, t, tap] = small[B2R * t : B2R * (t + 1)]
        return carry

    lax.fori_loop(0, UNPACK_TAPS, tap_body, 0)

    @pl.when(pl.program_id(1) == 0)
    def _():
        channels = reduce_out.shape[-1]
        tiles = -(-channels // 128)
        reduce_out[0] = lanes(low.at[0, 0:196], tiles, REDUCE, channels).astype(F32)
        pool_out[0] = lanes(low.at[0, 196:252], tiles, BP, channels).T.astype(F32)
        gain_out[...] = gain[...]
        bias_out[...] = bias[...]


def unpack(grads, gain, bias, channels):
    n = UNPACK_TAPS
    shapes = ((2, 3, 9, B1R, B1), (2, 3, 9, B2R, B2), (2, REDUCE, channels), (2, channels, BP))
    shapes += (gain.shape, bias.shape)
    norms = [pl.BlockSpec(gain.shape, lambda i, j: (0, 0))] * 2
    mid_grad, small_grad, reduce_grad, pool_grad, gain, bias = pl.pallas_call(
        unpack_body,
        grid=(2, 9 // n),
        out_shape=[jax.ShapeDtypeStruct(shape, F32) for shape in shapes],
        in_specs=[
            pl.BlockSpec((1, n * TAP_BLOCKS, 16, 128), lambda i, j: (i, j, 0, 0)),
            pl.BlockSpec((1, 256, 16, 128), lambda i, j: (i, LOW_OUT // 256, 0, 0)),
        ]
        + norms,
        out_specs=[
            pl.BlockSpec((1, 3, n, B1R, B1), lambda i, j: (i, 0, j, 0, 0)),
            pl.BlockSpec((1, 3, n, B2R, B2), lambda i, j: (i, 0, j, 0, 0)),
            pl.BlockSpec((1, REDUCE, channels), lambda i, j: (i, 0, 0)),
            pl.BlockSpec((1, channels, BP), lambda i, j: (i, 0, 0)),
        ]
        + norms,
        compiler_params=pltpu.CompilerParams(vmem_limit_bytes=60 * 1024 * 1024),
        name="unpack",
    )(grads, grads, gain, bias)
    return (
        jnp.swapaxes(reduce_grad, 1, 2),
        mid_grad.reshape(2, 27, B1R, B1),
        small_grad.reshape(2, 27, B2R, B2),
        pool_grad,
        gain,
        bias,
    )


def on_device(
    n_batch, n_wa, clip_features, frame_counts, w_reduce, w_mid, w_small, w_pool, norm_gain, norm_bias, out_grad
):
    frames, rows, cols, channels = clip_features.shape
    clips = frame_counts.shape[0]
    slot = frames // clips
    layers = (
        Layer(0, rows, cols, clips, slot),
        Layer(1, rows // 2, cols // 2, clips, slot // 2),
    )
    one, two = layers
    chips = n_batch * n_wa

    operands = dict(
        features=clip_features,
        frame_counts=frame_counts,
        w_reduce=jnp.swapaxes(w_reduce, 1, 2),
        w_mid=w_mid.reshape(2, 3, 9, B1R, B1),
        w_small=w_small.reshape(2, 3, 9, B2R, B2),
        w_pool=w_pool,
        gain=norm_gain,
        bias=norm_bias,
        out_grad=out_grad,
    )
    in_space = dict(frame_counts=pltpu.SMEM, gain=pltpu.VMEM, bias=pltpu.VMEM)
    out_space = dict(weight_grads=pl.ANY)
    results = dict(
        block_output=jax.ShapeDtypeStruct(out_grad.shape, BF16),
        input_grad=jax.ShapeDtypeStruct(clip_features.shape, BF16),
        weight_grads=jax.ShapeDtypeStruct((2, LOW_OUT + 256, 16, 128), BF16),
        gain_grad=jax.ShapeDtypeStruct(norm_gain.shape, F32),
        bias_grad=jax.ShapeDtypeStruct(norm_bias.shape, F32),
    )
    scratch = {}
    for name in ("w_reduce", "w_pool", "out_grad"):
        scratch["v_" + name] = pltpu.VMEM(operands[name].shape, BF16)
    scratch.update(
        v_w_mid=pltpu.VMEM((2, 9, 3 * B1R, B1), BF16),
        v_w_small=pltpu.VMEM((2, 9, 3 * B2R, B2), BF16),
    )
    small_pad = (two.rows + 2, two.cols + 2)
    scratch.update(
        slopes=pltpu.VMEM((two.cells, channels), BF16),
        pairs=pltpu.VMEM((two.cols, (B0 + SECOND_WIDTH) // 128, one.frames, 128), F32),
        spread=pltpu.VMEM(
            (two.rows, two.cols, (B0 + SECOND_WIDTH) // 128, one.frames, 128), F32
        ),
        border_spread=pltpu.VMEM(small_pad + (SECOND_WIDTH // 128, one.frames, 128), F32),
        grad_border=pltpu.VMEM((2,) + small_pad + (two.frames, SECOND_WIDTH), BF16),
        sums=pltpu.VMEM((8, 1, SUM_WIDTH), F32),
        pair_sums=pltpu.VMEM((8, 1, SUM_WIDTH), F32),
        chip_sums=pltpu.VMEM((2, chips, 1, SUM_WIDTH), F32),
        load_sem=pltpu.SemaphoreType.DMA((17,)),
        feature_sem=pltpu.SemaphoreType.DMA((one.rows // one.step,)),
        pair_sem=pltpu.SemaphoreType.DMA((2, 8)),
        chip_sem=pltpu.SemaphoreType.DMA((2, 8)),
        normed_sem=pltpu.SemaphoreType.DMA((2, 4, 3)),
        halo_sem=pltpu.SemaphoreType.DMA((2, 6, 5)),
        grads=pltpu.VMEM((2, GRAD_BLOCKS, 16, 128), BF16),
        got_half=pltpu.VMEM((2, GRAD_BLOCKS // 2, 16, 128), BF16),
        got_eighth=pltpu.VMEM((2, GRAD_BLOCKS // 4, 16, 128), BF16),
        got_piece=pltpu.VMEM((2, GRAD_BLOCKS // 8, 16, 128), BF16),
        got_chunk=pltpu.VMEM((2, n_batch, GRAD_BLOCKS // 32, 16, 128), BF16),
        got_total=pltpu.VMEM((2, OWNERS, GRAD_BLOCKS // 32, 16, 128), BF16),
        free_sem=pltpu.SemaphoreType.REGULAR((2, 3, 3)),
        grad_sem=pltpu.SemaphoreType.DMA((2, 2, 3, 18)),
        out_sem=pltpu.SemaphoreType.DMA((2, 3)),
    )
    names = list(operands) + list(results) + list(scratch)
    layer_scratch = [lay.scratch(channels) for lay in layers]

    def body(*refs):
        rest = refs[len(names) :]
        for lay, parts in zip(layers, layer_scratch):
            lay.s = SimpleNamespace(**dict(zip(parts, rest[: len(parts)])))
            rest = rest[len(parts) :]
        kernel_body(names, (n_batch, n_wa, layers), refs[: len(names)])

    out = pl.pallas_call(
        body,
        out_shape=list(results.values()),
        in_specs=[pl.BlockSpec(memory_space=in_space.get(name, pl.ANY)) for name in operands],
        out_specs=[pl.BlockSpec(memory_space=out_space.get(name, pltpu.VMEM)) for name in results],
        scratch_shapes=list(scratch.values()) + [r for parts in layer_scratch for r in parts.values()],
        compiler_params=pltpu.CompilerParams(
            collective_id=0, has_side_effects=True, vmem_limit_bytes=63 * 1024 * 1024
        ),
        name="layers",
    )(*operands.values())
    out = dict(zip(results, out))

    kernels_and_norms = unpack(out["weight_grads"], out["gain_grad"], out["bias_grad"], channels)

    return (
        out["block_output"],
        out["input_grad"],
        *kernels_and_norms,
    )


def solution(mesh):
    in_specs = (
        P("batch", "ha", "wa", None),
        P("batch"),
        P(),
        P(),
        P(),
        P(),
        P(),
        P(),
        P("batch", "ha", "wa", None),
    )
    out_specs = (
        P("batch", "ha", "wa", None),
        P("batch", "ha", "wa", None),
        P(),
        P(),
        P(),
        P(),
        P(),
        P(),
    )
    return jax.shard_map(
        functools.partial(on_device, mesh.shape["batch"], mesh.shape["wa"]),
        mesh=mesh,
        in_specs=in_specs,
        out_specs=out_specs,
        check_vma=False,
    )
```

```python
import functools
from types import SimpleNamespace

import jax
import jax.numpy as jnp
from jax import lax
from jax.experimental import pallas as pl
from jax.experimental.pallas import tpu as pltpu
from jax.sharding import PartitionSpec as P

HEIGHT = 14
EPSILON = 1e-05
MESH = pl.DeviceIdType.MESH
F32 = jnp.float32
BF16 = jnp.bfloat16

B0, B1R, B2R, B1, B2, BP = 256, 160, 32, 320, 128, 128
NARROW = B1R + B2R
REDUCE = B0 + NARROW
SECOND = (B1, B2, BP)
SECOND_AT = (0, 384, 512)
SECOND_WIDTH = 640
SUM_WIDTH = 1280
AXES = ("batch", "ha", "wa")

TAP_BLOCKS = 88
LOW_AT = 800
LOW_OUT = 1024
GRAD_BLOCKS = 1056
BUNDLES = ((0, 352), (352, 448), (800, 256))
OWNERS = 4

SCHEDULE = {
    (1, (5, 3)): ((1, 0),),
    (1, (5, 8)): ((1, 1),),
    (1, 6): ((1, 0),),
    (1, 8): ((1, 2),),
    (0, 0): ((1, 2), (1, 0),),
    (0, 1): ((1, 0), (1, 2),),
    (0, (5, 0)): ((1, 1),),
    (0, (5, 3)): ((0, 0),),
    (0, (5, 5)): ((1, 2),),
    (0, (5, 6)): ((0, 0),),
    (0, (5, 7)): ((1, 0),),
    (0, (5, 8)): ((0, 1),),
    (0, (2, 0)): ((1, 1),),
    (0, (2, 4)): ((1, 2), (0, 0),),
    (0, (2, 5)): ((0, 1), (1, 1),),
    (0, (2, 8)): ((1, 0), (0, 0),),
    (0, 3): ((1, 2),),
    (0, 6): ((0, 1), (1, 1), (1, 0),),
    (0, 7): ((1, 2),),
    (0, 8): ((0, 2), (0, 1), (0, 0),),
}
EARLY_TAPS = (9, 0)
LAST_STEPS = (
    (1, 0),
    (0, 2),
    (1, 1),
    (1, 2),
    (1, 0),
    (1, 0),
    (0, 1),
    (0, 2),
    (1, 2),
    (1, 1),
    (1, 2),
    (0, 2),
    (0, 1),
    (0, 2),
    (0, 0),
    (0, 1),
    (0, 2),
    (0, 0),
    (1, 1),
    (0, 1),
    (1, 1),
    (0, 2),
    (1, 1),
    (0, 1),
    (0, 1),
    (0, 0),
    (0, 2),
    (0, 0),
    (0, 2),
    (0, 0),
    (0, 2),
)

NORMED_AT = ((0,), (1,), (2,), (3,), ())

NN = (((1,), (0,)), ((), ()))
NT = (((1,), (1,)), ((), ()))


def dot(a, b, dims=NN):
    return lax.dot_general(a, b, dims, preferred_element_type=F32)


def softplus(x):
    return jnp.maximum(x, 0.0) + jnp.log(1.0 + jnp.exp(-jnp.abs(x)))


def sigmoid(x):
    return 1.0 / (1.0 + jnp.exp(-x))


def loop(count, body, init):
    return body(0, init) if count == 1 else lax.fori_loop(0, count, body, init)


class Layer:
    def __init__(self, index, rows, cols, clips, slot):
        self.index, self.rows, self.cols = index, rows, cols
        self.clips, self.slot = clips, slot
        self.frames = clips * slot
        self.cells = rows * cols * self.frames
        self.row_cells = cols * self.frames
        self.step = rows if index else 2
        self.pad_step = rows + 2 if index else 2

    def scratch(self, channels):
        r, c, t, n = self.rows, self.cols, self.frames, self.cells
        pad = (r + 2, c + 2, t)
        return dict(
            mask=pltpu.VMEM(pad + (1,), F32),
            block_in=pltpu.VMEM((r, c, t, channels), BF16),
            first=pltpu.VMEM((r, c, t, B0), F32),
            narrow=pltpu.VMEM(pad + (NARROW,), F32),
            border=pltpu.VMEM(pad + (BP + NARROW,), BF16),
            mid_in=pltpu.VMEM(pad + (3 * B1R,), BF16),
            small_in=pltpu.VMEM(pad + (3 * B2R,), BF16),
            box=pltpu.VMEM((r + 2, c, t, BP), F32),
            mid=pltpu.VMEM((n, 3 * B1R), F32),
            small=pltpu.VMEM((n, B2), F32),
            pool=pltpu.VMEM((n, BP), F32),
            normed=pltpu.VMEM(pad + (SECOND_WIDTH,), BF16),
            projected_slope=pltpu.VMEM((n, BP), BF16),
            low=pltpu.VMEM((n, REDUCE), BF16),
        )


def batch_norm_scale(total, square, count, gain):
    average = total / count
    variance = square / count - average * average
    inv_std = lax.rsqrt(variance + EPSILON)
    return average, inv_std, inv_std * gain


def kernel_body(names, sizes, refs):
    k = SimpleNamespace(**dict(zip(names, refs)))
    n_batch, n_wa, layers = sizes
    b, h, w = (lax.axis_index(a) for a in AXES)
    chips = n_batch * n_wa
    my_chip = b * n_wa + w
    one, two = layers

    def chip_at(p):
        return lax.div(p, n_wa), h, lax.rem(p, n_wa)

    def rotated(i):
        return lax.rem(my_chip + i, chips)

    def load(at, source, target):
        return pltpu.make_async_copy(source, target, k.load_sem.at[at])

    output_store = pltpu.make_async_copy(k.v_block_output, k.block_output, k.result_sem.at[0])
    input_store = pltpu.make_async_copy(k.v_input_grad, k.input_grad, k.result_sem.at[1])

    def load_features(i):
        rows = pl.ds(i * one.step, one.step)
        return pltpu.make_async_copy(
            k.features.at[:, rows], k.v_input_grad.at[:, rows], k.feature_sem.at[i]
        )

    def load_cubes(at, layer):
        copies = []
        for t in range(3):
            mid, small = pl.ds(B1R * t, B1R), pl.ds(B2R * t, B2R)
            copies.append(load(at + 2 * t, k.w_mid.at[layer, t], k.v_w_mid.at[layer, :, mid]))
            copies.append(load(at + 2 * t + 1, k.w_small.at[layer, t], k.v_w_small.at[layer, :, small]))
        return copies

    def load_flat(at, layer):
        return [
            load(at, k.w_reduce.at[layer], k.v_w_reduce.at[layer]),
            load(at + 1, k.w_pool.at[layer], k.v_w_pool.at[layer]),
        ]

    flat_one, flat_two = load_flat(0, 0), load_flat(2, 1)
    cubes_one, cubes_two = load_cubes(4, 0), load_cubes(10, 1)
    slope_load = load(16, k.out_grad, k.v_out_grad)
    for copy in flat_one:
        copy.start()
    for i in range(one.rows // one.step):
        load_features(i).start()
    for lay in layers:
        s = lay.s
        for ref in (s.border, s.normed):
            for row in (0, lay.rows + 1):
                ref[row] = jnp.zeros(ref.shape[1:], ref.dtype)
            for col in (0, lay.cols + 1):
                ref[:, col] = jnp.zeros((ref.shape[0],) + ref.shape[2:], ref.dtype)
    ref = k.grad_border
    ref[...] = jnp.zeros(ref.shape, ref.dtype)
    for layer in range(2):
        for begin, end in ((9 * TAP_BLOCKS, LOW_AT), (LOW_AT + 252, GRAD_BLOCKS)):
            k.grads[layer, begin:end] = jnp.zeros((end - begin, 16, 128), BF16)
    k.sums[...] = jnp.zeros(k.sums.shape, F32)

    barrier = pltpu.get_barrier_semaphore()
    pl.semaphore_signal(barrier, inc=1, device_id=(b, 1 - h, w), device_id_type=MESH)

    @pl.when(w > 0)
    def _():
        pl.semaphore_signal(barrier, inc=1, device_id=(b, 1 - h, w - 1), device_id_type=MESH)

    @pl.when(w < n_wa - 1)
    def _():
        pl.semaphore_signal(barrier, inc=1, device_id=(b, 1 - h, w + 1), device_id_type=MESH)

    def greet(i, carry):
        pl.semaphore_signal(barrier, inc=1, device_id=chip_at(rotated(i)), device_id_type=MESH)
        return carry

    lax.fori_loop(1, chips, greet, 0)

    for lay in layers:
        frame_at = lax.broadcasted_iota(jnp.int32, (lay.frames, 1), 0)
        inside = jnp.zeros((lay.frames, 1), F32)
        for clip in range(lay.clips):
            valid = k.frame_counts[clip]
            valid = valid if lay.index == 0 else lax.div(valid, 2)
            begin = clip * lay.slot
            inside = jnp.where((frame_at >= begin) & (frame_at < begin + valid), 1.0, inside)
        height = HEIGHT if lay.index == 0 else HEIGHT // 2
        for row in range(lay.rows + 2):
            at_row = h * lay.rows + row - 1
            for col in range(lay.cols + 2):
                at_col = w * lay.cols + col - 1
                good = (at_row >= 0) & (at_row < height) & (at_col >= 0) & (at_col < height)
                lay.s.mask[row, col] = inside * good.astype(F32)

    def start_sum(at):
        pair = pltpu.make_async_remote_copy(
            src_ref=k.sums.at[at],
            dst_ref=k.pair_sums.at[at],
            send_sem=k.pair_sem.at[0, at],
            recv_sem=k.pair_sem.at[1, at],
            device_id=(b, 1 - h, w),
            device_id_type=MESH,
        )
        pair.start()
        pair.wait_recv()
        k.chip_sums[at % 2, my_chip] = k.sums[at] + k.pair_sums[at]

        def send(i, carry):
            pltpu.make_async_remote_copy(
                src_ref=k.chip_sums.at[at % 2, my_chip],
                dst_ref=k.chip_sums.at[at % 2, my_chip],
                send_sem=k.chip_sem.at[0, at],
                recv_sem=k.chip_sem.at[1, at],
                device_id=chip_at(rotated(i)),
                device_id_type=MESH,
            ).start()
            return carry

        if chips <= 16:
            for i in range(1, chips):
                send(i, 0)
        else:
            lax.fori_loop(1, chips, send, 0)
        pair.wait_send()

    def end_sum(at):
        for way in (1, 0):
            others = k.chip_sums.at[at % 2, pl.ds(0, chips - 1)]
            pltpu.make_async_copy(others, others, k.chip_sem.at[way, at]).wait()
        total = k.chip_sums[at % 2, 0]
        for p in range(1, chips):
            total = total + k.chip_sums[at % 2, p]
        return total

    def halo_copies(lay, ref, at):
        src_row = jnp.where(h == 0, lay.rows, 1)
        dst_row = jnp.where(h == 0, 0, lay.rows + 1)
        rows, cols = lay.rows, lay.cols

        def remote(src, dst, way, device):
            return lambda: pltpu.make_async_remote_copy(
                src_ref=ref.at[src],
                dst_ref=ref.at[dst],
                send_sem=k.halo_sem.at[0, at, way],
                recv_sem=k.halo_sem.at[1, at, way],
                device_id=device,
                device_id_type=MESH,
            )

        all_rows, all_cols = pl.ds(1, rows), pl.ds(1, cols)
        row = remote((src_row, all_cols), (dst_row, all_cols), 0, (b, 1 - h, w))
        to_left = [
            remote((all_rows, 1), (all_rows, cols + 1), 1, (b, h, w - 1)),
            remote((src_row, 1), (dst_row, cols + 1), 2, (b, 1 - h, w - 1)),
        ]
        to_right = [
            remote((all_rows, cols), (all_rows, 0), 3, (b, h, w + 1)),
            remote((src_row, cols), (dst_row, 0), 4, (b, 1 - h, w + 1)),
        ]
        return row, to_left, to_right

    def normed_copies():
        ref, rows, cols = one.s.normed, one.rows, one.cols
        half = rows // 2
        src_row = jnp.where(h == 0, rows, 1)
        dst_row = jnp.where(h == 0, 0, rows + 1)

        def remote(part, slot, src, dst, device):
            return lambda: pltpu.make_async_remote_copy(
                src_ref=ref.at[src],
                dst_ref=ref.at[dst],
                send_sem=k.normed_sem.at[0, part, slot],
                recv_sem=k.normed_sem.at[1, part, slot],
                device_id=device,
                device_id_type=MESH,
            )

        parts = []
        for part in range(4):
            left, low = part < 2, part % 2 == 0
            src, dst = (1, cols + 1) if left else (cols, 0)
            way = w - 1 if left else w + 1
            run = pl.ds(1 if low else 1 + half, half)
            copies = [remote(part, 0, (run, src), (run, dst), (b, h, way))]
            if not low:
                copies.append(remote(part, 1, (src_row, src), (dst_row, dst), (b, 1 - h, way)))
            parts.append((w > 0 if left else w < n_wa - 1, w < n_wa - 1 if left else w > 0, copies))
        inner = pl.ds(1, cols)
        row = remote(1, 2, (src_row, inner), (dst_row, inner), (b, 1 - h, w))
        return row, parts

    def start_normed(*which):
        row, parts = normed_copies()
        if 1 in which:
            row().start()
        for part in which:
            sends, _, copies = parts[part]

            @pl.when(sends)
            def _(copies=copies):
                for copy in copies:
                    copy().start()

    def end_normed():
        row, parts = normed_copies()
        row().wait()
        for sends, receives, copies in parts:

            @pl.when(sends)
            def _(copies=copies):
                for copy in copies:
                    copy().wait_send()

            @pl.when(receives)
            def _(copies=copies):
                for copy in copies:
                    copy().wait_recv()

    def start_halo(lay, ref, at, first=True, last=True):
        row, to_left, to_right = halo_copies(lay, ref, at)
        if first:
            row().start()

            @pl.when(w > 0)
            def _():
                for copy in to_left:
                    copy().start()

        if last:

            @pl.when(w < n_wa - 1)
            def _():
                for copy in to_right:
                    copy().start()

    def end_halo(lay, ref, at, rows=True, cols=True):
        row, to_left, to_right = halo_copies(lay, ref, at)
        if rows:
            row().wait()
        if not cols:
            return

        @pl.when(w > 0)
        def _():
            for copy in to_left:
                copy().wait_send()
            for copy in to_right:
                copy().wait_recv()

        @pl.when(w < n_wa - 1)
        def _():
            for copy in to_right:
                copy().wait_send()
            for copy in to_left:
                copy().wait_recv()

    def exchange(layer, number):
        begin, count = BUNDLES[number]
        half, quarter, eighth = count // 2, count // 4, count // 8
        piece, chunk = count // 16, count // 32
        stride = n_batch // OWNERS
        g = k.grads.at[layer]
        r1, r2, r3, r4, r5 = (
            r.at[layer] for r in (k.got_half, k.got_eighth, k.got_piece, k.got_chunk, k.got_total)
        )
        to_half, to_eighth, to_piece, to_chunk = begin // 2, begin // 4, begin // 8, begin // 32

        def places():
            b, h, w = (lax.axis_index(a) for a in AXES)
            x, y = lax.rem(w, 2), lax.div(w, 2)
            at = SimpleNamespace(b=b, h=h, w=w)
            at.pair, at.beside, at.below = (b, 1 - h, w), (b, h, w + 1 - 2 * x), (b, h, w + 2 - 4 * y)
            at.mine, at.other = begin + h * half, begin + (1 - h) * half
            half_a, half_b = at.mine, at.mine + quarter
            at.eighth_a, at.eighth_b = half_a + x * eighth, half_b + y * eighth
            at.a, at.b_ = at.eighth_a + y * piece, at.eighth_b + x * piece
            at.sent_a, at.sent_b = half_a + (1 - x) * eighth, half_b + (1 - y) * eighth
            at.last_a, at.last_b = at.eighth_a + (1 - y) * piece, at.eighth_b + (1 - x) * piece
            at.rank = lax.div(b, stride)
            at.chunk = jnp.where(at.rank < 2, at.a, at.b_) + lax.rem(at.rank, 2) * chunk
            at.chunks = [(at.a, at.b_)[owner // 2] + owner % 2 * chunk for owner in range(OWNERS)]
            return at

        def copy(source, at, target, to, size, slot, device):
            return pltpu.make_async_remote_copy(
                src_ref=source.at[pl.ds(at, size)],
                dst_ref=target.at[pl.ds(to, size)],
                send_sem=k.grad_sem.at[0, layer, number, slot],
                recv_sem=k.grad_sem.at[1, layer, number, slot],
                device_id=device,
                device_id_type=MESH,
            )

        def pair_copies(at):
            return [copy(g, at.other, r1, to_half, half, 0, at.pair)]

        def eighth_copies(at):
            return [
                copy(g, at.sent_a, r2, to_eighth, eighth, 1, at.beside),
                copy(g, at.sent_b, r2, to_eighth + eighth, eighth, 2, at.below),
            ]

        def piece_copies(at):
            return [
                copy(g, at.last_a, r3, to_piece, piece, 3, at.below),
                copy(g, at.last_b, r3, to_piece + piece, piece, 4, at.beside),
            ]

        def piece_returns(at):
            return [
                copy(g, at.a, g, at.a, piece, 13, at.below),
                copy(g, at.b_, g, at.b_, piece, 14, at.beside),
            ]

        def eighth_returns(at):
            return [
                copy(g, at.eighth_a, g, at.eighth_a, eighth, 15, at.beside),
                copy(g, at.eighth_b, g, at.eighth_b, eighth, 16, at.below),
            ]

        def pair_returns(at):
            return [copy(g, at.mine, g, at.mine, half, 17, at.pair)]

        def go(copies):
            for c in copies:
                c.start()

        def end(copies):
            for c in copies:
                c.wait()

        def add(at, other, to, size):
            step = 16 if size % 16 == 0 else size

            def body(i, carry):
                mine = pl.ds(at + i * step, step)
                g[mine] = g[mine] + other[pl.ds(to + i * step, step)]
                return carry

            lax.fori_loop(0, size // step, body, 0)

        def free(slot, device):
            sem = k.free_sem.at[layer, number, slot]
            pl.semaphore_signal(sem, inc=1, device_id=device, device_id_type=MESH)

        def wait_free(slot):
            pl.semaphore_wait(k.free_sem.at[layer, number, slot], 1)

        def for_owner(at, do):
            if stride == 1:
                do()
            else:
                pl.when(lax.rem(at.b, stride) == 0)(do)

        def for_others(at, do):
            for owner in range(OWNERS):
                pl.when(at.b != owner * stride)(functools.partial(do, owner))

        def share_copies(at):
            return [
                pltpu.make_async_remote_copy(
                    src_ref=g.at[pl.ds(at.chunk, chunk)],
                    dst_ref=r5.at[at.rank, pl.ds(to_chunk, chunk)],
                    send_sem=k.grad_sem.at[0, layer, number, 9],
                    recv_sem=k.grad_sem.at[1, layer, number, 9 + at.rank],
                    device_id=(lax.rem(at.b + i, n_batch), at.h, at.w),
                    device_id_type=MESH,
                )
                for i in range(1, n_batch)
            ]

        def start_pair():
            go(pair_copies(places()))

        def start_eighths():
            at = places()
            end(pair_copies(at))
            free(0, at.pair)
            add(at.mine, r1, to_half, half)
            go(eighth_copies(at))

        def start_pieces():
            at = places()
            end(eighth_copies(at))
            add(at.eighth_a, r2, to_eighth, eighth)
            add(at.eighth_b, r2, to_eighth + eighth, eighth)
            go(piece_copies(at))

        def start_chunks():
            at = places()
            end(piece_copies(at))
            free(1, at.below)
            free(2, at.beside)
            add(at.a, r3, to_piece, piece)
            add(at.b_, r3, to_piece + piece, piece)

            def send_chunk(owner):
                pltpu.make_async_remote_copy(
                    src_ref=g.at[pl.ds(at.chunks[owner], chunk)],
                    dst_ref=r4.at[at.b, pl.ds(to_chunk, chunk)],
                    send_sem=k.grad_sem.at[0, layer, number, 5 + owner],
                    recv_sem=k.grad_sem.at[1, layer, number, 5],
                    device_id=(owner * stride, at.h, at.w),
                    device_id_type=MESH,
                ).start()

            for_others(at, send_chunk)

        def share_chunk():
            at = places()

            def collect():
                others = r4.at[pl.ds(0, n_batch - 1), pl.ds(to_chunk, chunk)]
                pltpu.make_async_copy(others, others, k.grad_sem.at[1, layer, number, 5]).wait()
                r4[at.b, pl.ds(to_chunk, chunk)] = g[pl.ds(at.chunk, chunk)]
                total = r4[0, pl.ds(to_chunk, chunk)].astype(F32)
                for slot in range(1, n_batch):
                    total = total + r4[slot, pl.ds(to_chunk, chunk)].astype(F32)
                g[pl.ds(at.chunk, chunk)] = total.astype(BF16)
                go(share_copies(at))

            for_owner(at, collect)

            def sent_chunk(owner):
                part = g.at[pl.ds(at.chunks[owner], chunk)]
                pltpu.make_async_copy(part, part, k.grad_sem.at[0, layer, number, 5 + owner]).wait()

            for_others(at, sent_chunk)

        def return_pieces():
            at = places()

            def shared():
                for c in share_copies(at):
                    c.wait_send()

            for_owner(at, shared)

            def take_chunk(owner):
                part = r5.at[owner, pl.ds(to_chunk, chunk)]
                pltpu.make_async_copy(part, part, k.grad_sem.at[1, layer, number, 9 + owner]).wait()
                g[pl.ds(at.chunks[owner], chunk)] = r5[owner, pl.ds(to_chunk, chunk)]

            for_others(at, take_chunk)
            wait_free(1)
            wait_free(2)
            go(piece_returns(at))

        def return_eighths():
            at = places()
            end(piece_returns(at))
            go(eighth_returns(at))

        def return_halves():
            at = places()
            end(eighth_returns(at))
            wait_free(0)
            go(pair_returns(at))

        def result():
            target = k.weight_grads.at[layer, pl.ds(LOW_OUT if begin == LOW_AT else begin, count)]
            sem = k.out_sem.at[layer, number]
            return pltpu.make_async_copy(g.at[pl.ds(begin, count)], target, sem)

        def start_result():
            end(pair_returns(places()))

            result().start()

        def end_result():
            result().wait()

        return (
            start_pair,
            start_eighths,
            start_pieces,
            start_chunks,
            share_chunk,
            return_pieces,
            return_eighths,
            return_halves,
            start_result,
            end_result,
        )

    exchanges = {(layer, number): exchange(layer, number) for layer in range(2) for number in range(3)}
    plan, taken = {}, dict.fromkeys(exchanges, 0)
    for point, keys in list(SCHEDULE.items()) + [(None, LAST_STEPS)]:
        for key in keys:
            plan.setdefault(point, []).append(exchanges[key][taken[key]])
            taken[key] += 1
    assert all(taken[key] == len(exchanges[key]) for key in exchanges)

    def progress(*point):
        for step in plan.get(point, ()):
            step()

    def flat_block(lay):
        block = lay.s.block_in[...]
        return block.reshape(lay.cells, block.shape[-1])

    def store_blocks(layer, at, value):
        rows, lanes = value.shape
        for lane in range(0, lanes, 128):
            size = min(128, lanes - lane)
            blocks = pl.ds(at + lane // 128 * (rows // 16), rows // 16)
            tile = value[:, lane : lane + size].reshape(rows // 16, 16, size)
            k.grads[layer, blocks, :, 0:size] = tile

    def column_sum(value):
        return jnp.sum(value, axis=0, keepdims=True)

    def center_mask(lay, row, count=1):
        mask = lay.s.mask[pl.ds(row + 1, count), 1 : lay.cols + 1]
        return mask.reshape(count * lay.row_cells, 1)

    def shifted(lay, value):
        count = value.shape[0]
        frame_at = lax.rem(lax.broadcasted_iota(jnp.int32, (count, 1), 0), lay.slot)
        before = jnp.where(frame_at == 0, 0.0, pltpu.roll(value, 1, 0))
        after = jnp.where(frame_at == lay.slot - 1, 0.0, pltpu.roll(value, count - 1, 0))
        return before, after

    def reorder(lay, value, cells_first):
        size, cols, frames = lay.row_cells, lay.cols, lay.frames
        to = lax.broadcasted_iota(jnp.int32, (size, size), 0)
        source = lax.broadcasted_iota(jnp.int32, (size, size), 1)
        if cells_first:
            wanted = lax.rem(to, frames) * cols + lax.div(to, frames)
        else:
            wanted = lax.rem(to, cols) * frames + lax.div(to, cols)
        swap = (source == wanted).astype(F32).astype(BF16)
        return dot(swap, value.reshape(size, value.shape[-1]))

    def cells_of(lay, i):
        size = lay.step * lay.row_cells
        return pl.ds(i * size if isinstance(i, int) else pl.multiple_of(i * size, size), size)

    def reduce_conv(lay):
        s, at, step = lay.s, lay.index, lay.step
        count = step * lay.row_cells

        def body(i, sums):
            mask = center_mask(lay, i * step, step)
            if lay.index == 0:
                load_features(i).wait()
            if lay.index == 0:
                block = [reorder(lay, k.v_input_grad[:, i * step + row], True) for row in range(step)]
                block = (jnp.concatenate(block, axis=0) * mask).astype(BF16)
                shape = (step, lay.cols, lay.frames, block.shape[-1])
                s.block_in[pl.ds(i * step, step)] = block.reshape(shape)
            else:
                block = s.block_in[pl.ds(i * step, step)]
                block = block.reshape(count, block.shape[-1])
            reduced = dot(block, k.v_w_reduce[at], NT)
            projected = dot(block, k.v_w_pool[at])
            rows = pl.ds(i * step, step)
            inner = pl.ds(i * step + 1, step)
            shape = (step, lay.cols, lay.frames)
            s.first[rows] = reduced[:, :B0].reshape(shape + (B0,))
            thin = reduced[:, B0:].reshape(shape + (NARROW,))
            s.narrow[inner, 1 : lay.cols + 1] = thin
            s.border[inner, 1 : lay.cols + 1, :, 0:BP] = projected.reshape(shape + (BP,)).astype(BF16)
            s.border[inner, 1 : lay.cols + 1, :, BP:] = thin.astype(BF16)
            total, square, valid = sums
            return (
                total + column_sum(reduced),
                square + column_sum(reduced * reduced),
                valid + column_sum(mask),
            )

        zero = jnp.zeros((1, REDUCE), F32)
        return loop(lay.rows // step, body, (zero, zero, jnp.zeros((1, 1), F32)))

    def narrow_cells(lay, norm, where):
        s = lay.s
        average, scale, bias = norm
        z = s.narrow[where]
        shape = z.shape[:-1]
        z = z.reshape(-1, NARROW)
        mask = s.mask[where].reshape(-1, 1)
        value = jnp.where(mask > 0.0, softplus((z - average) * scale + bias), 0.0)
        before, after = shifted(lay, value)
        parts = (before, value, after)
        mid = jnp.concatenate([p[:, :B1R] for p in parts], axis=1)
        small = jnp.concatenate([p[:, B1R:] for p in parts], axis=1)
        s.mid_in[where] = mid.astype(BF16).reshape(shape + (3 * B1R,))
        s.small_in[where] = small.astype(BF16).reshape(shape + (3 * B2R,))

    def narrow_center(lay, norm):
        s, step = lay.s, lay.pad_step
        inner = slice(1, lay.cols + 1)
        for row in (0, lay.rows + 1):
            s.narrow[row, inner] = s.border[row, inner, :, BP:].astype(F32)

        def body(i, carry):
            narrow_cells(lay, norm, (pl.ds(i * step, step), inner))
            return carry

        loop((lay.rows + 2) // step, body, 0)

    def narrow_sides(lay, norm):
        s, step = lay.s, lay.pad_step
        for col in (0, lay.cols + 1):
            s.narrow[:, col] = s.border[:, col, :, BP:].astype(F32)
            narrow_cells(lay, norm, (slice(None), col))

        def body(i, carry):
            at = pl.ds(i * step, step)
            s.box[at] = box_row(lay, s.border[at, :, :, 0:BP].astype(F32))
            return carry

        loop((lay.rows + 2) // step, body, 0)

    def box_row(lay, value):
        cols, t, step = lay.cols, lay.frames, lay.pad_step
        flat = value.reshape(step * (cols + 2) * t, BP)
        before, after = shifted(lay, flat)
        flat = (flat + before + after).reshape(step, cols + 2, t, BP)
        return flat[:, 0:cols] + flat[:, 1 : cols + 1] + flat[:, 2 : cols + 2]

    def box_rows(lay, row):
        box, step = lay.s.box, lay.step
        total = box[pl.ds(row, step)] + box[pl.ds(row + 1, step)] + box[pl.ds(row + 2, step)]
        return total.reshape(step * lay.row_cells, BP) * (1.0 / 27.0)

    def window(lay, ref, row, col, width):
        value = ref[pl.ds(row, lay.rows), pl.ds(col, lay.cols)]
        return value.reshape(lay.cells, width)

    def taps(lay, body, at, begin=0, end=9):
        if lay.index:
            for tap in range(begin, end):
                body(tap, 0)
                progress(1, (at, tap))
            return

        def with_progress(tap, carry):
            body(tap, carry)
            for some in range(begin, end):
                if (0, (at, some)) in SCHEDULE:

                    @pl.when(tap == some)
                    def _(some=some):
                        progress(0, (at, some))

            return carry

        lax.fori_loop(begin, end, with_progress, 0)

    def tap_at(tap):
        return (tap // 3, tap % 3) if isinstance(tap, int) else (lax.div(tap, 3), lax.rem(tap, 3))

    def cube_conv(lay, meanwhile):
        s, at = lay.s, lay.index
        s.mid[:, 0:B1] = jnp.zeros((lay.cells, B1), F32)
        s.small[...] = jnp.zeros(s.small.shape, F32)

        def body(tap, carry):
            row, col = tap_at(tap)
            s.mid[:, 0:B1] += dot(window(lay, s.mid_in, row, col, 3 * B1R), k.v_w_mid[at, tap])
            s.small[...] += dot(window(lay, s.small_in, row, col, 3 * B2R), k.v_w_small[at, tap])
            return carry

        def inner_tap(i):
            return 3 * i + 1

        def outer_tap(i):
            return 3 * (i // 2) + 2 * (i % 2) if isinstance(i, int) else 3 * lax.div(i, 2) + 2 * lax.rem(i, 2)

        for count, to_tap in ((3, inner_tap), (6, outer_tap)):
            if lay.index:
                for i in range(count):
                    body(to_tap(i), 0)
            else:
                lax.fori_loop(0, count, lambda i, carry, to_tap=to_tap: body(to_tap(i), carry), 0)
            if to_tap is inner_tap:
                meanwhile()

    def second_rows(lay, i):
        cells = cells_of(lay, i)
        return [
            ref[cells, 0:n] for ref, n in zip((lay.s.mid, lay.s.small, lay.s.pool), SECOND)
        ]

    def second_sums(lay):
        def body(i, sums):
            lay.s.pool[cells_of(lay, i), :] = box_rows(lay, i * lay.step)
            mask = center_mask(lay, i * lay.step, lay.step)
            out = []
            for (total, square), value in zip(sums, second_rows(lay, i)):
                inside = value * mask
                out.append((total + column_sum(inside), square + column_sum(inside * value)))
            return tuple(out)

        zero = tuple((jnp.zeros((1, n), F32),) * 2 for n in SECOND)
        return loop(lay.rows // lay.step, body, zero)

    def put_second(at, sums):
        for which in range(2):
            for begin, part, width in zip(SECOND_AT, sums, SECOND):
                begin += which * SECOND_WIDTH
                k.sums[at, :, begin : begin + width] = part[which]

    def get_second(total, which):
        return [total[:, which * SECOND_WIDTH + a : which * SECOND_WIDTH + a + n] for a, n in zip(SECOND_AT, SECOND)]

    def put_first(at, sums):
        for which in range(2):
            k.sums[at, :, which * 512 : which * 512 + REDUCE] = sums[which]

    def get_first(total, which):
        return total[:, which * 512 : which * 512 + REDUCE]

    def second_params(k_of, at):
        row = k_of[at : at + 1, :]
        out, begin = [], REDUCE
        for width in SECOND:
            out.append(row[:, begin : begin + width])
            begin += width
        return out

    def first_params(k_of, at):
        return k_of[at : at + 1, 0:REDUCE]

    def forward(lay, at, count, cubes, before, first_idle, after_first, in_conv, second_idle):
        s = lay.s
        total, square, valid = reduce_conv(lay)
        before()
        put_first(at, (total, square))
        if count is None:
            k.sums[at, :, 1024:1152] = jnp.broadcast_to(valid, (1, 128))
        start_sum(at)
        start_halo(lay, s.border, 2 * lay.index)
        first_idle()
        end_halo(lay, s.border, 2 * lay.index, cols=False)
        for copy in cubes:
            copy.wait()
        summed = end_sum(at)
        if count is None:
            count = summed[:, 1024:1025]
        gain = first_params(k.gain, lay.index)
        first = batch_norm_scale(get_first(summed, 0), get_first(summed, 1), count, gain)
        first += (first_params(k.bias, lay.index), gain)
        after_first()
        thin = (first[0][:, B0:], first[2][:, B0:], first[3][:, B0:])
        narrow_center(lay, thin)

        def sides():
            end_halo(lay, s.border, 2 * lay.index, rows=False)
            narrow_sides(lay, thin)
            in_conv()

        cube_conv(lay, sides)
        put_second(at + 1, second_sums(lay))
        start_sum(at + 1)
        second_idle()
        summed = end_sum(at + 1)
        second = []
        for total, square, gain, bias in zip(
            get_second(summed, 0),
            get_second(summed, 1),
            second_params(k.gain, lay.index),
            second_params(k.bias, lay.index),
        ):
            second.append(batch_norm_scale(total, square, count, gain) + (bias, gain))
        return first, second, count

    def normalised(value, norm):
        average, inv_std, scale, bias, gain = norm
        return (value - average) * inv_std

    def affine(value, norm):
        average, inv_std, scale, bias, gain = norm
        return (value - average) * scale + bias

    def left_half(norm):
        return tuple(p[:, :B0] for p in norm)

    def outputs(lay, i, first, second):
        mask = center_mask(lay, i * lay.step, lay.step)
        z = lay.s.first[pl.ds(i * lay.step, lay.step)].reshape(lay.step * lay.row_cells, B0)
        parts = [softplus(affine(z, left_half(first))) * mask]
        parts += [softplus(affine(v, n)) * mask for v, n in zip(second_rows(lay, i), second)]
        return parts

    def put_normed(lay, second, begin, end, cols):
        step = min(lay.step, end - begin)
        skipped, count = cols.start, cols.stop - cols.start

        def body(i, carry):
            row = begin + i * step
            inner = (pl.ds(row + 1, step), pl.ds(skipped + 1, count))
            size = lay.row_cells
            cells = pl.ds(row * size if isinstance(i, int) else pl.multiple_of(row * size, size), step * size)
            for a, width, ref, n in zip(SECOND_AT, SECOND, (lay.s.mid, lay.s.small, lay.s.pool), second):
                value = ref[cells, 0:width].reshape(step, lay.cols, lay.frames, width)
                value = value[:, cols].reshape(step * count * lay.frames, width)
                normed = normalised(value, n).astype(BF16).reshape(step, count, lay.frames, width)
                lay.s.normed[inner + (slice(None), slice(a, a + width))] = normed
            return carry

        loop((end - begin) // step, body, 0)

    for copy in flat_one:
        copy.wait()

    def wait_barrier():
        for copy in cubes_one + [slope_load] + flat_two + cubes_two:
            copy.start()
        beside = (w > 0).astype(jnp.int32) + (w < n_wa - 1).astype(jnp.int32)
        pl.semaphore_wait(barrier, chips + beside)

    def spread_two():
        slope_load.wait()
        for row in range(two.rows):
            k.slopes[pl.ds(row * two.row_cells, two.row_cells), :] = reorder(
                two, k.v_out_grad[:, row], True
            ).astype(BF16)
        for a, part, width in zip(SECOND_AT, slope_two(0)[1:], SECOND):
            part = part.reshape(two.rows, two.cols, two.frames, width).astype(BF16)
            k.grad_border[0, 1 : two.rows + 1, 1 : two.cols + 1, :, a : a + width] = part
        start_halo(two, k.grad_border.at[0], 4)

    def nothing():
        return None

    def split(value):
        a, b_, c, d = B0, B0 + B1, B0 + B1 + B2, B0 + B1 + B2 + BP
        return [value[:, :a], value[:, a:b_], value[:, b_:c], value[:, c:d]]

    def slope_two(i):
        return split(k.slopes[...].astype(F32))

    first_one, second_one, count_one = forward(
        one, 0, None, cubes_one, wait_barrier, nothing, nothing, spread_two, nothing
    )

    def halve(row, carry):
        begin = 0
        for p in outputs(one, row, first_one, second_one):
            width = p.shape[-1]
            both = p.reshape(2, two.cols, 2, one.frames, width)
            both = both[0, :, 0] + both[0, :, 1] + both[1, :, 0] + both[1, :, 1]
            for lane in range(0, width, 128):
                size = min(128, width - lane)
                k.pairs[:, begin + lane // 128, :, 0:size] = both[:, :, lane : lane + size]
            begin += -(-width // 128)
        for col in range(two.cols):
            tiles = []
            for lane in range(begin):
                even = k.pairs[col, lane, pl.ds(0, two.frames, stride=2), :]
                odd = k.pairs[col, lane, pl.ds(1, two.frames, stride=2), :]
                tiles.append((even + odd) * 0.125)
            half = (B0 + B1) // 128
            tiles[half] = tiles[half][:, : (B0 + B1) % 128]
            mean = jnp.concatenate(tiles, axis=1)
            two.s.block_in[row, col] = mean.astype(BF16)
        return carry

    half_rows = one.rows // 2
    put_normed(one, second_one, 0, half_rows, slice(0, 1))
    start_normed(*NORMED_AT[0])
    lax.fori_loop(0, two.rows, halve, 0)

    for copy in flat_two:
        copy.wait()

    def share_normed():
        put_normed(one, second_one, 0, half_rows, slice(1, one.cols))
        put_normed(one, second_one, half_rows, one.rows, slice(0, one.cols))
        start_normed(*NORMED_AT[1])

    def share_third():
        start_normed(*NORMED_AT[2])

    def share_rest():
        start_normed(*NORMED_AT[3])

    first_two, second_two, count_two = forward(
        two, 2, count_one * 0.125, cubes_two, nothing, share_normed, share_third, nothing, share_rest
    )

    def level(lay, begin, end):
        return softplus(k.bias[lay.index : lay.index + 1, begin:end]).astype(BF16).astype(F32)

    def center_windows(lay):
        mid, small = level(lay, B0, B0 + B1R), level(lay, B0 + B1R, REDUCE)
        mid, small = (jnp.concatenate([v] * 3, axis=1) for v in (mid, small))
        s, step = lay.s, lay.pad_step

        def body(i, carry):
            at = pl.ds(i * step, step)
            for ref, value in ((s.mid_in, mid), (s.small_in, small)):
                shape = (step,) + ref.shape[1:]
                part = ref[at].reshape(-1, shape[-1]).astype(F32) - value
                ref[at] = part.astype(BF16).reshape(shape)
            return carry

        loop((lay.rows + 2) // step, body, 0)

    def centered_block(lay):
        if lay.index == 0:
            return flat_block(lay)
        value = jnp.concatenate([level(one, 0, B0), level(one, REDUCE, k.bias.shape[1])], axis=1)
        return (flat_block(lay).astype(F32) - value).astype(BF16)

    def backward(lay, out_slope, border_slope, at, first, second, count, before_end, after_end, before_low):
        s, index, step = lay.s, lay.index, lay.step
        chunks = lay.rows // step
        per_cell = 1.0 / count

        def second_slope(i):
            mask = center_mask(lay, i * step, step)
            values = second_rows(lay, i)
            normed = [normalised(v, n) for v, n in zip(values, second)]
            slopes = [
                g * mask * sigmoid(m * n[4] + n[3])
                for g, m, n in zip(out_slope(i)[1:], normed, second)
            ]
            return mask, normed, slopes

        def sum_body(i, sums):
            mask, normed, slopes = second_slope(i)
            return tuple(
                (t + column_sum(g), q + column_sum(g * m))
                for (t, q), g, m in zip(sums, slopes, normed)
            )

        zero = tuple((jnp.zeros((1, n), F32),) * 2 for n in SECOND)
        put_second(at, loop(chunks, sum_body, zero))
        start_sum(at)
        before_end()
        center_windows(lay)
        progress(index, 0)
        summed = end_sum(at)
        after_end()
        totals = list(zip(get_second(summed, 0), get_second(summed, 1)))
        begin = REDUCE
        for (bias_grad, gain_grad), width in zip(totals, SECOND):
            k.bias_grad[index : index + 1, begin : begin + width] = bias_grad
            k.gain_grad[index : index + 1, begin : begin + width] = gain_grad
            begin += width
        totals = [(t * per_cell, q * per_cell) for t, q in totals]

        def pre_slope(g, m, norm, total):
            return norm[2] * (g - (total[0] + m * total[1]))

        def center_body(i, carry):
            mask, normed, slopes = second_slope(i)
            inner = pl.ds(i * step + 1, step)
            for a, width, g, m, n, total in zip(SECOND_AT, SECOND, slopes, normed, second, totals):
                value = (pre_slope(g, m, n, total) * mask).astype(BF16)
                s.normed[inner, 1 : lay.cols + 1, :, a : a + width] = value.reshape(
                    step, lay.cols, lay.frames, width
                )
            return carry

        loop(chunks, center_body, 0)

        def border_cells(where, slopes):
            mask = s.mask[where]
            cells = mask.shape[0]
            mask = mask.reshape(cells * lay.frames, 1)
            normed = s.normed[where].astype(F32).reshape(cells * lay.frames, SECOND_WIDTH)
            for a, width, g, n, total in zip(SECOND_AT, SECOND, slopes, second, totals):
                m = normed[:, a : a + width]
                g = g * sigmoid(m * n[4] + n[3])
                value = jnp.where(mask > 0.0, pre_slope(g, m, n, total), 0.0).astype(BF16)
                s.normed[where + (slice(None), slice(a, a + width))] = value.reshape(
                    cells, lay.frames, width
                )

        border_cells((jnp.where(h == 0, lay.rows + 1, 0), slice(None)), border_slope(True, None))
        for col in (0, lay.cols + 1):
            border_cells((slice(1, lay.rows + 1), col), border_slope(False, col > 0))

        progress(index, 1)

        center = s.normed[1 : lay.rows + 1, 1 : lay.cols + 1].reshape(lay.cells, SECOND_WIDTH)
        turned_mid = center[:, 0:B1].T
        turned_small = center[:, 384:512].T

        def tap_body(tap, carry):
            row, col = tap_at(tap)
            mid = dot(turned_mid, window(lay, s.mid_in, row, col, 3 * B1R)).astype(BF16)
            small = dot(turned_small, window(lay, s.small_in, row, col, 3 * B2R)).astype(BF16)
            store_blocks(index, tap * TAP_BLOCKS, mid)
            store_blocks(index, tap * TAP_BLOCKS + 80, small)
            return carry

        taps(lay, tap_body, 5, 0, EARLY_TAPS[index])

        s.mid[...] = jnp.zeros(s.mid.shape, F32)
        s.small[:, 0 : 3 * B2R] = jnp.zeros((lay.cells, 3 * B2R), F32)

        def back_body(tap, carry):
            row, col = tap_at(tap)
            slope = window(lay, s.normed, 2 - row, 2 - col, SECOND_WIDTH)
            s.mid[...] += dot(slope[:, 0:B1], k.v_w_mid[index, tap], NT)
            s.small[:, 0 : 3 * B2R] += dot(slope[:, 384:512], k.v_w_small[index, tap], NT)
            return carry

        taps(lay, back_body, 2)

        def box_body(i, carry):
            at = pl.ds(i * lay.pad_step, lay.pad_step)
            s.box[at] = box_row(lay, s.normed[at, :, :, 512:640].astype(F32))
            return carry

        loop((lay.rows + 2) // lay.pad_step, box_body, 0)
        progress(index, 3)

        def first_normed(i):
            size = step * lay.row_cells
            z = s.first[pl.ds(i * step, step)].reshape(size, B0)
            z_thin = s.narrow[pl.ds(i * step + 1, step), 1 : lay.cols + 1].reshape(size, NARROW)
            return normalised(jnp.concatenate([z, z_thin], axis=1), first)

        def first_body(i, sums):
            cells = cells_of(lay, i)
            s.projected_slope[cells, :] = box_rows(lay, i * step).astype(BF16)
            mid = s.mid[cells, :]
            small = s.small[cells, 0 : 3 * B2R]
            thirds = [
                jnp.concatenate(
                    [mid[:, B1R * t : B1R * (t + 1)], small[:, B2R * t : B2R * (t + 1)]], axis=1
                )
                for t in range(3)
            ]
            thin = thirds[1] + shifted(lay, thirds[2])[0] + shifted(lay, thirds[0])[1]
            mask = center_mask(lay, i * step, step)
            normed = first_normed(i)
            g = jnp.concatenate([out_slope(i)[0], thin], axis=1)
            g = g * mask * sigmoid(normed * first[4] + first[3])
            s.mid[cells, 0:REDUCE] = g
            return sums[0] + column_sum(g), sums[1] + column_sum(g * normed)

        zero = (jnp.zeros((1, REDUCE), F32),) * 2
        put_first(at + 1, loop(chunks, first_body, zero))
        start_sum(at + 1)

        progress(index, 4)

        taps(lay, tap_body, 5, EARLY_TAPS[index])
        store_blocks(index, LOW_AT + 196, dot(s.projected_slope[...].T, flat_block(lay)).astype(BF16))
        progress(index, 6)
        summed = end_sum(at + 1)
        total = (get_first(summed, 0), get_first(summed, 1))
        k.bias_grad[index : index + 1, 0:REDUCE] = total[0]
        k.gain_grad[index : index + 1, 0:REDUCE] = total[1]

        total = (total[0] * per_cell, total[1] * per_cell)

        def low_body(i, carry):
            cells = cells_of(lay, i)
            mask = center_mask(lay, i * step, step)
            value = pre_slope(s.mid[cells, 0:REDUCE], first_normed(i), first, total) * mask
            s.low[cells, :] = value.astype(BF16)
            return carry

        loop(chunks, low_body, 0)
        before_low()
        progress(index, 7)
        store_blocks(index, LOW_AT, dot(s.low[...].T, centered_block(lay)).astype(BF16))
        progress(index, 8)

    def widen(ref, begin, value):
        width = value.shape[-1]
        for lane in range(0, width, 128):
            size = min(128, width - lane)
            for odd in range(2):
                ref[(begin + lane) // 128, pl.ds(odd, two.frames, stride=2), 0:size] = value[
                    :, lane : lane + size
                ]

    def wide(value, a, width):
        tiles = [value[..., lane // 128, :, :] for lane in range(a, a + width, 128)]
        return jnp.concatenate(tiles, axis=-1)[..., :width]

    def put_two(i, slope):
        slope = slope * 0.125
        for a, part in zip((0,) + tuple(B0 + a for a in SECOND_AT), split(slope)):
            width = part.shape[-1]
            part = part.reshape(two.rows, two.cols, two.frames, width)
            for row in range(two.rows):
                for col in range(two.cols):
                    widen(k.spread.at[row, col], a, part[row, col])
            if a >= B0:
                inner = (slice(1, two.rows + 1), slice(1, two.cols + 1), slice(None))
                k.grad_border[(1,) + inner + (slice(a - B0, a - B0 + width),)] = part.astype(BF16)

    def input_slope(lay, low, projected):
        slope = dot(low, k.v_w_reduce[lay.index])
        return slope + dot(projected, k.v_w_pool[lay.index], NT)

    def low_two():
        mask = center_mask(two, 0, two.rows)
        put_two(0, input_slope(two, two.s.low[...], two.s.projected_slope[...]) * mask)

    def side(lay, across, last):
        if across:
            return (jnp.where(h == 0, lay.rows + 1, 0), slice(None))
        return (slice(1, lay.rows + 1), lay.cols + 1 if last else 0)

    def border_two(across, last):
        value = k.grad_border[(0,) + side(two, across, last)].astype(F32)
        value = value.reshape(value.shape[0] * two.frames, SECOND_WIDTH)
        return [value[:, a : a + n] for a, n in zip(SECOND_AT, SECOND)]

    def end_two():
        put_normed(two, second_two, 0, two.rows, slice(0, two.cols))
        start_halo(two, two.s.normed, 3)
        value = jnp.concatenate(outputs(two, 0, first_two, second_two), axis=1).astype(BF16)
        for row in range(two.rows):
            part = reorder(two, value[row * two.row_cells : (row + 1) * two.row_cells], False)
            k.v_block_output[:, row] = part.reshape(two.frames, two.cols, -1).astype(BF16)
        output_store.start()
        end_halo(two, two.s.normed, 3)
        end_halo(two, k.grad_border.at[0], 4)

    def after_two():
        start_normed(*NORMED_AT[4])

    backward(two, slope_two, border_two, 4, first_two, second_two, count_two, end_two, after_two, low_two)
    start_halo(two, k.grad_border.at[1], 5)

    def slope_one(i):
        value = k.spread[i]
        out = []
        for a, width in zip((0,) + tuple(B0 + a for a in SECOND_AT), (B0,) + SECOND):
            part = wide(value, a, width)
            pieces = [part[col // 2] for col in range(one.cols)]
            out.append(jnp.concatenate(pieces * one.step, axis=0))
        return out

    def border_one(across, last):
        where = side(two, across, last)
        value = k.border_spread[where] if across else k.border_spread[:, where[1]]
        cells = range(one.cols + 2) if across else range(1, one.rows + 1)
        out = []
        for a, n in zip(SECOND_AT, SECOND):
            part = wide(value, a, n)
            out.append(jnp.concatenate([part[(cell + 1) // 2] for cell in cells], axis=0))
        return out

    def end_one():
        end_normed()
        end_halo(two, k.grad_border.at[1], 5)
        places = [(side(two, True, None)[0], col) for col in range(two.cols + 2)]
        places += [(row, col) for row in range(1, two.rows + 1) for col in (0, two.cols + 1)]
        for row, col in places:
            widen(k.border_spread.at[row, col], 0, k.grad_border[1, row, col].astype(F32))

    backward(one, slope_one, border_one, 6, first_one, second_one, count_one, end_one, nothing, nothing)

    def input_row(row, carry):
        cells = pl.ds(pl.multiple_of(row * one.row_cells, one.row_cells), one.row_cells)
        low = reorder(one, one.s.low[cells, :], False).astype(BF16)
        projected = one.s.projected_slope[cells, :].astype(F32) * center_mask(one, row)
        projected = reorder(one, projected.astype(BF16), False).astype(BF16)
        slope = input_slope(one, low, projected)
        k.v_input_grad[:, row] = slope.reshape(one.frames, one.cols, -1).astype(BF16)
        return carry

    lax.fori_loop(0, one.rows, input_row, 0)
    input_store.start()
    for step in plan[None]:
        step()
    output_store.wait()
    input_store.wait()


UNPACK_TAPS = 9


def unpack_body(taps, low, gain, bias, mid_out, small_out, reduce_out, pool_out, gain_out, bias_out):
    def lanes(blocks, tiles, rows, width):
        parts = []
        for tile in range(tiles):
            size = min(128, width - 128 * tile)
            part = blocks[tile * (rows // 16) : (tile + 1) * (rows // 16), :, 0:size]
            parts.append(part.reshape(rows, size))
        return jnp.concatenate(parts, axis=1)

    def tap_body(tap, carry):
        blocks = taps.at[0, pl.ds(tap * TAP_BLOCKS, TAP_BLOCKS)]
        mid = lanes(blocks, 4, B1, 3 * B1R).T.astype(F32)
        small = lanes(blocks.at[80:88], 1, B2, 3 * B2R).T.astype(F32)
        for t in range(3):
            mid_out[0, t, tap] = mid[B1R * t : B1R * (t + 1)]
            small_out[0, t, tap] = small[B2R * t : B2R * (t + 1)]
        return carry

    lax.fori_loop(0, UNPACK_TAPS, tap_body, 0)

    @pl.when(pl.program_id(1) == 0)
    def _():
        channels = reduce_out.shape[-1]
        tiles = -(-channels // 128)
        reduce_out[0] = lanes(low.at[0, 0:196], tiles, REDUCE, channels).astype(F32)
        pool_out[0] = lanes(low.at[0, 196:252], tiles, BP, channels).T.astype(F32)
        gain_out[...] = gain[...]
        bias_out[...] = bias[...]


def unpack(grads, gain, bias, channels):
    n = UNPACK_TAPS
    shapes = ((2, 3, 9, B1R, B1), (2, 3, 9, B2R, B2), (2, REDUCE, channels), (2, channels, BP))
    shapes += (gain.shape, bias.shape)
    norms = [pl.BlockSpec(gain.shape, lambda i, j: (0, 0))] * 2
    mid_grad, small_grad, reduce_grad, pool_grad, gain, bias = pl.pallas_call(
        unpack_body,
        grid=(2, 9 // n),
        out_shape=[jax.ShapeDtypeStruct(shape, F32) for shape in shapes],
        in_specs=[
            pl.BlockSpec((1, n * TAP_BLOCKS, 16, 128), lambda i, j: (i, j, 0, 0)),
            pl.BlockSpec((1, 256, 16, 128), lambda i, j: (i, LOW_OUT // 256, 0, 0)),
        ]
        + norms,
        out_specs=[
            pl.BlockSpec((1, 3, n, B1R, B1), lambda i, j: (i, 0, j, 0, 0)),
            pl.BlockSpec((1, 3, n, B2R, B2), lambda i, j: (i, 0, j, 0, 0)),
            pl.BlockSpec((1, REDUCE, channels), lambda i, j: (i, 0, 0)),
            pl.BlockSpec((1, channels, BP), lambda i, j: (i, 0, 0)),
        ]
        + norms,
        compiler_params=pltpu.CompilerParams(vmem_limit_bytes=60 * 1024 * 1024),
        name="unpack",
    )(grads, grads, gain, bias)
    return (
        jnp.swapaxes(reduce_grad, 1, 2),
        mid_grad.reshape(2, 27, B1R, B1),
        small_grad.reshape(2, 27, B2R, B2),
        pool_grad,
        gain,
        bias,
    )


def on_device(
    n_batch, n_wa, clip_features, frame_counts, w_reduce, w_mid, w_small, w_pool, norm_gain, norm_bias, out_grad
):
    frames, rows, cols, channels = clip_features.shape
    clips = frame_counts.shape[0]
    slot = frames // clips
    layers = (
        Layer(0, rows, cols, clips, slot),
        Layer(1, rows // 2, cols // 2, clips, slot // 2),
    )
    one, two = layers
    chips = n_batch * n_wa

    operands = dict(
        features=clip_features,
        frame_counts=frame_counts,
        w_reduce=jnp.swapaxes(w_reduce, 1, 2),
        w_mid=w_mid.reshape(2, 3, 9, B1R, B1),
        w_small=w_small.reshape(2, 3, 9, B2R, B2),
        w_pool=w_pool,
        gain=norm_gain,
        bias=norm_bias,
        out_grad=out_grad,
    )
    in_space = dict(frame_counts=pltpu.SMEM, gain=pltpu.VMEM, bias=pltpu.VMEM)
    out_space = dict(weight_grads=pl.ANY, block_output=pl.ANY, input_grad=pl.ANY)
    results = dict(
        block_output=jax.ShapeDtypeStruct(out_grad.shape, BF16),
        input_grad=jax.ShapeDtypeStruct(clip_features.shape, BF16),
        weight_grads=jax.ShapeDtypeStruct((2, LOW_OUT + 256, 16, 128), BF16),
        gain_grad=jax.ShapeDtypeStruct(norm_gain.shape, F32),
        bias_grad=jax.ShapeDtypeStruct(norm_bias.shape, F32),
    )
    scratch = {}
    for name in ("w_reduce", "w_pool", "out_grad"):
        scratch["v_" + name] = pltpu.VMEM(operands[name].shape, BF16)
    scratch.update(
        v_w_mid=pltpu.VMEM((2, 9, 3 * B1R, B1), BF16),
        v_w_small=pltpu.VMEM((2, 9, 3 * B2R, B2), BF16),
    )
    small_pad = (two.rows + 2, two.cols + 2)
    scratch.update(
        slopes=pltpu.VMEM((two.cells, channels), BF16),
        v_block_output=pltpu.VMEM(out_grad.shape, BF16),
        v_input_grad=pltpu.VMEM(clip_features.shape, BF16),
        result_sem=pltpu.SemaphoreType.DMA((2,)),
        pairs=pltpu.VMEM((two.cols, (B0 + SECOND_WIDTH) // 128, one.frames, 128), F32),
        spread=pltpu.VMEM(
            (two.rows, two.cols, (B0 + SECOND_WIDTH) // 128, one.frames, 128), F32
        ),
        border_spread=pltpu.VMEM(small_pad + (SECOND_WIDTH // 128, one.frames, 128), F32),
        grad_border=pltpu.VMEM((2,) + small_pad + (two.frames, SECOND_WIDTH), BF16),
        sums=pltpu.VMEM((8, 1, SUM_WIDTH), F32),
        pair_sums=pltpu.VMEM((8, 1, SUM_WIDTH), F32),
        chip_sums=pltpu.VMEM((2, chips, 1, SUM_WIDTH), F32),
        load_sem=pltpu.SemaphoreType.DMA((17,)),
        feature_sem=pltpu.SemaphoreType.DMA((one.rows // one.step,)),
        pair_sem=pltpu.SemaphoreType.DMA((2, 8)),
        chip_sem=pltpu.SemaphoreType.DMA((2, 8)),
        normed_sem=pltpu.SemaphoreType.DMA((2, 4, 3)),
        halo_sem=pltpu.SemaphoreType.DMA((2, 6, 5)),
        grads=pltpu.VMEM((2, GRAD_BLOCKS, 16, 128), BF16),
        got_half=pltpu.VMEM((2, GRAD_BLOCKS // 2, 16, 128), BF16),
        got_eighth=pltpu.VMEM((2, GRAD_BLOCKS // 4, 16, 128), BF16),
        got_piece=pltpu.VMEM((2, GRAD_BLOCKS // 8, 16, 128), BF16),
        got_chunk=pltpu.VMEM((2, n_batch, GRAD_BLOCKS // 32, 16, 128), BF16),
        got_total=pltpu.VMEM((2, OWNERS, GRAD_BLOCKS // 32, 16, 128), BF16),
        free_sem=pltpu.SemaphoreType.REGULAR((2, 3, 3)),
        grad_sem=pltpu.SemaphoreType.DMA((2, 2, 3, 18)),
        out_sem=pltpu.SemaphoreType.DMA((2, 3)),
    )
    names = list(operands) + list(results) + list(scratch)
    layer_scratch = [lay.scratch(channels) for lay in layers]

    def body(*refs):
        rest = refs[len(names) :]
        for lay, parts in zip(layers, layer_scratch):
            lay.s = SimpleNamespace(**dict(zip(parts, rest[: len(parts)])))
            rest = rest[len(parts) :]
        kernel_body(names, (n_batch, n_wa, layers), refs[: len(names)])

    out = pl.pallas_call(
        body,
        out_shape=list(results.values()),
        in_specs=[pl.BlockSpec(memory_space=in_space.get(name, pl.ANY)) for name in operands],
        out_specs=[pl.BlockSpec(memory_space=out_space.get(name, pltpu.VMEM)) for name in results],
        scratch_shapes=list(scratch.values()) + [r for parts in layer_scratch for r in parts.values()],
        compiler_params=pltpu.CompilerParams(
            collective_id=0, has_side_effects=True, vmem_limit_bytes=63 * 1024 * 1024
        ),
        name="layers",
    )(*operands.values())
    out = dict(zip(results, out))

    kernels_and_norms = unpack(out["weight_grads"], out["gain_grad"], out["bias_grad"], channels)

    return (
        out["block_output"],
        out["input_grad"],
        *kernels_and_norms,
    )


def solution(mesh):
    in_specs = (
        P("batch", "ha", "wa", None),
        P("batch"),
        P(),
        P(),
        P(),
        P(),
        P(),
        P(),
        P("batch", "ha", "wa", None),
    )
    out_specs = (
        P("batch", "ha", "wa", None),
        P("batch", "ha", "wa", None),
        P(),
        P(),
        P(),
        P(),
        P(),
        P(),
    )
    return jax.shard_map(
        functools.partial(on_device, mesh.shape["batch"], mesh.shape["wa"]),
        mesh=mesh,
        in_specs=in_specs,
        out_specs=out_specs,
        check_vma=False,
    )
```

```python
import functools
from types import SimpleNamespace

import jax
import jax.numpy as jnp
from jax import lax
from jax.experimental import pallas as pl
from jax.experimental.pallas import tpu as pltpu
from jax.sharding import PartitionSpec as P

HEIGHT = 14
EPSILON = 1e-05
MESH = pl.DeviceIdType.MESH
F32 = jnp.float32
BF16 = jnp.bfloat16

B0, B1R, B2R, B1, B2, BP = 256, 160, 32, 320, 128, 128
NARROW = B1R + B2R
REDUCE = B0 + NARROW
SECOND = (B1, B2, BP)
SECOND_AT = (0, 384, 512)
SECOND_WIDTH = 640
SUM_WIDTH = 1280
AXES = ("batch", "ha", "wa")

TAP_BLOCKS = 88
LOW_AT = 800
LOW_OUT = 1024
GRAD_BLOCKS = 1056
BUNDLES = ((0, 352), (352, 448), (800, 256))
OWNERS = 4

SCHEDULE = {
    (1, (5, 3)): ((1, 0),),
    (1, (5, 8)): ((1, 1),),
    (1, 6): ((1, 0),),
    (1, 8): ((1, 2),),
    (0, 0): ((1, 2), (1, 0),),
    (0, 1): ((1, 2),),
    (0, (5, 0)): ((1, 0),),
    (0, (5, 1)): ((1, 1),),
    (0, (5, 3)): ((0, 0),),
    (0, (5, 4)): ((1, 2),),
    (0, (5, 6)): ((0, 0),),
    (0, (5, 8)): ((0, 1),),
    (0, (2, 0)): ((1, 0),),
    (0, (2, 1)): ((1, 1),),
    (0, (2, 3)): ((1, 2),),
    (0, (2, 5)): ((0, 0),),
    (0, (2, 6)): ((0, 1),),
    (0, (2, 7)): ((1, 1),),
    (0, (2, 8)): ((1, 0),),
    (0, 4): ((1, 2),),
    (0, 6): ((0, 0), (0, 1), (1, 1),),
    (0, 7): ((1, 0),),
    (0, 8): ((0, 2), (0, 0), (0, 2), (1, 2),),
}
EARLY_TAPS = (9, 0)
LAST_STEPS = (
    (0, 1),
    (0, 2),
    (1, 1),
    (0, 0),
    (0, 2),
    (1, 0),
    (0, 1),
    (1, 1),
    (1, 0),
    (0, 0),
    (0, 2),
    (1, 1),
    (1, 2),
    (0, 1),
    (1, 0),
    (1, 1),
    (0, 2),
    (0, 0),
    (1, 2),
    (1, 1),
    (0, 1),
    (1, 2),
    (0, 2),
    (0, 0),
    (0, 0),
    (0, 1),
    (0, 2),
    (0, 1),
    (0, 2),
    (0, 1),
    (0, 2),
)

NORMED_AT = ((0,), (1,), (2,), (3,), ())

NN = (((1,), (0,)), ((), ()))
NT = (((1,), (1,)), ((), ()))


def dot(a, b, dims=NN):
    return lax.dot_general(a, b, dims, preferred_element_type=F32)


def softplus(x):
    return jnp.maximum(x, 0.0) + jnp.log(1.0 + jnp.exp(-jnp.abs(x)))


def sigmoid(x):
    return 1.0 / (1.0 + jnp.exp(-x))


def loop(count, body, init):
    return body(0, init) if count == 1 else lax.fori_loop(0, count, body, init)


class Layer:
    def __init__(self, index, rows, cols, clips, slot):
        self.index, self.rows, self.cols = index, rows, cols
        self.clips, self.slot = clips, slot
        self.frames = clips * slot
        self.cells = rows * cols * self.frames
        self.row_cells = cols * self.frames
        self.step = rows if index else 2
        self.pad_step = rows + 2 if index else 2

    def scratch(self, channels):
        r, c, t, n = self.rows, self.cols, self.frames, self.cells
        pad = (r + 2, c + 2, t)
        return dict(
            mask=pltpu.VMEM(pad + (1,), F32),
            block_in=pltpu.VMEM((r, c, t, channels), BF16),
            first=pltpu.VMEM((r, c, t, B0), F32),
            narrow=pltpu.VMEM(pad + (NARROW,), F32),
            border=pltpu.VMEM(pad + (BP + NARROW,), BF16),
            mid_in=pltpu.VMEM(pad + (3 * B1R,), BF16),
            small_in=pltpu.VMEM(pad + (3 * B2R,), BF16),
            box=pltpu.VMEM((r + 2, c, t, BP), F32),
            mid=pltpu.VMEM((n, 3 * B1R), F32),
            small=pltpu.VMEM((n, B2), F32),
            pool=pltpu.VMEM((n, BP), F32),
            normed=pltpu.VMEM(pad + (SECOND_WIDTH,), BF16),
            projected_slope=pltpu.VMEM((n, BP), BF16),
            low=pltpu.VMEM((n, REDUCE), BF16),
        )


def batch_norm_scale(total, square, count, gain):
    average = total / count
    variance = square / count - average * average
    inv_std = lax.rsqrt(variance + EPSILON)
    return average, inv_std, inv_std * gain


def kernel_body(names, sizes, refs):
    k = SimpleNamespace(**dict(zip(names, refs)))
    n_batch, n_wa, layers = sizes
    b, h, w = (lax.axis_index(a) for a in AXES)
    chips = n_batch * n_wa
    my_chip = b * n_wa + w
    one, two = layers

    def chip_at(p):
        return lax.div(p, n_wa), h, lax.rem(p, n_wa)

    def rotated(i):
        return lax.rem(my_chip + i, chips)

    def load(at, source, target):
        return pltpu.make_async_copy(source, target, k.load_sem.at[at])

    output_store = pltpu.make_async_copy(k.v_block_output, k.block_output, k.result_sem.at[0])
    input_store = pltpu.make_async_copy(k.v_input_grad, k.input_grad, k.result_sem.at[1])

    def load_features(i):
        rows = pl.ds(i * one.step, one.step)
        return pltpu.make_async_copy(
            k.features.at[:, rows], k.v_input_grad.at[:, rows], k.feature_sem.at[i]
        )

    def load_cubes(at, layer):
        copies = []
        for t in range(3):
            mid, small = pl.ds(B1R * t, B1R), pl.ds(B2R * t, B2R)
            copies.append(load(at + 2 * t, k.w_mid.at[layer, t], k.v_w_mid.at[layer, :, mid]))
            copies.append(load(at + 2 * t + 1, k.w_small.at[layer, t], k.v_w_small.at[layer, :, small]))
        return copies

    def load_flat(at, layer):
        return [
            load(at, k.w_reduce.at[layer], k.v_w_reduce.at[layer]),
            load(at + 1, k.w_pool.at[layer], k.v_w_pool.at[layer]),
        ]

    flat_one, flat_two = load_flat(0, 0), load_flat(2, 1)
    cubes_one, cubes_two = load_cubes(4, 0), load_cubes(10, 1)
    slope_load = load(16, k.out_grad, k.v_out_grad)
    for copy in flat_one:
        copy.start()
    for i in range(one.rows // one.step):
        load_features(i).start()
    for lay in layers:
        s = lay.s
        for ref in (s.border, s.normed):
            for row in (0, lay.rows + 1):
                ref[row] = jnp.zeros(ref.shape[1:], ref.dtype)
            for col in (0, lay.cols + 1):
                ref[:, col] = jnp.zeros((ref.shape[0],) + ref.shape[2:], ref.dtype)
    ref = k.grad_border
    ref[...] = jnp.zeros(ref.shape, ref.dtype)
    for layer in range(2):
        for begin, end in ((9 * TAP_BLOCKS, LOW_AT), (LOW_AT + 252, GRAD_BLOCKS)):
            k.grads[layer, begin:end] = jnp.zeros((end - begin, 16, 128), BF16)
    k.sums[...] = jnp.zeros(k.sums.shape, F32)

    barrier = pltpu.get_barrier_semaphore()
    pl.semaphore_signal(barrier, inc=1, device_id=(b, 1 - h, w), device_id_type=MESH)

    @pl.when(w > 0)
    def _():
        pl.semaphore_signal(barrier, inc=1, device_id=(b, 1 - h, w - 1), device_id_type=MESH)

    @pl.when(w < n_wa - 1)
    def _():
        pl.semaphore_signal(barrier, inc=1, device_id=(b, 1 - h, w + 1), device_id_type=MESH)

    def greet(i, carry):
        pl.semaphore_signal(barrier, inc=1, device_id=chip_at(rotated(i)), device_id_type=MESH)
        return carry

    lax.fori_loop(1, chips, greet, 0)

    for lay in layers:
        frame_at = lax.broadcasted_iota(jnp.int32, (lay.frames, 1), 0)
        inside = jnp.zeros((lay.frames, 1), F32)
        for clip in range(lay.clips):
            valid = k.frame_counts[clip]
            valid = valid if lay.index == 0 else lax.div(valid, 2)
            begin = clip * lay.slot
            inside = jnp.where((frame_at >= begin) & (frame_at < begin + valid), 1.0, inside)
        height = HEIGHT if lay.index == 0 else HEIGHT // 2
        for row in range(lay.rows + 2):
            at_row = h * lay.rows + row - 1
            for col in range(lay.cols + 2):
                at_col = w * lay.cols + col - 1
                good = (at_row >= 0) & (at_row < height) & (at_col >= 0) & (at_col < height)
                lay.s.mask[row, col] = inside * good.astype(F32)

    def start_sum(at):
        pair = pltpu.make_async_remote_copy(
            src_ref=k.sums.at[at],
            dst_ref=k.pair_sums.at[at],
            send_sem=k.pair_sem.at[0, at],
            recv_sem=k.pair_sem.at[1, at],
            device_id=(b, 1 - h, w),
            device_id_type=MESH,
        )
        pair.start()
        pair.wait_recv()
        k.chip_sums[at % 2, my_chip] = k.sums[at] + k.pair_sums[at]

        def send(i, carry):
            pltpu.make_async_remote_copy(
                src_ref=k.chip_sums.at[at % 2, my_chip],
                dst_ref=k.chip_sums.at[at % 2, my_chip],
                send_sem=k.chip_sem.at[0, at],
                recv_sem=k.chip_sem.at[1, at],
                device_id=chip_at(rotated(i)),
                device_id_type=MESH,
            ).start()
            return carry

        if chips <= 16:
            for i in range(1, chips):
                send(i, 0)
        else:
            lax.fori_loop(1, chips, send, 0)
        pair.wait_send()

    def end_sum(at):
        for way in (1, 0):
            others = k.chip_sums.at[at % 2, pl.ds(0, chips - 1)]
            pltpu.make_async_copy(others, others, k.chip_sem.at[way, at]).wait()
        total = k.chip_sums[at % 2, 0]
        for p in range(1, chips):
            total = total + k.chip_sums[at % 2, p]
        return total

    def halo_copies(lay, ref, at):
        src_row = jnp.where(h == 0, lay.rows, 1)
        dst_row = jnp.where(h == 0, 0, lay.rows + 1)
        rows, cols = lay.rows, lay.cols

        def remote(src, dst, way, device):
            return lambda: pltpu.make_async_remote_copy(
                src_ref=ref.at[src],
                dst_ref=ref.at[dst],
                send_sem=k.halo_sem.at[0, at, way],
                recv_sem=k.halo_sem.at[1, at, way],
                device_id=device,
                device_id_type=MESH,
            )

        all_rows, all_cols = pl.ds(1, rows), pl.ds(1, cols)
        row = remote((src_row, all_cols), (dst_row, all_cols), 0, (b, 1 - h, w))
        to_left = [
            remote((all_rows, 1), (all_rows, cols + 1), 1, (b, h, w - 1)),
            remote((src_row, 1), (dst_row, cols + 1), 2, (b, 1 - h, w - 1)),
        ]
        to_right = [
            remote((all_rows, cols), (all_rows, 0), 3, (b, h, w + 1)),
            remote((src_row, cols), (dst_row, 0), 4, (b, 1 - h, w + 1)),
        ]
        return row, to_left, to_right

    def normed_copies():
        ref, rows, cols = one.s.normed, one.rows, one.cols
        half = rows // 2
        src_row = jnp.where(h == 0, rows, 1)
        dst_row = jnp.where(h == 0, 0, rows + 1)

        def remote(part, slot, src, dst, device):
            return lambda: pltpu.make_async_remote_copy(
                src_ref=ref.at[src],
                dst_ref=ref.at[dst],
                send_sem=k.normed_sem.at[0, part, slot],
                recv_sem=k.normed_sem.at[1, part, slot],
                device_id=device,
                device_id_type=MESH,
            )

        parts = []
        for part in range(4):
            left, low = part < 2, part % 2 == 0
            src, dst = (1, cols + 1) if left else (cols, 0)
            way = w - 1 if left else w + 1
            run = pl.ds(1 if low else 1 + half, half)
            copies = [remote(part, 0, (run, src), (run, dst), (b, h, way))]
            if not low:
                copies.append(remote(part, 1, (src_row, src), (dst_row, dst), (b, 1 - h, way)))
            parts.append((w > 0 if left else w < n_wa - 1, w < n_wa - 1 if left else w > 0, copies))
        inner = pl.ds(1, cols)
        row = remote(1, 2, (src_row, inner), (dst_row, inner), (b, 1 - h, w))
        return row, parts

    def start_normed(*which):
        row, parts = normed_copies()
        if 1 in which:
            row().start()
        for part in which:
            sends, _, copies = parts[part]

            @pl.when(sends)
            def _(copies=copies):
                for copy in copies:
                    copy().start()

    def end_normed():
        row, parts = normed_copies()
        row().wait()
        for sends, receives, copies in parts:

            @pl.when(sends)
            def _(copies=copies):
                for copy in copies:
                    copy().wait_send()

            @pl.when(receives)
            def _(copies=copies):
                for copy in copies:
                    copy().wait_recv()

    def start_halo(lay, ref, at, first=True, last=True):
        row, to_left, to_right = halo_copies(lay, ref, at)
        if first:
            row().start()

            @pl.when(w > 0)
            def _():
                for copy in to_left:
                    copy().start()

        if last:

            @pl.when(w < n_wa - 1)
            def _():
                for copy in to_right:
                    copy().start()

    def end_halo(lay, ref, at, rows=True, cols=True):
        row, to_left, to_right = halo_copies(lay, ref, at)
        if rows:
            row().wait()
        if not cols:
            return

        @pl.when(w > 0)
        def _():
            for copy in to_left:
                copy().wait_send()
            for copy in to_right:
                copy().wait_recv()

        @pl.when(w < n_wa - 1)
        def _():
            for copy in to_right:
                copy().wait_send()
            for copy in to_left:
                copy().wait_recv()

    def exchange(layer, number):
        begin, count = BUNDLES[number]
        half, quarter, eighth = count // 2, count // 4, count // 8
        piece, chunk = count // 16, count // 32
        stride = n_batch // OWNERS
        g = k.grads.at[layer]
        r1, r2, r3, r4, r5 = (
            r.at[layer] for r in (k.got_half, k.got_eighth, k.got_piece, k.got_chunk, k.got_total)
        )
        to_half, to_eighth, to_piece, to_chunk = begin // 2, begin // 4, begin // 8, begin // 32

        def places():
            b, h, w = (lax.axis_index(a) for a in AXES)
            x, y = lax.rem(w, 2), lax.div(w, 2)
            at = SimpleNamespace(b=b, h=h, w=w)
            at.pair, at.beside, at.below = (b, 1 - h, w), (b, h, w + 1 - 2 * x), (b, h, w + 2 - 4 * y)
            at.mine, at.other = begin + h * half, begin + (1 - h) * half
            half_a, half_b = at.mine, at.mine + quarter
            at.eighth_a, at.eighth_b = half_a + x * eighth, half_b + y * eighth
            at.a, at.b_ = at.eighth_a + y * piece, at.eighth_b + x * piece
            at.sent_a, at.sent_b = half_a + (1 - x) * eighth, half_b + (1 - y) * eighth
            at.last_a, at.last_b = at.eighth_a + (1 - y) * piece, at.eighth_b + (1 - x) * piece
            at.rank = lax.div(b, stride)
            at.chunk = jnp.where(at.rank < 2, at.a, at.b_) + lax.rem(at.rank, 2) * chunk
            at.chunks = [(at.a, at.b_)[owner // 2] + owner % 2 * chunk for owner in range(OWNERS)]
            return at

        def copy(source, at, target, to, size, slot, device):
            return pltpu.make_async_remote_copy(
                src_ref=source.at[pl.ds(at, size)],
                dst_ref=target.at[pl.ds(to, size)],
                send_sem=k.grad_sem.at[0, layer, number, slot],
                recv_sem=k.grad_sem.at[1, layer, number, slot],
                device_id=device,
                device_id_type=MESH,
            )

        def pair_copies(at):
            return [copy(g, at.other, r1, to_half, half, 0, at.pair)]

        def eighth_copies(at):
            return [
                copy(g, at.sent_a, r2, to_eighth, eighth, 1, at.beside),
                copy(g, at.sent_b, r2, to_eighth + eighth, eighth, 2, at.below),
            ]

        def piece_copies(at):
            return [
                copy(g, at.last_a, r3, to_piece, piece, 3, at.below),
                copy(g, at.last_b, r3, to_piece + piece, piece, 4, at.beside),
            ]

        def piece_returns(at):
            return [
                copy(g, at.a, g, at.a, piece, 13, at.below),
                copy(g, at.b_, g, at.b_, piece, 14, at.beside),
            ]

        def eighth_returns(at):
            return [
                copy(g, at.eighth_a, g, at.eighth_a, eighth, 15, at.beside),
                copy(g, at.eighth_b, g, at.eighth_b, eighth, 16, at.below),
            ]

        def pair_returns(at):
            return [copy(g, at.mine, g, at.mine, half, 17, at.pair)]

        def go(copies):
            for c in copies:
                c.start()

        def end(copies):
            for c in copies:
                c.wait()

        def add(at, other, to, size):
            step = 16 if size % 16 == 0 else size

            def body(i, carry):
                mine = pl.ds(at + i * step, step)
                g[mine] = g[mine] + other[pl.ds(to + i * step, step)]
                return carry

            lax.fori_loop(0, size // step, body, 0)

        def free(slot, device):
            sem = k.free_sem.at[layer, number, slot]
            pl.semaphore_signal(sem, inc=1, device_id=device, device_id_type=MESH)

        def wait_free(slot):
            pl.semaphore_wait(k.free_sem.at[layer, number, slot], 1)

        def for_owner(at, do):
            if stride == 1:
                do()
            else:
                pl.when(lax.rem(at.b, stride) == 0)(do)

        def for_others(at, do):
            for owner in range(OWNERS):
                pl.when(at.b != owner * stride)(functools.partial(do, owner))

        def share_copies(at):
            return [
                pltpu.make_async_remote_copy(
                    src_ref=g.at[pl.ds(at.chunk, chunk)],
                    dst_ref=r5.at[at.rank, pl.ds(to_chunk, chunk)],
                    send_sem=k.grad_sem.at[0, layer, number, 9],
                    recv_sem=k.grad_sem.at[1, layer, number, 9 + at.rank],
                    device_id=(lax.rem(at.b + i, n_batch), at.h, at.w),
                    device_id_type=MESH,
                )
                for i in range(1, n_batch)
            ]

        def start_pair():
            go(pair_copies(places()))

        def start_eighths():
            at = places()
            end(pair_copies(at))
            free(0, at.pair)
            add(at.mine, r1, to_half, half)
            go(eighth_copies(at))

        def start_pieces():
            at = places()
            end(eighth_copies(at))
            add(at.eighth_a, r2, to_eighth, eighth)
            add(at.eighth_b, r2, to_eighth + eighth, eighth)
            go(piece_copies(at))

        def start_chunks():
            at = places()
            end(piece_copies(at))
            free(1, at.below)
            free(2, at.beside)
            add(at.a, r3, to_piece, piece)
            add(at.b_, r3, to_piece + piece, piece)

            def send_chunk(owner):
                pltpu.make_async_remote_copy(
                    src_ref=g.at[pl.ds(at.chunks[owner], chunk)],
                    dst_ref=r4.at[at.b, pl.ds(to_chunk, chunk)],
                    send_sem=k.grad_sem.at[0, layer, number, 5 + owner],
                    recv_sem=k.grad_sem.at[1, layer, number, 5],
                    device_id=(owner * stride, at.h, at.w),
                    device_id_type=MESH,
                ).start()

            for_others(at, send_chunk)

        def share_chunk():
            at = places()

            def collect():
                others = r4.at[pl.ds(0, n_batch - 1), pl.ds(to_chunk, chunk)]
                pltpu.make_async_copy(others, others, k.grad_sem.at[1, layer, number, 5]).wait()
                r4[at.b, pl.ds(to_chunk, chunk)] = g[pl.ds(at.chunk, chunk)]
                total = r4[0, pl.ds(to_chunk, chunk)].astype(F32)
                for slot in range(1, n_batch):
                    total = total + r4[slot, pl.ds(to_chunk, chunk)].astype(F32)
                g[pl.ds(at.chunk, chunk)] = total.astype(BF16)
                go(share_copies(at))

            for_owner(at, collect)

            def sent_chunk(owner):
                part = g.at[pl.ds(at.chunks[owner], chunk)]
                pltpu.make_async_copy(part, part, k.grad_sem.at[0, layer, number, 5 + owner]).wait()

            for_others(at, sent_chunk)

        def return_pieces():
            at = places()

            def shared():
                for c in share_copies(at):
                    c.wait_send()

            for_owner(at, shared)

            def take_chunk(owner):
                part = r5.at[owner, pl.ds(to_chunk, chunk)]
                pltpu.make_async_copy(part, part, k.grad_sem.at[1, layer, number, 9 + owner]).wait()
                g[pl.ds(at.chunks[owner], chunk)] = r5[owner, pl.ds(to_chunk, chunk)]

            for_others(at, take_chunk)
            wait_free(1)
            wait_free(2)
            go(piece_returns(at))

        def return_eighths():
            at = places()
            end(piece_returns(at))
            go(eighth_returns(at))

        def return_halves():
            at = places()
            end(eighth_returns(at))
            wait_free(0)
            go(pair_returns(at))

        def result():
            target = k.weight_grads.at[layer, pl.ds(LOW_OUT if begin == LOW_AT else begin, count)]
            sem = k.out_sem.at[layer, number]
            return pltpu.make_async_copy(g.at[pl.ds(begin, count)], target, sem)

        def start_result():
            end(pair_returns(places()))

            result().start()

        def end_result():
            result().wait()

        return (
            start_pair,
            start_eighths,
            start_pieces,
            start_chunks,
            share_chunk,
            return_pieces,
            return_eighths,
            return_halves,
            start_result,
            end_result,
        )

    exchanges = {(layer, number): exchange(layer, number) for layer in range(2) for number in range(3)}
    plan, taken = {}, dict.fromkeys(exchanges, 0)
    for point, keys in list(SCHEDULE.items()) + [(None, LAST_STEPS)]:
        for key in keys:
            plan.setdefault(point, []).append(exchanges[key][taken[key]])
            taken[key] += 1
    assert all(taken[key] == len(exchanges[key]) for key in exchanges)

    def progress(*point):
        for step in plan.get(point, ()):
            step()

    def flat_block(lay):
        block = lay.s.block_in[...]
        return block.reshape(lay.cells, block.shape[-1])

    def store_blocks(layer, at, value):
        rows, lanes = value.shape
        for lane in range(0, lanes, 128):
            size = min(128, lanes - lane)
            blocks = pl.ds(at + lane // 128 * (rows // 16), rows // 16)
            tile = value[:, lane : lane + size].reshape(rows // 16, 16, size)
            k.grads[layer, blocks, :, 0:size] = tile

    def column_sum(value):
        return jnp.sum(value, axis=0, keepdims=True)

    def center_mask(lay, row, count=1):
        mask = lay.s.mask[pl.ds(row + 1, count), 1 : lay.cols + 1]
        return mask.reshape(count * lay.row_cells, 1)

    def shifted(lay, value):
        count = value.shape[0]
        frame_at = lax.rem(lax.broadcasted_iota(jnp.int32, (count, 1), 0), lay.slot)
        before = jnp.where(frame_at == 0, 0.0, pltpu.roll(value, 1, 0))
        after = jnp.where(frame_at == lay.slot - 1, 0.0, pltpu.roll(value, count - 1, 0))
        return before, after

    def reorder(lay, value, cells_first):
        size, cols, frames = lay.row_cells, lay.cols, lay.frames
        to = lax.broadcasted_iota(jnp.int32, (size, size), 0)
        source = lax.broadcasted_iota(jnp.int32, (size, size), 1)
        if cells_first:
            wanted = lax.rem(to, frames) * cols + lax.div(to, frames)
        else:
            wanted = lax.rem(to, cols) * frames + lax.div(to, cols)
        swap = (source == wanted).astype(F32).astype(BF16)
        return dot(swap, value.reshape(size, value.shape[-1]))

    def cells_of(lay, i):
        size = lay.step * lay.row_cells
        return pl.ds(i * size if isinstance(i, int) else pl.multiple_of(i * size, size), size)

    def reduce_conv(lay):
        s, at, step = lay.s, lay.index, lay.step
        count = step * lay.row_cells

        def body(i, sums):
            mask = center_mask(lay, i * step, step)
            if lay.index == 0:
                load_features(i).wait()
            if lay.index == 0:
                block = [reorder(lay, k.v_input_grad[:, i * step + row], True) for row in range(step)]
                block = (jnp.concatenate(block, axis=0) * mask).astype(BF16)
                shape = (step, lay.cols, lay.frames, block.shape[-1])
                s.block_in[pl.ds(i * step, step)] = block.reshape(shape)
            else:
                block = s.block_in[pl.ds(i * step, step)]
                block = block.reshape(count, block.shape[-1])
            reduced = dot(block, k.v_w_reduce[at], NT)
            projected = dot(block, k.v_w_pool[at])
            rows = pl.ds(i * step, step)
            inner = pl.ds(i * step + 1, step)
            shape = (step, lay.cols, lay.frames)
            s.first[rows] = reduced[:, :B0].reshape(shape + (B0,))
            thin = reduced[:, B0:].reshape(shape + (NARROW,))
            s.narrow[inner, 1 : lay.cols + 1] = thin
            s.border[inner, 1 : lay.cols + 1, :, 0:BP] = projected.reshape(shape + (BP,)).astype(BF16)
            s.border[inner, 1 : lay.cols + 1, :, BP:] = thin.astype(BF16)
            total, square, valid = sums
            return (
                total + column_sum(reduced),
                square + column_sum(reduced * reduced),
                valid + column_sum(mask),
            )

        zero = jnp.zeros((1, REDUCE), F32)
        return loop(lay.rows // step, body, (zero, zero, jnp.zeros((1, 1), F32)))

    def narrow_cells(lay, norm, where):
        s = lay.s
        average, scale, bias = norm
        z = s.narrow[where]
        shape = z.shape[:-1]
        z = z.reshape(-1, NARROW)
        mask = s.mask[where].reshape(-1, 1)
        value = jnp.where(mask > 0.0, softplus((z - average) * scale + bias), 0.0)
        before, after = shifted(lay, value)
        parts = (before, value, after)
        mid = jnp.concatenate([p[:, :B1R] for p in parts], axis=1)
        small = jnp.concatenate([p[:, B1R:] for p in parts], axis=1)
        s.mid_in[where] = mid.astype(BF16).reshape(shape + (3 * B1R,))
        s.small_in[where] = small.astype(BF16).reshape(shape + (3 * B2R,))

    def narrow_center(lay, norm):
        s, step = lay.s, lay.pad_step
        inner = slice(1, lay.cols + 1)
        for row in (0, lay.rows + 1):
            s.narrow[row, inner] = s.border[row, inner, :, BP:].astype(F32)

        def body(i, carry):
            narrow_cells(lay, norm, (pl.ds(i * step, step), inner))
            return carry

        loop((lay.rows + 2) // step, body, 0)

    def narrow_sides(lay, norm):
        s, step = lay.s, lay.pad_step
        for col in (0, lay.cols + 1):
            s.narrow[:, col] = s.border[:, col, :, BP:].astype(F32)
            narrow_cells(lay, norm, (slice(None), col))

        def body(i, carry):
            at = pl.ds(i * step, step)
            s.box[at] = box_row(lay, s.border[at, :, :, 0:BP].astype(F32))
            return carry

        loop((lay.rows + 2) // step, body, 0)

    def box_row(lay, value):
        cols, t, step = lay.cols, lay.frames, lay.pad_step
        flat = value.reshape(step * (cols + 2) * t, BP)
        before, after = shifted(lay, flat)
        flat = (flat + before + after).reshape(step, cols + 2, t, BP)
        return flat[:, 0:cols] + flat[:, 1 : cols + 1] + flat[:, 2 : cols + 2]

    def box_rows(lay, row):
        box, step = lay.s.box, lay.step
        total = box[pl.ds(row, step)] + box[pl.ds(row + 1, step)] + box[pl.ds(row + 2, step)]
        return total.reshape(step * lay.row_cells, BP) * (1.0 / 27.0)

    def window(lay, ref, row, col, width):
        value = ref[pl.ds(row, lay.rows), pl.ds(col, lay.cols)]
        return value.reshape(lay.cells, width)

    def taps(lay, body, at, begin=0, end=9):
        if lay.index:
            for tap in range(begin, end):
                body(tap, 0)
                progress(1, (at, tap))
            return

        def with_progress(tap, carry):
            body(tap, carry)
            for some in range(begin, end):
                if (0, (at, some)) in SCHEDULE:

                    @pl.when(tap == some)
                    def _(some=some):
                        progress(0, (at, some))

            return carry

        lax.fori_loop(begin, end, with_progress, 0)

    def tap_at(tap):
        return (tap // 3, tap % 3) if isinstance(tap, int) else (lax.div(tap, 3), lax.rem(tap, 3))

    def cube_conv(lay, meanwhile):
        s, at = lay.s, lay.index
        s.mid[:, 0:B1] = jnp.zeros((lay.cells, B1), F32)
        s.small[...] = jnp.zeros(s.small.shape, F32)

        def body(tap, carry):
            row, col = tap_at(tap)
            s.mid[:, 0:B1] += dot(window(lay, s.mid_in, row, col, 3 * B1R), k.v_w_mid[at, tap])
            s.small[...] += dot(window(lay, s.small_in, row, col, 3 * B2R), k.v_w_small[at, tap])
            return carry

        def inner_tap(i):
            return 3 * i + 1

        def outer_tap(i):
            return 3 * (i // 2) + 2 * (i % 2) if isinstance(i, int) else 3 * lax.div(i, 2) + 2 * lax.rem(i, 2)

        for count, to_tap in ((3, inner_tap), (6, outer_tap)):
            if lay.index:
                for i in range(count):
                    body(to_tap(i), 0)
            else:
                lax.fori_loop(0, count, lambda i, carry, to_tap=to_tap: body(to_tap(i), carry), 0)
            if to_tap is inner_tap:
                meanwhile()

    def second_rows(lay, i):
        cells = cells_of(lay, i)
        return [
            ref[cells, 0:n] for ref, n in zip((lay.s.mid, lay.s.small, lay.s.pool), SECOND)
        ]

    def second_sums(lay):
        def body(i, sums):
            lay.s.pool[cells_of(lay, i), :] = box_rows(lay, i * lay.step)
            mask = center_mask(lay, i * lay.step, lay.step)
            out = []
            for (total, square), value in zip(sums, second_rows(lay, i)):
                inside = value * mask
                out.append((total + column_sum(inside), square + column_sum(inside * value)))
            return tuple(out)

        zero = tuple((jnp.zeros((1, n), F32),) * 2 for n in SECOND)
        return loop(lay.rows // lay.step, body, zero)

    def put_second(at, sums):
        for which in range(2):
            for begin, part, width in zip(SECOND_AT, sums, SECOND):
                begin += which * SECOND_WIDTH
                k.sums[at, :, begin : begin + width] = part[which]

    def get_second(total, which):
        return [total[:, which * SECOND_WIDTH + a : which * SECOND_WIDTH + a + n] for a, n in zip(SECOND_AT, SECOND)]

    def put_first(at, sums):
        for which in range(2):
            k.sums[at, :, which * 512 : which * 512 + REDUCE] = sums[which]

    def get_first(total, which):
        return total[:, which * 512 : which * 512 + REDUCE]

    def second_params(k_of, at):
        row = k_of[at : at + 1, :]
        out, begin = [], REDUCE
        for width in SECOND:
            out.append(row[:, begin : begin + width])
            begin += width
        return out

    def first_params(k_of, at):
        return k_of[at : at + 1, 0:REDUCE]

    def forward(lay, at, count, cubes, before, first_idle, after_first, in_conv, second_idle):
        s = lay.s
        total, square, valid = reduce_conv(lay)
        before()
        put_first(at, (total, square))
        if count is None:
            k.sums[at, :, 1024:1152] = jnp.broadcast_to(valid, (1, 128))
        start_sum(at)
        start_halo(lay, s.border, 2 * lay.index)
        first_idle()
        end_halo(lay, s.border, 2 * lay.index, cols=False)
        for copy in cubes:
            copy.wait()
        summed = end_sum(at)
        if count is None:
            count = summed[:, 1024:1025]
        gain = first_params(k.gain, lay.index)
        first = batch_norm_scale(get_first(summed, 0), get_first(summed, 1), count, gain)
        first += (first_params(k.bias, lay.index), gain)
        after_first()
        thin = (first[0][:, B0:], first[2][:, B0:], first[3][:, B0:])
        narrow_center(lay, thin)

        def sides():
            end_halo(lay, s.border, 2 * lay.index, rows=False)
            narrow_sides(lay, thin)
            in_conv()

        cube_conv(lay, sides)
        put_second(at + 1, second_sums(lay))
        start_sum(at + 1)
        second_idle()
        summed = end_sum(at + 1)
        second = []
        for total, square, gain, bias in zip(
            get_second(summed, 0),
            get_second(summed, 1),
            second_params(k.gain, lay.index),
            second_params(k.bias, lay.index),
        ):
            second.append(batch_norm_scale(total, square, count, gain) + (bias, gain))
        return first, second, count

    def normalised(value, norm):
        average, inv_std, scale, bias, gain = norm
        return (value - average) * inv_std

    def affine(value, norm):
        average, inv_std, scale, bias, gain = norm
        return (value - average) * scale + bias

    def left_half(norm):
        return tuple(p[:, :B0] for p in norm)

    def outputs(lay, i, first, second):
        mask = center_mask(lay, i * lay.step, lay.step)
        z = lay.s.first[pl.ds(i * lay.step, lay.step)].reshape(lay.step * lay.row_cells, B0)
        parts = [softplus(affine(z, left_half(first))) * mask]
        parts += [softplus(affine(v, n)) * mask for v, n in zip(second_rows(lay, i), second)]
        return parts

    def put_normed(lay, second, begin, end, cols):
        step = min(lay.step, end - begin)
        skipped, count = cols.start, cols.stop - cols.start

        def body(i, carry):
            row = begin + i * step
            inner = (pl.ds(row + 1, step), pl.ds(skipped + 1, count))
            size = lay.row_cells
            cells = pl.ds(row * size if isinstance(i, int) else pl.multiple_of(row * size, size), step * size)
            for a, width, ref, n in zip(SECOND_AT, SECOND, (lay.s.mid, lay.s.small, lay.s.pool), second):
                value = ref[cells, 0:width].reshape(step, lay.cols, lay.frames, width)
                value = value[:, cols].reshape(step * count * lay.frames, width)
                normed = normalised(value, n).astype(BF16).reshape(step, count, lay.frames, width)
                lay.s.normed[inner + (slice(None), slice(a, a + width))] = normed
            return carry

        loop((end - begin) // step, body, 0)

    for copy in flat_one:
        copy.wait()

    def wait_barrier():
        for copy in cubes_one + [slope_load] + flat_two + cubes_two:
            copy.start()
        beside = (w > 0).astype(jnp.int32) + (w < n_wa - 1).astype(jnp.int32)
        pl.semaphore_wait(barrier, chips + beside)

    def spread_two():
        slope_load.wait()
        for row in range(two.rows):
            k.slopes[pl.ds(row * two.row_cells, two.row_cells), :] = reorder(
                two, k.v_out_grad[:, row], True
            ).astype(BF16)
        for a, part, width in zip(SECOND_AT, slope_two(0)[1:], SECOND):
            part = part.reshape(two.rows, two.cols, two.frames, width).astype(BF16)
            k.grad_border[0, 1 : two.rows + 1, 1 : two.cols + 1, :, a : a + width] = part
        start_halo(two, k.grad_border.at[0], 4)

    def nothing():
        return None

    def split(value):
        a, b_, c, d = B0, B0 + B1, B0 + B1 + B2, B0 + B1 + B2 + BP
        return [value[:, :a], value[:, a:b_], value[:, b_:c], value[:, c:d]]

    def slope_two(i):
        return split(k.slopes[...].astype(F32))

    first_one, second_one, count_one = forward(
        one, 0, None, cubes_one, wait_barrier, nothing, nothing, spread_two, nothing
    )

    def halve(row, carry):
        begin = 0
        for p in outputs(one, row, first_one, second_one):
            width = p.shape[-1]
            both = p.reshape(2, two.cols, 2, one.frames, width)
            both = both[0, :, 0] + both[0, :, 1] + both[1, :, 0] + both[1, :, 1]
            for lane in range(0, width, 128):
                size = min(128, width - lane)
                k.pairs[:, begin + lane // 128, :, 0:size] = both[:, :, lane : lane + size]
            begin += -(-width // 128)
        for col in range(two.cols):
            tiles = []
            for lane in range(begin):
                even = k.pairs[col, lane, pl.ds(0, two.frames, stride=2), :]
                odd = k.pairs[col, lane, pl.ds(1, two.frames, stride=2), :]
                tiles.append((even + odd) * 0.125)
            half = (B0 + B1) // 128
            tiles[half] = tiles[half][:, : (B0 + B1) % 128]
            mean = jnp.concatenate(tiles, axis=1)
            two.s.block_in[row, col] = mean.astype(BF16)
        return carry

    half_rows = one.rows // 2
    put_normed(one, second_one, 0, half_rows, slice(0, 1))
    start_normed(*NORMED_AT[0])
    lax.fori_loop(0, two.rows, halve, 0)

    for copy in flat_two:
        copy.wait()

    def share_normed():
        put_normed(one, second_one, 0, half_rows, slice(1, one.cols))
        put_normed(one, second_one, half_rows, one.rows, slice(0, one.cols))
        start_normed(*NORMED_AT[1])

    def share_third():
        start_normed(*NORMED_AT[2])

    def share_rest():
        start_normed(*NORMED_AT[3])

    first_two, second_two, count_two = forward(
        two, 2, count_one * 0.125, cubes_two, nothing, share_normed, share_third, nothing, share_rest
    )

    def level(lay, begin, end):
        return softplus(k.bias[lay.index : lay.index + 1, begin:end]).astype(BF16).astype(F32)

    def center_windows(lay):
        mid, small = level(lay, B0, B0 + B1R), level(lay, B0 + B1R, REDUCE)
        mid, small = (jnp.concatenate([v] * 3, axis=1) for v in (mid, small))
        s, step = lay.s, lay.pad_step

        def body(i, carry):
            at = pl.ds(i * step, step)
            for ref, value in ((s.mid_in, mid), (s.small_in, small)):
                shape = (step,) + ref.shape[1:]
                part = ref[at].reshape(-1, shape[-1]).astype(F32) - value
                ref[at] = part.astype(BF16).reshape(shape)
            return carry

        loop((lay.rows + 2) // step, body, 0)

    def centered_block(lay):
        if lay.index == 0:
            return flat_block(lay)
        value = jnp.concatenate([level(one, 0, B0), level(one, REDUCE, k.bias.shape[1])], axis=1)
        return (flat_block(lay).astype(F32) - value).astype(BF16)

    def backward(lay, out_slope, border_slope, at, first, second, count, before_end, after_end, before_low):
        s, index, step = lay.s, lay.index, lay.step
        chunks = lay.rows // step
        per_cell = 1.0 / count

        def second_slope(i):
            mask = center_mask(lay, i * step, step)
            values = second_rows(lay, i)
            normed = [normalised(v, n) for v, n in zip(values, second)]
            slopes = [
                g * mask * sigmoid(m * n[4] + n[3])
                for g, m, n in zip(out_slope(i)[1:], normed, second)
            ]
            return mask, normed, slopes

        def sum_body(i, sums):
            mask, normed, slopes = second_slope(i)
            return tuple(
                (t + column_sum(g), q + column_sum(g * m))
                for (t, q), g, m in zip(sums, slopes, normed)
            )

        zero = tuple((jnp.zeros((1, n), F32),) * 2 for n in SECOND)
        put_second(at, loop(chunks, sum_body, zero))
        start_sum(at)
        before_end()
        center_windows(lay)
        progress(index, 0)
        summed = end_sum(at)
        after_end()
        totals = list(zip(get_second(summed, 0), get_second(summed, 1)))
        begin = REDUCE
        for (bias_grad, gain_grad), width in zip(totals, SECOND):
            k.bias_grad[index : index + 1, begin : begin + width] = bias_grad
            k.gain_grad[index : index + 1, begin : begin + width] = gain_grad
            begin += width
        totals = [(t * per_cell, q * per_cell) for t, q in totals]

        def pre_slope(g, m, norm, total):
            return norm[2] * (g - (total[0] + m * total[1]))

        def center_body(i, carry):
            mask, normed, slopes = second_slope(i)
            inner = pl.ds(i * step + 1, step)
            for a, width, g, m, n, total in zip(SECOND_AT, SECOND, slopes, normed, second, totals):
                value = (pre_slope(g, m, n, total) * mask).astype(BF16)
                s.normed[inner, 1 : lay.cols + 1, :, a : a + width] = value.reshape(
                    step, lay.cols, lay.frames, width
                )
            return carry

        loop(chunks, center_body, 0)

        def border_cells(where, slopes):
            mask = s.mask[where]
            cells = mask.shape[0]
            mask = mask.reshape(cells * lay.frames, 1)
            normed = s.normed[where].astype(F32).reshape(cells * lay.frames, SECOND_WIDTH)
            for a, width, g, n, total in zip(SECOND_AT, SECOND, slopes, second, totals):
                m = normed[:, a : a + width]
                g = g * sigmoid(m * n[4] + n[3])
                value = jnp.where(mask > 0.0, pre_slope(g, m, n, total), 0.0).astype(BF16)
                s.normed[where + (slice(None), slice(a, a + width))] = value.reshape(
                    cells, lay.frames, width
                )

        border_cells((jnp.where(h == 0, lay.rows + 1, 0), slice(None)), border_slope(True, None))
        for col in (0, lay.cols + 1):
            border_cells((slice(1, lay.rows + 1), col), border_slope(False, col > 0))

        progress(index, 1)

        center = s.normed[1 : lay.rows + 1, 1 : lay.cols + 1].reshape(lay.cells, SECOND_WIDTH)
        turned_mid = center[:, 0:B1].T
        turned_small = center[:, 384:512].T

        def tap_body(tap, carry):
            row, col = tap_at(tap)
            mid = dot(turned_mid, window(lay, s.mid_in, row, col, 3 * B1R)).astype(BF16)
            small = dot(turned_small, window(lay, s.small_in, row, col, 3 * B2R)).astype(BF16)
            store_blocks(index, tap * TAP_BLOCKS, mid)
            store_blocks(index, tap * TAP_BLOCKS + 80, small)
            return carry

        taps(lay, tap_body, 5, 0, EARLY_TAPS[index])

        s.mid[...] = jnp.zeros(s.mid.shape, F32)
        s.small[:, 0 : 3 * B2R] = jnp.zeros((lay.cells, 3 * B2R), F32)

        def back_body(tap, carry):
            row, col = tap_at(tap)
            slope = window(lay, s.normed, 2 - row, 2 - col, SECOND_WIDTH)
            s.mid[...] += dot(slope[:, 0:B1], k.v_w_mid[index, tap], NT)
            s.small[:, 0 : 3 * B2R] += dot(slope[:, 384:512], k.v_w_small[index, tap], NT)
            return carry

        taps(lay, back_body, 2)

        def box_body(i, carry):
            at = pl.ds(i * lay.pad_step, lay.pad_step)
            s.box[at] = box_row(lay, s.normed[at, :, :, 512:640].astype(F32))
            return carry

        loop((lay.rows + 2) // lay.pad_step, box_body, 0)
        progress(index, 3)

        def first_normed(i):
            size = step * lay.row_cells
            z = s.first[pl.ds(i * step, step)].reshape(size, B0)
            z_thin = s.narrow[pl.ds(i * step + 1, step), 1 : lay.cols + 1].reshape(size, NARROW)
            return normalised(jnp.concatenate([z, z_thin], axis=1), first)

        def first_body(i, sums):
            cells = cells_of(lay, i)
            s.projected_slope[cells, :] = box_rows(lay, i * step).astype(BF16)
            mid = s.mid[cells, :]
            small = s.small[cells, 0 : 3 * B2R]
            thirds = [
                jnp.concatenate(
                    [mid[:, B1R * t : B1R * (t + 1)], small[:, B2R * t : B2R * (t + 1)]], axis=1
                )
                for t in range(3)
            ]
            thin = thirds[1] + shifted(lay, thirds[2])[0] + shifted(lay, thirds[0])[1]
            mask = center_mask(lay, i * step, step)
            normed = first_normed(i)
            g = jnp.concatenate([out_slope(i)[0], thin], axis=1)
            g = g * mask * sigmoid(normed * first[4] + first[3])
            s.mid[cells, 0:REDUCE] = g
            return sums[0] + column_sum(g), sums[1] + column_sum(g * normed)

        zero = (jnp.zeros((1, REDUCE), F32),) * 2
        put_first(at + 1, loop(chunks, first_body, zero))
        start_sum(at + 1)

        progress(index, 4)

        taps(lay, tap_body, 5, EARLY_TAPS[index])
        store_blocks(index, LOW_AT + 196, dot(s.projected_slope[...].T, flat_block(lay)).astype(BF16))
        progress(index, 6)
        summed = end_sum(at + 1)
        total = (get_first(summed, 0), get_first(summed, 1))
        k.bias_grad[index : index + 1, 0:REDUCE] = total[0]
        k.gain_grad[index : index + 1, 0:REDUCE] = total[1]

        total = (total[0] * per_cell, total[1] * per_cell)

        def low_body(i, carry):
            cells = cells_of(lay, i)
            mask = center_mask(lay, i * step, step)
            value = pre_slope(s.mid[cells, 0:REDUCE], first_normed(i), first, total) * mask
            s.low[cells, :] = value.astype(BF16)
            return carry

        loop(chunks, low_body, 0)
        before_low()
        progress(index, 7)
        store_blocks(index, LOW_AT, dot(s.low[...].T, centered_block(lay)).astype(BF16))
        progress(index, 8)

    def widen(ref, begin, value):
        width = value.shape[-1]
        for lane in range(0, width, 128):
            size = min(128, width - lane)
            for odd in range(2):
                ref[(begin + lane) // 128, pl.ds(odd, two.frames, stride=2), 0:size] = value[
                    :, lane : lane + size
                ]

    def wide(value, a, width):
        tiles = [value[..., lane // 128, :, :] for lane in range(a, a + width, 128)]
        return jnp.concatenate(tiles, axis=-1)[..., :width]

    def put_two(i, slope):
        slope = slope * 0.125
        for a, part in zip((0,) + tuple(B0 + a for a in SECOND_AT), split(slope)):
            width = part.shape[-1]
            part = part.reshape(two.rows, two.cols, two.frames, width)
            for row in range(two.rows):
                for col in range(two.cols):
                    widen(k.spread.at[row, col], a, part[row, col])
            if a >= B0:
                inner = (slice(1, two.rows + 1), slice(1, two.cols + 1), slice(None))
                k.grad_border[(1,) + inner + (slice(a - B0, a - B0 + width),)] = part.astype(BF16)

    def input_slope(lay, low, projected):
        slope = dot(low, k.v_w_reduce[lay.index])
        return slope + dot(projected, k.v_w_pool[lay.index], NT)

    def low_two():
        mask = center_mask(two, 0, two.rows)
        put_two(0, input_slope(two, two.s.low[...], two.s.projected_slope[...]) * mask)

    def side(lay, across, last):
        if across:
            return (jnp.where(h == 0, lay.rows + 1, 0), slice(None))
        return (slice(1, lay.rows + 1), lay.cols + 1 if last else 0)

    def border_two(across, last):
        value = k.grad_border[(0,) + side(two, across, last)].astype(F32)
        value = value.reshape(value.shape[0] * two.frames, SECOND_WIDTH)
        return [value[:, a : a + n] for a, n in zip(SECOND_AT, SECOND)]

    def end_two():
        put_normed(two, second_two, 0, two.rows, slice(0, two.cols))
        start_halo(two, two.s.normed, 3)
        value = jnp.concatenate(outputs(two, 0, first_two, second_two), axis=1).astype(BF16)
        for row in range(two.rows):
            part = reorder(two, value[row * two.row_cells : (row + 1) * two.row_cells], False)
            k.v_block_output[:, row] = part.reshape(two.frames, two.cols, -1).astype(BF16)
        output_store.start()
        end_halo(two, two.s.normed, 3)
        end_halo(two, k.grad_border.at[0], 4)

    def after_two():
        start_normed(*NORMED_AT[4])

    backward(two, slope_two, border_two, 4, first_two, second_two, count_two, end_two, after_two, low_two)
    start_halo(two, k.grad_border.at[1], 5)

    def slope_one(i):
        value = k.spread[i]
        out = []
        for a, width in zip((0,) + tuple(B0 + a for a in SECOND_AT), (B0,) + SECOND):
            part = wide(value, a, width)
            pieces = [part[col // 2] for col in range(one.cols)]
            out.append(jnp.concatenate(pieces * one.step, axis=0))
        return out

    def border_one(across, last):
        where = side(two, across, last)
        value = k.border_spread[where] if across else k.border_spread[:, where[1]]
        cells = range(one.cols + 2) if across else range(1, one.rows + 1)
        out = []
        for a, n in zip(SECOND_AT, SECOND):
            part = wide(value, a, n)
            out.append(jnp.concatenate([part[(cell + 1) // 2] for cell in cells], axis=0))
        return out

    def end_one():
        end_normed()
        end_halo(two, k.grad_border.at[1], 5)
        places = [(side(two, True, None)[0], col) for col in range(two.cols + 2)]
        places += [(row, col) for row in range(1, two.rows + 1) for col in (0, two.cols + 1)]
        for row, col in places:
            widen(k.border_spread.at[row, col], 0, k.grad_border[1, row, col].astype(F32))

    backward(one, slope_one, border_one, 6, first_one, second_one, count_one, end_one, nothing, nothing)

    def input_row(row, carry):
        cells = pl.ds(pl.multiple_of(row * one.row_cells, one.row_cells), one.row_cells)
        low = reorder(one, one.s.low[cells, :], False).astype(BF16)
        projected = one.s.projected_slope[cells, :].astype(F32) * center_mask(one, row)
        projected = reorder(one, projected.astype(BF16), False).astype(BF16)
        slope = input_slope(one, low, projected)
        k.v_input_grad[:, row] = slope.reshape(one.frames, one.cols, -1).astype(BF16)
        return carry

    lax.fori_loop(0, one.rows, input_row, 0)
    input_store.start()
    for step in plan[None]:
        step()
    output_store.wait()
    input_store.wait()


UNPACK_TAPS = 9


def unpack_body(taps, low, gain, bias, mid_out, small_out, reduce_out, pool_out, gain_out, bias_out):
    def lanes(blocks, tiles, rows, width):
        parts = []
        for tile in range(tiles):
            size = min(128, width - 128 * tile)
            part = blocks[tile * (rows // 16) : (tile + 1) * (rows // 16), :, 0:size]
            parts.append(part.reshape(rows, size))
        return jnp.concatenate(parts, axis=1)

    def tap_body(tap, carry):
        blocks = taps.at[0, pl.ds(tap * TAP_BLOCKS, TAP_BLOCKS)]
        mid = lanes(blocks, 4, B1, 3 * B1R).T.astype(F32)
        small = lanes(blocks.at[80:88], 1, B2, 3 * B2R).T.astype(F32)
        for t in range(3):
            mid_out[0, t, tap] = mid[B1R * t : B1R * (t + 1)]
            small_out[0, t, tap] = small[B2R * t : B2R * (t + 1)]
        return carry

    lax.fori_loop(0, UNPACK_TAPS, tap_body, 0)

    @pl.when(pl.program_id(1) == 0)
    def _():
        channels = reduce_out.shape[-1]
        tiles = -(-channels // 128)
        reduce_out[0] = lanes(low.at[0, 0:196], tiles, REDUCE, channels).astype(F32)
        pool_out[0] = lanes(low.at[0, 196:252], tiles, BP, channels).T.astype(F32)
        gain_out[...] = gain[...]
        bias_out[...] = bias[...]


def unpack(grads, gain, bias, channels):
    n = UNPACK_TAPS
    shapes = ((2, 3, 9, B1R, B1), (2, 3, 9, B2R, B2), (2, REDUCE, channels), (2, channels, BP))
    shapes += (gain.shape, bias.shape)
    norms = [pl.BlockSpec(gain.shape, lambda i, j: (0, 0))] * 2
    mid_grad, small_grad, reduce_grad, pool_grad, gain, bias = pl.pallas_call(
        unpack_body,
        grid=(2, 9 // n),
        out_shape=[jax.ShapeDtypeStruct(shape, F32) for shape in shapes],
        in_specs=[
            pl.BlockSpec((1, n * TAP_BLOCKS, 16, 128), lambda i, j: (i, j, 0, 0)),
            pl.BlockSpec((1, 256, 16, 128), lambda i, j: (i, LOW_OUT // 256, 0, 0)),
        ]
        + norms,
        out_specs=[
            pl.BlockSpec((1, 3, n, B1R, B1), lambda i, j: (i, 0, j, 0, 0)),
            pl.BlockSpec((1, 3, n, B2R, B2), lambda i, j: (i, 0, j, 0, 0)),
            pl.BlockSpec((1, REDUCE, channels), lambda i, j: (i, 0, 0)),
            pl.BlockSpec((1, channels, BP), lambda i, j: (i, 0, 0)),
        ]
        + norms,
        compiler_params=pltpu.CompilerParams(vmem_limit_bytes=60 * 1024 * 1024),
        name="unpack",
    )(grads, grads, gain, bias)
    return (
        jnp.swapaxes(reduce_grad, 1, 2),
        mid_grad.reshape(2, 27, B1R, B1),
        small_grad.reshape(2, 27, B2R, B2),
        pool_grad,
        gain,
        bias,
    )


def on_device(
    n_batch, n_wa, clip_features, frame_counts, w_reduce, w_mid, w_small, w_pool, norm_gain, norm_bias, out_grad
):
    frames, rows, cols, channels = clip_features.shape
    clips = frame_counts.shape[0]
    slot = frames // clips
    layers = (
        Layer(0, rows, cols, clips, slot),
        Layer(1, rows // 2, cols // 2, clips, slot // 2),
    )
    one, two = layers
    chips = n_batch * n_wa

    operands = dict(
        features=clip_features,
        frame_counts=frame_counts,
        w_reduce=jnp.swapaxes(w_reduce, 1, 2),
        w_mid=w_mid.reshape(2, 3, 9, B1R, B1),
        w_small=w_small.reshape(2, 3, 9, B2R, B2),
        w_pool=w_pool,
        gain=norm_gain,
        bias=norm_bias,
        out_grad=out_grad,
    )
    in_space = dict(frame_counts=pltpu.SMEM, gain=pltpu.VMEM, bias=pltpu.VMEM)
    out_space = dict(weight_grads=pl.ANY, block_output=pl.ANY, input_grad=pl.ANY)
    results = dict(
        block_output=jax.ShapeDtypeStruct(out_grad.shape, BF16),
        input_grad=jax.ShapeDtypeStruct(clip_features.shape, BF16),
        weight_grads=jax.ShapeDtypeStruct((2, LOW_OUT + 256, 16, 128), BF16),
        gain_grad=jax.ShapeDtypeStruct(norm_gain.shape, F32),
        bias_grad=jax.ShapeDtypeStruct(norm_bias.shape, F32),
    )
    scratch = {}
    for name in ("w_reduce", "w_pool", "out_grad"):
        scratch["v_" + name] = pltpu.VMEM(operands[name].shape, BF16)
    scratch.update(
        v_w_mid=pltpu.VMEM((2, 9, 3 * B1R, B1), BF16),
        v_w_small=pltpu.VMEM((2, 9, 3 * B2R, B2), BF16),
    )
    small_pad = (two.rows + 2, two.cols + 2)
    scratch.update(
        slopes=pltpu.VMEM((two.cells, channels), BF16),
        v_block_output=pltpu.VMEM(out_grad.shape, BF16),
        v_input_grad=pltpu.VMEM(clip_features.shape, BF16),
        result_sem=pltpu.SemaphoreType.DMA((2,)),
        pairs=pltpu.VMEM((two.cols, (B0 + SECOND_WIDTH) // 128, one.frames, 128), F32),
        spread=pltpu.VMEM(
            (two.rows, two.cols, (B0 + SECOND_WIDTH) // 128, one.frames, 128), F32
        ),
        border_spread=pltpu.VMEM(small_pad + (SECOND_WIDTH // 128, one.frames, 128), F32),
        grad_border=pltpu.VMEM((2,) + small_pad + (two.frames, SECOND_WIDTH), BF16),
        sums=pltpu.VMEM((8, 1, SUM_WIDTH), F32),
        pair_sums=pltpu.VMEM((8, 1, SUM_WIDTH), F32),
        chip_sums=pltpu.VMEM((2, chips, 1, SUM_WIDTH), F32),
        load_sem=pltpu.SemaphoreType.DMA((17,)),
        feature_sem=pltpu.SemaphoreType.DMA((one.rows // one.step,)),
        pair_sem=pltpu.SemaphoreType.DMA((2, 8)),
        chip_sem=pltpu.SemaphoreType.DMA((2, 8)),
        normed_sem=pltpu.SemaphoreType.DMA((2, 4, 3)),
        halo_sem=pltpu.SemaphoreType.DMA((2, 6, 5)),
        grads=pltpu.VMEM((2, GRAD_BLOCKS, 16, 128), BF16),
        got_half=pltpu.VMEM((2, GRAD_BLOCKS // 2, 16, 128), BF16),
        got_eighth=pltpu.VMEM((2, GRAD_BLOCKS // 4, 16, 128), BF16),
        got_piece=pltpu.VMEM((2, GRAD_BLOCKS // 8, 16, 128), BF16),
        got_chunk=pltpu.VMEM((2, n_batch, GRAD_BLOCKS // 32, 16, 128), BF16),
        got_total=pltpu.VMEM((2, OWNERS, GRAD_BLOCKS // 32, 16, 128), BF16),
        free_sem=pltpu.SemaphoreType.REGULAR((2, 3, 3)),
        grad_sem=pltpu.SemaphoreType.DMA((2, 2, 3, 18)),
        out_sem=pltpu.SemaphoreType.DMA((2, 3)),
    )
    names = list(operands) + list(results) + list(scratch)
    layer_scratch = [lay.scratch(channels) for lay in layers]

    def body(*refs):
        rest = refs[len(names) :]
        for lay, parts in zip(layers, layer_scratch):
            lay.s = SimpleNamespace(**dict(zip(parts, rest[: len(parts)])))
            rest = rest[len(parts) :]
        kernel_body(names, (n_batch, n_wa, layers), refs[: len(names)])

    out = pl.pallas_call(
        body,
        out_shape=list(results.values()),
        in_specs=[pl.BlockSpec(memory_space=in_space.get(name, pl.ANY)) for name in operands],
        out_specs=[pl.BlockSpec(memory_space=out_space.get(name, pltpu.VMEM)) for name in results],
        scratch_shapes=list(scratch.values()) + [r for parts in layer_scratch for r in parts.values()],
        compiler_params=pltpu.CompilerParams(
            collective_id=0, has_side_effects=True, vmem_limit_bytes=63 * 1024 * 1024
        ),
        name="layers",
    )(*operands.values())
    out = dict(zip(results, out))

    kernels_and_norms = unpack(out["weight_grads"], out["gain_grad"], out["bias_grad"], channels)

    return (
        out["block_output"],
        out["input_grad"],
        *kernels_and_norms,
    )


def solution(mesh):
    in_specs = (
        P("batch", "ha", "wa", None),
        P("batch"),
        P(),
        P(),
        P(),
        P(),
        P(),
        P(),
        P("batch", "ha", "wa", None),
    )
    out_specs = (
        P("batch", "ha", "wa", None),
        P("batch", "ha", "wa", None),
        P(),
        P(),
        P(),
        P(),
        P(),
        P(),
    )
    return jax.shard_map(
        functools.partial(on_device, mesh.shape["batch"], mesh.shape["wa"]),
        mesh=mesh,
        in_specs=in_specs,
        out_specs=out_specs,
        check_vma=False,
    )
```
